32 devices in a mesh: pb: 4 (over y, x), dp: 8 (over z, core).
Axes of the slice: x: 2, y: 2, z: 4, core: 2. Of those that a mesh axis runs over, the one named last changes fastest.
Arguments:
- tokens: bfloat16 [32, 100, 512], P('dp', 'pb'), may hold values from -6 to 6
- query_pos: bfloat16 [100, 512], replicated, may hold values from -6 to 6
- features: bfloat16 [32, 1200, 512], P('dp'), may hold values from -6 to 6
- camera_mask: int32 [32, 4], P('dp'), may hold values from 0 to 1, as said below
- out_grad: bfloat16 [32, 100, 512], P('dp', 'pb'), may hold values from -6 to 6
- self_proj: bfloat16 [3, 512, 512], replicated, may hold values from -0.25 to 0.25
- self_out: bfloat16 [512, 512], replicated, may hold values from -0.75 to 0.75
- self_bias: bfloat16 [3, 512], replicated, may hold values from -3 to 3
- cross_proj: bfloat16 [3, 512, 512], replicated, may hold values from -0.25 to 0.25
- cross_out: bfloat16 [512, 512], replicated, may hold values from -1 to 1
- cross_bias: bfloat16 [3, 512], replicated, may hold values from -3 to 3
- w_up: bfloat16 [512, 3200], P(None, 'pb'), may hold values from -0.25 to 0.25
- b_up: bfloat16 [3200], P('pb'), may hold values from -3 to 3
- w_down: bfloat16 [512, 3200], P(None, 'pb'), may hold values from -0.109375 to 0.109375
- b_down: bfloat16 [512], replicated, may hold values from -3 to 3
- norm_gain: bfloat16 [3, 512], replicated, may hold values from 0.5 to 1.5
- norm_bias: bfloat16 [3, 512], replicated, may hold values from -2 to 2
- in_proj: bfloat16 [512, 512], replicated, may hold values from -0.25 to 0.25
- in_bias: bfloat16 [512], replicated, may hold values from -3 to 3
Outputs:
- layer_out: bfloat16 [32, 100, 512], P('dp', 'pb')
- grad_tokens: bfloat16 [32, 100, 512], P('dp', 'pb')
- grad_features: bfloat16 [32, 1200, 512], P('dp', 'pb')
- grad_query_pos: float32 [100, 512], replicated
- grad_self_proj: float32 [3, 512, 512], replicated
- grad_self_out: float32 [512, 512], replicated
- grad_self_bias: float32 [3, 512], replicated
- grad_cross_proj: float32 [3, 512, 512], replicated
- grad_cross_out: float32 [512, 512], replicated
- grad_cross_bias: float32 [3, 512], replicated
- grad_w_up: float32 [512, 3200], P('dp', 'pb')
- grad_b_up: float32 [3200], replicated
- grad_w_down: float32 [512, 3200], P('dp', 'pb')
- grad_b_down: float32 [512], replicated
- grad_norm_gain: float32 [3, 512], replicated
- grad_norm_bias: float32 [3, 512], replicated
- grad_in_proj: float32 [512, 512], replicated
- grad_in_bias: float32 [512], replicated
The draws below stay inside these ranges and needn't reach their ends.
Inputs may be any that keep to these rules, and one draw needn't show every extreme that they name: `camera_mask`: each episode has between 2 and 4 cameras present, in any combination of slots.
All inputs are finite; a program needn't handle non-finite values.
Results may differ from the reference program's by a relative error of at most 0.03.
Values may be sent and summed in bfloat16 or wider, within the bound.
No kernel may reach another device: no remote copies, remote signals or barrier semaphores. Data moves between devices by JAX's collectives and lax.ppermute only.
A program may use at most 128 MiB of HBM per device.

```python
import jax
import jax.numpy as jnp
from jax import lax

D = 512
H = 8
HD = 64
FF = 3200
FEAT = 512
NQ = 100
NCAM = 4
CAM_TOK = 300
EPISODES = 32
MEM = 1200


def draw_camera_mask(key, part):
    key = jax.random.fold_in(key, 7)
    count_key, order_key = jax.random.split(key)
    counts = jax.random.randint(count_key, (EPISODES,), 2, NCAM + 1)
    counts = counts.at[0].set(NCAM).at[1].set(2)
    scores = jax.random.randint(order_key, (EPISODES, NCAM), 0, 1 << 20) * NCAM + jnp.arange(NCAM)[None, :]
    ranking = jnp.argsort(jnp.argsort(scores, axis=1), axis=1)
    return (ranking < counts[:, None]).astype(jnp.int32)


def shard_levels(stream_key, dims, shards, low, top_value):
    loudness = 1.0
    for position, parts in shards:
        heights = jax.random.uniform(jax.random.fold_in(jax.random.fold_in(stream_key, 6), position), (parts,), jnp.float32, low / len(shards), top_value / len(shards))
        loudness = loudness * jnp.repeat(jnp.exp(heights), dims[position] // parts).reshape((-1,) + (1,) * (len(dims) - 1 - position))
    return loudness


def centred(own_key, extent, width, limit, cuts=(), dtype=jnp.bfloat16):
    drawn = jax.random.normal(own_key, extent, jnp.float32) * width
    if len(cuts) > 0:
        drawn = shard_levels(own_key, extent, cuts, -0.22, 0.18) * drawn
    return jnp.clip(drawn, min=-limit, max=limit).astype(dtype)


def setup_inputs(seed: int = 0) -> dict:
    arg_keys = jax.random.split(jax.random.key(seed), 20)
    tokens = centred(arg_keys[0], (EPISODES, NQ, D), 1.0, 6.0, ((0, 8), (1, 4)))
    query_pos = centred(arg_keys[1], (NQ, D), 1.0, 6.0)
    features = centred(arg_keys[2], (EPISODES, MEM, FEAT), 1.0, 6.0, ((0, 8),))
    camera_mask = draw_camera_mask(jax.random.fold_in(arg_keys[19], 71), 0)
    out_grad = centred(arg_keys[4], (EPISODES, NQ, D), 1.0, 6.0, ((0, 8), (1, 4)))
    self_proj = centred(arg_keys[5], (3, D, D), D ** -0.5, 0.25)
    self_out = centred(arg_keys[6], (D, D), (D // 8) ** -0.5, 0.75)
    self_bias = centred(arg_keys[7], (3, D), 0.5, 3.0)
    cross_proj = centred(arg_keys[8], (3, D, D), D ** -0.5, 0.25)
    cross_out = centred(arg_keys[9], (D, D), (D // 16) ** -0.5, 1.0)
    cross_bias = centred(arg_keys[10], (3, D), 0.5, 3.0)
    w_up = centred(arg_keys[11], (D, FF), D ** -0.5, 0.25, ((1, 4),))
    b_up = centred(arg_keys[12], (FF,), 0.5, 3.0, ((0, 4),))
    w_down = centred(arg_keys[13], (D, FF), FF ** -0.5, 0.109375, ((1, 4),))
    b_down = centred(arg_keys[14], (D,), 0.5, 3.0)
    norm_gain = jnp.clip(1.0 + 0.1 * jax.random.normal(arg_keys[15], (3, D), jnp.float32), 0.5, 1.5).astype(jnp.bfloat16)
    norm_bias = centred(arg_keys[16], (3, D), 0.3, 2.0)
    in_proj = centred(arg_keys[17], (FEAT, D), FEAT ** -0.5, 0.25)
    in_bias = centred(arg_keys[18], (D,), 0.5, 3.0)
    return {"tokens": tokens, "query_pos": query_pos, "features": features, "camera_mask": camera_mask, "out_grad": out_grad, "self_proj": self_proj, "self_out": self_out, "self_bias": self_bias, "cross_proj": cross_proj, "cross_out": cross_out, "cross_bias": cross_bias, "w_up": w_up, "b_up": b_up, "w_down": w_down, "b_down": b_down, "norm_gain": norm_gain, "norm_bias": norm_bias, "in_proj": in_proj, "in_bias": in_bias}


@jax.custom_vjp
def low(v):
    return lax.optimization_barrier(v.astype(jnp.bfloat16)).astype(jnp.float32)

@jax.custom_vjp
def low_back(v):
    return v

def low_keep(v):
    return (low(v), None)

def low_pass(kept, grad):
    return (grad,)

def back_keep(v):
    return (v, None)

def back_low(kept, grad):
    return (low(grad),)
low.defvjp(low_keep, low_pass)
low_back.defvjp(back_keep, back_low)

def both_round(value):
    return low(low_back(value))

def dense(left, weight):
    return jnp.dot(left, weight, precision=lax.Precision.HIGHEST)

def layer_norm(value, gain, shift):
    center = value - lax.optimization_barrier(jnp.mean(value, -1, keepdims=True))
    spread = lax.optimization_barrier(jnp.mean(center * center, -1, keepdims=True))
    return center * lax.rsqrt(spread + 1e-05) * gain + shift

def sinusoid(count, model_width):
    places = jnp.arange(count).astype(jnp.float32)[:, None]
    column = jnp.arange(model_width)
    exponent = (column // 2 * 2).astype(jnp.float32) / model_width
    angle = places / 10000.0 ** exponent
    return jnp.where(column % 2 == 0, jnp.sin(angle), jnp.cos(angle))

def attention(queries, keys, values, bias):
    query_heads = queries.reshape(queries.shape[0], H, HD)
    key_heads = keys.reshape(keys.shape[0], H, HD)
    value_heads = values.reshape(values.shape[0], H, HD)
    scores = low_back(jnp.einsum('qhd,khd->hqk', query_heads, key_heads, precision=lax.Precision.HIGHEST)) + bias
    weights = both_round(jax.nn.softmax(scores, axis=-1))
    mixed = jnp.einsum('hqk,khd->qhd', weights, value_heads, precision=lax.Precision.HIGHEST)
    return mixed.reshape(queries.shape[0], H * HD)

def episode(params, inputs, feats, live_slots):
    query_pos, self_proj, self_out, self_bias, cross_proj, cross_out, cross_bias, w_up, b_up, w_down, b_down, norm_gain, norm_bias, in_proj, in_bias = params
    attn_input = low(inputs + query_pos)
    self_q = both_round((dense(attn_input, self_proj[0]) + self_bias[0]) * 0.125)
    self_k = both_round(dense(attn_input, self_proj[1]))
    self_v = both_round(dense(inputs, self_proj[2]) + self_bias[1])
    self_mix = both_round(attention(self_q, self_k, self_v, 0.0))
    hidden_one = layer_norm(inputs + low_back(dense(self_mix, self_out) + self_bias[2]), norm_gain[0], norm_bias[0])
    memory = low_back(dense(feats, in_proj) + in_bias)
    key_input = low(memory + sinusoid(MEM, D))
    value_input = low(memory)
    cross_k = both_round(dense(key_input, cross_proj[1]))
    cross_v = both_round(dense(value_input, cross_proj[2]) + cross_bias[1])
    cross_input = low(hidden_one + query_pos)
    cross_q = both_round((dense(cross_input, cross_proj[0]) + cross_bias[0]) * 0.125)
    live_bias = jnp.where(live_slots > 0, 0.0, -1000000000.0)
    cross_mix = both_round(attention(cross_q, cross_k, cross_v, live_bias))
    hidden_two = layer_norm(hidden_one + low_back(dense(cross_mix, cross_out) + cross_bias[2]), norm_gain[1], norm_bias[1])
    pre_act = low_back(dense(low(hidden_two), w_up) + b_up)
    activated = both_round(jax.nn.gelu(pre_act, approximate=False))
    third_sum = hidden_two + low_back(dense(activated, w_down.T) + b_down)
    return layer_norm(third_sum, norm_gain[2], norm_bias[2])

def reference(tokens, query_pos, features, camera_mask, out_grad, self_proj, self_out, self_bias, cross_proj, cross_out, cross_bias, w_up, b_up, w_down, b_down, norm_gain, norm_bias, in_proj, in_bias):
    params = tuple((weight.astype(jnp.float32) for weight in (query_pos, self_proj, self_out, self_bias, cross_proj, cross_out, cross_bias, w_up, b_up, w_down, b_down, norm_gain, norm_bias, in_proj, in_bias)))
    live_slots = jnp.broadcast_to(camera_mask[:, :, None], (camera_mask.shape[0], NCAM, CAM_TOK)).reshape(camera_mask.shape[0], MEM)
    inputs = tokens.astype(jnp.float32)
    feats = features.astype(jnp.float32)

    def forward(inputs, feats, params):
        single = jax.checkpoint(lambda item: episode(params, item[0], item[1], item[2]))
        return lax.map(single, (inputs, feats, live_slots))
    result, pull = jax.vjp(forward, inputs, feats, params)
    grad_inputs, grad_feats, grads = pull(out_grad.astype(jnp.float32))
    return (result.astype(jnp.bfloat16), grad_inputs.astype(jnp.bfloat16), grad_feats.astype(jnp.bfloat16), grads[0], grads[1], grads[2], grads[3], grads[4], grads[5], grads[6], grads[7], grads[8], grads[9], grads[10], grads[11], grads[12], grads[13], grads[14])
```

```python
import jax
import jax.numpy as jnp
from jax import lax
from jax.sharding import PartitionSpec as P

H = 8
HD = 64
BF = jnp.bfloat16
F32 = jnp.float32


def dot(left, right):
    return jnp.einsum("nd,df->nf", left, right, preferred_element_type=F32)


def dot_back(left, right):
    return jnp.einsum("nf,df->nd", left, right, preferred_element_type=F32)


def dot_rows(left, right):
    return jnp.einsum("nd,nf->df", left, right, preferred_element_type=F32)


def column_sum(grad):
    return jnp.sum(grad.astype(F32), 0)


def layer_norm(value, gain, shift):
    center = value - jnp.mean(value, -1, keepdims=True)
    spread = jnp.mean(center * center, -1, keepdims=True)
    return center * lax.rsqrt(spread + 1e-05) * gain + shift


def norm_back(value, gain, shift, grad):
    unused, pull = jax.vjp(layer_norm, value, gain.astype(F32), shift.astype(F32))
    return pull(grad)


def sinusoid(count, model_width):
    places = jnp.arange(count).astype(F32)[:, None]
    column = jnp.arange(model_width)
    exponent = (column // 2 * 2).astype(F32) / model_width
    angle = places / 10000.0**exponent
    return jnp.where(column % 2 == 0, jnp.sin(angle), jnp.cos(angle))


def split_heads(value):
    return value.reshape(value.shape[0], H, HD)


def softmax_of(queries, keys, bias):
    scores = jnp.einsum(
        "qhd,khd->hqk", split_heads(queries), split_heads(keys), preferred_element_type=F32
    )
    return jax.nn.softmax(scores + bias, axis=-1)


def mix(probs, values):
    mixed = jnp.einsum(
        "hqk,khd->qhd", probs.astype(BF), split_heads(values), preferred_element_type=F32
    )
    return mixed.reshape(probs.shape[1], -1).astype(BF)


def attend_back(queries, keys, values, probs, grad_mix):
    grad_heads = split_heads(grad_mix)
    grad_weights = (
        jnp.einsum("qhd,khd->hqk", grad_heads, split_heads(values), preferred_element_type=F32)
        .astype(BF)
        .astype(F32)
    )
    grad_values = jnp.einsum(
        "hqk,qhd->khd", probs.astype(BF), grad_heads, preferred_element_type=F32
    ).reshape(keys.shape)
    grad_scores = (
        probs * (grad_weights - jnp.sum(probs * grad_weights, -1, keepdims=True))
    ).astype(BF)
    grad_queries = jnp.einsum(
        "hqk,khd->qhd", grad_scores, split_heads(keys), preferred_element_type=F32
    ).reshape(queries.shape)
    grad_keys = jnp.einsum(
        "hqk,qhd->khd", grad_scores, split_heads(queries), preferred_element_type=F32
    ).reshape(keys.shape)
    return grad_queries.astype(BF), grad_keys.astype(BF), grad_values.astype(BF)


def swap(value, axis, bit):
    size = lax.axis_size(axis)
    return lax.ppermute(value, axis, [(i, i ^ bit) for i in range(size)])


def bit_of(axis, bit):
    return (lax.axis_index(axis) // bit) % 2


def halve(value, axis, bit):
    mine = bit_of(axis, bit)
    half = value.shape[0] // 2
    keep = lax.dynamic_slice_in_dim(value, mine * half, half, 0)
    send = lax.dynamic_slice_in_dim(value, (1 - mine) * half, half, 0)
    return (keep.astype(F32) + swap(send, axis, bit).astype(F32)).astype(BF)


def double(value, axis, bit):
    other = swap(value, axis, bit)
    mine = bit_of(axis, bit)
    return jnp.where(
        mine == 0, jnp.concatenate([value, other]), jnp.concatenate([other, value])
    )


def all_sum(value):
    bits = [("dp", 1 << i) for i in range(1, lax.axis_size("dp").bit_length() - 1)]
    bits_pb = [("pb", 1 << i) for i in range(lax.axis_size("pb").bit_length() - 1)]
    first = bits_pb + bits[:1]
    later = bits[1:]
    orders = [first[i:] + first[:i] + later for i in range(3)]
    value = halve(value, "dp", 1)
    cut = value.shape[0]
    unit = 1 << len(orders[0])
    sizes = [cut // unit // 3 * unit] * 2
    parts = [value[: sizes[0]], value[sizes[0] : 2 * sizes[0]], value[2 * sizes[0] :]]
    for step in range(len(orders[0])):
        parts = [halve(part, *order[step]) for part, order in zip(parts, orders)]
    for step in reversed(range(len(orders[0]))):
        parts = [double(part, *order[step]) for part, order in zip(parts, orders)]
    return double(jnp.concatenate(parts), "dp", 1)


def on_device(
    tokens,
    query_pos,
    features,
    camera_mask,
    out_grad,
    self_proj,
    self_out,
    self_bias,
    cross_proj,
    cross_out,
    cross_bias,
    w_up,
    b_up,
    w_down,
    b_down,
    norm_gain,
    norm_bias,
    in_proj,
    in_bias,
):
    pb = lax.axis_index("pb")
    devices = lax.axis_size("pb") * lax.axis_size("dp")
    core = bit_of("dp", 1)
    width = tokens.shape[2]
    mem = features.shape[1]
    cameras = camera_mask.shape[1]
    units = b_up.shape[0]

    def gather(value, axis=1):
        return lax.all_to_all(value, "pb", 0, 1, tiled=True)[0]

    def scatter(value):
        return lax.all_to_all(value[None], "pb", 1, 0, tiled=True)

    up_block = jnp.concatenate([w_up, b_up[None], jnp.zeros((15, units), BF)])
    down_block = jnp.concatenate([w_down, jnp.zeros((16, units), BF)])
    mine = jnp.where(core == 0, up_block, down_block)
    fetched = jnp.stack([swap(mine, "pb", k) for k in range(1, lax.axis_size("pb"))])
    swapped = swap(fetched, "dp", 1)
    ups = jnp.concatenate([up_block[None], jnp.where(core == 0, fetched, swapped)])
    downs = jnp.concatenate([down_block[None], jnp.where(core == 0, swapped, fetched)])[:, :width]
    b_ups = ups[:, width]
    ups = ups[:, :width]

    both = gather(jnp.concatenate([tokens, out_grad], -1))
    inputs_bf = both[:, :width]
    out_cot = both[:, width:].astype(F32)

    positions = query_pos.astype(F32)
    inputs = inputs_bf.astype(F32)

    feats = lax.dynamic_index_in_dim(features, pb, 0, keepdims=False)
    live = lax.dynamic_index_in_dim(camera_mask, pb, 0, keepdims=False)
    live_bias = jnp.where(jnp.repeat(live, mem // cameras) > 0, 0.0, -1000000000.0).astype(F32)
    memory = dot(feats, in_proj) + in_bias
    key_input = (memory + sinusoid(mem, width)).astype(BF)
    value_input = memory.astype(BF)
    cross_k = dot(key_input, cross_proj[1]).astype(BF)
    cross_v = (dot(value_input, cross_proj[2]) + cross_bias[1]).astype(BF)

    attn_input = (inputs + positions).astype(BF)
    self_q = ((dot(attn_input, self_proj[0]) + self_bias[0]) * 0.125).astype(BF)
    self_k = dot(attn_input, self_proj[1]).astype(BF)
    self_v = (dot(inputs_bf, self_proj[2]) + self_bias[1]).astype(BF)
    self_probs = softmax_of(self_q, self_k, 0.0)
    self_mix = mix(self_probs, self_v)
    first_sum = inputs + dot(self_mix, self_out) + self_bias[2]
    hidden_one = layer_norm(first_sum, norm_gain[0].astype(F32), norm_bias[0].astype(F32))

    cross_input = (hidden_one + positions).astype(BF)
    cross_q = ((dot(cross_input, cross_proj[0]) + cross_bias[0]) * 0.125).astype(BF)
    cross_probs = softmax_of(cross_q, cross_k, live_bias)
    cross_mix = mix(cross_probs, cross_v)
    second_sum = hidden_one + dot(cross_mix, cross_out) + cross_bias[2]
    hidden_two = layer_norm(second_sum, norm_gain[1].astype(F32), norm_bias[1].astype(F32))

    ffn_input = hidden_two.astype(BF)
    pre_act = jnp.einsum("nd,pdf->npf", ffn_input, ups, preferred_element_type=F32) + b_ups
    gelu = lambda value: jax.nn.gelu(value, approximate=False)
    activated, gelu_pull = jax.vjp(gelu, pre_act)
    down = jnp.einsum("npf,pdf->nd", activated.astype(BF), downs, preferred_element_type=F32)
    third_sum = hidden_two + down + b_down
    result = layer_norm(
        third_sum, norm_gain[2].astype(F32), norm_bias[2].astype(F32)
    ).astype(BF)

    grad_third, gain_three, shift_three = norm_back(third_sum, norm_gain[2], norm_bias[2], out_cot)
    grad_branch = grad_third.astype(BF)
    grad_bdown = column_sum(grad_branch)
    grad_act = jnp.einsum("nd,pdf->npf", grad_branch, downs, preferred_element_type=F32).astype(BF)
    grad_pre = gelu_pull(grad_act.astype(F32))[0].astype(BF)
    grad_hidden_two = grad_third + jnp.einsum(
        "npf,pdf->nd", grad_pre, ups, preferred_element_type=F32
    )

    rows = jnp.concatenate([ffn_input, grad_branch], -1)
    rows = jnp.concatenate([rows] + [swap(rows, "pb", k) for k in range(1, lax.axis_size("pb"))])
    all_inputs = rows[:, :width]
    all_branch = rows[:, width:]
    part_act, part_pull = jax.vjp(gelu, dot(all_inputs, w_up) + b_up)
    part_grad = part_pull(dot(all_branch, w_down).astype(BF).astype(F32))[0].astype(BF)
    grad_up = dot_rows(all_inputs, part_grad).astype(BF)
    grad_down = dot_rows(all_branch, part_act.astype(BF)).astype(BF)
    grad_bup = column_sum(part_grad)
    ffn_up = lax.psum_scatter(grad_up, "dp", scatter_dimension=0, tiled=True).astype(F32)
    ffn_down = lax.psum_scatter(grad_down, "dp", scatter_dimension=0, tiled=True).astype(F32)

    grad_second, gain_two, shift_two = norm_back(
        second_sum, norm_gain[1], norm_bias[1], grad_hidden_two
    )
    cross_branch = grad_second.astype(BF)
    grad_cross_out = dot_rows(cross_mix, cross_branch)
    grad_cross_mix = dot_back(cross_branch, cross_out).astype(BF)
    grad_cq, grad_ck, grad_cv = attend_back(
        cross_q, cross_k, cross_v, cross_probs, grad_cross_mix
    )
    grad_cq = grad_cq * 0.125
    grad_cross_input = dot_back(grad_cq, cross_proj[0])
    grad_first, gain_one, shift_one = norm_back(
        first_sum, norm_gain[0], norm_bias[0], grad_second + grad_cross_input
    )
    self_branch = grad_first.astype(BF)
    grad_self_out = dot_rows(self_mix, self_branch)
    grad_self_mix = dot_back(self_branch, self_out).astype(BF)
    grad_sq, grad_sk, grad_sv = attend_back(self_q, self_k, self_v, self_probs, grad_self_mix)
    grad_sq = grad_sq * 0.125
    grad_attn_input = dot_back(grad_sq, self_proj[0]) + dot_back(grad_sk, self_proj[1])
    grad_inputs = grad_first + grad_attn_input + dot_back(grad_sv, self_proj[2])
    grad_positions = grad_attn_input + grad_cross_input

    grad_memory = (dot_back(grad_ck, cross_proj[1]) + dot_back(grad_cv, cross_proj[2])).astype(BF)
    grad_features = scatter(dot_back(grad_memory, in_proj).astype(BF))

    outs = scatter(jnp.concatenate([result, grad_inputs.astype(BF)], -1))
    layer_out = outs[..., :width]
    grad_tokens = outs[..., width:]

    full_bup = lax.dynamic_update_slice_in_dim(
        jnp.zeros((units * lax.axis_size("pb"),), F32), grad_bup, pb * units, 0
    )
    pieces = [
        dot_rows(attn_input, grad_sq),
        dot_rows(attn_input, grad_sk),
        dot_rows(inputs_bf, grad_sv),
        grad_self_out,
        dot_rows(cross_input, grad_cq),
        dot_rows(key_input, grad_ck),
        dot_rows(value_input, grad_cv),
        grad_cross_out,
        dot_rows(feats, grad_memory),
        grad_positions,
        column_sum(grad_sq)[None],
        column_sum(grad_sv)[None],
        column_sum(self_branch)[None],
        column_sum(grad_cq)[None],
        column_sum(grad_cv)[None],
        column_sum(cross_branch)[None],
        grad_bdown[None],
        gain_one[None],
        gain_two[None],
        gain_three[None],
        shift_one[None],
        shift_two[None],
        shift_three[None],
        column_sum(grad_memory)[None],
    ]
    bup_rows = -(-full_bup.shape[0] // width)
    pieces.append(
        jnp.pad(full_bup, (0, bup_rows * width - full_bup.shape[0])).reshape(bup_rows, width)
    )
    marks = [0]
    for piece in pieces:
        marks.append(marks[-1] + piece.shape[0])
    spare = -marks[-1] % (devices * 4)
    pieces.append(jnp.zeros((spare, width), F32))
    total = all_sum(jnp.concatenate([piece.astype(BF) for piece in pieces])).astype(F32)
    got = [total[a:b] for a, b in zip(marks[:-1], marks[1:])]

    return (
        layer_out,
        grad_tokens,
        grad_features,
        got[9],
        total[: 3 * width].reshape(3, width, width),
        got[3],
        total[marks[10] : marks[13]],
        total[marks[4] : marks[7]].reshape(3, width, width),
        got[7],
        total[marks[13] : marks[16]],
        ffn_up,
        got[24].reshape(-1)[: full_bup.shape[0]],
        ffn_down,
        got[16][0],
        total[marks[17] : marks[20]],
        total[marks[20] : marks[23]],
        got[8],
        got[23][0],
    )


def solution(mesh):
    return jax.shard_map(
        on_device,
        mesh=mesh,
        in_specs=(
            P("dp", "pb", None),
            P(),
            P("dp", None, None),
            P("dp", None),
            P("dp", "pb", None),
            P(),
            P(),
            P(),
            P(),
            P(),
            P(),
            P(None, "pb"),
            P("pb"),
            P(None, "pb"),
            P(),
            P(),
            P(),
            P(),
            P(),
        ),
        out_specs=(
            P("dp", "pb", None),
            P("dp", "pb", None),
            P("dp", "pb", None),
            P(),
            P(),
            P(),
            P(),
            P(),
            P(),
            P(),
            P("dp", "pb"),
            P(),
            P("dp", "pb"),
            P(),
            P(),
            P(),
            P(),
            P(),
        ),
        check_vma=False,
    )
```

```python
import functools

import jax
import jax.numpy as jnp
import numpy as np
from jax import lax
from jax.experimental import pallas as pl
from jax.experimental.pallas import tpu as pltpu
from jax.sharding import PartitionSpec as P

BF = jnp.bfloat16
F32 = jnp.float32
HEADS = 8
LANES = 128
GROUPS = 4
FAR = -1e30


def dims(left, right, a, b):
    return lax.dot_general(left, right, (((a,), (b,)), ((), ())), preferred_element_type=F32)


def nn(left, right):
    return dims(left, right, 1, 0)


def nt(left, right):
    return dims(left, right, 1, 1)


def tn(left, right):
    return dims(left, right, 0, 0)


def lane_masks(dtype=BF):
    lane = lax.broadcasted_iota(jnp.int32, (1, LANES), 1)
    low = (lane < LANES // 2).astype(F32)
    return low.astype(dtype), (1.0 - low).astype(dtype)


def pair(value, group):
    part = value[:, group * LANES : (group + 1) * LANES]
    low, high = lane_masks()
    return jnp.concatenate([part * low, part * high], axis=0)


def unpair(value):
    rows = value.shape[0] // 2
    lane = lax.broadcasted_iota(jnp.int32, (rows, LANES), 1)
    return jnp.where(lane < LANES // 2, value[:rows], value[rows:])


def eights(value, op):
    return op(value.reshape(value.shape[0] // 8, 8, value.shape[1]), axis=0)


def norm(value):
    center = value - jnp.mean(value, -1, keepdims=True)
    rstd = lax.rsqrt(jnp.mean(center * center, -1, keepdims=True) + 1e-05)
    return center * rstd, rstd


def norm_back(xhat, rstd, gain, grad):
    scaled = grad * gain
    inner = jnp.mean(scaled, -1, keepdims=True) + xhat * jnp.mean(
        scaled * xhat, -1, keepdims=True
    )
    return (
        rstd * (scaled - inner),
        jnp.sum(grad * xhat, 0, keepdims=True),
        jnp.sum(grad, 0, keepdims=True),
    )


def column_sum(value):
    return jnp.sum(value.astype(F32), 0, keepdims=True)


def row(ref, index):
    return ref[index : index + 1, :].astype(F32)


def cdf(value):
    return 0.5 * (1.0 + lax.erf(value * np.float32(0.7071067811865476)))


def density(value):
    return jnp.exp(-0.5 * value * value) * np.float32(0.3989422804014327)


def put_halves(core, value, index, keep_ref, send_ref, scratch):
    half = value.shape[0] // 2
    scratch[...] = value
    mine = pl.multiple_of(core * half, half)
    other = pl.multiple_of((1 - core) * half, half)
    for block in range(value.shape[1] // LANES):
        lanes = slice(block * LANES, (block + 1) * LANES)
        keep_ref[index + block] = scratch[pl.ds(mine, half), lanes].astype(BF)
        send_ref[index + block] = scratch[pl.ds(other, half), lanes].astype(BF)


def memory_kernel(
    ids, feats, table, in_proj, in_bias, cross_proj, cross_bias, featp, ki, vi, k, v, buf, sem
):
    copy = pltpu.make_async_copy(feats.at[ids[0]], buf, sem)
    copy.start()
    copy.wait()
    slots = buf.shape[0]
    blocks = GROUPS
    part = slots // blocks
    padded = featp.shape[0] // blocks
    for j in range(blocks):
        here = slice(j * padded, (j + 1) * padded)
        featp[(j + 1) * padded - 16 : (j + 1) * padded] = jnp.zeros((16, featp.shape[1]), BF)
        featp[j * padded : j * padded + part] = buf[j * part : (j + 1) * part]
        memory = nn(featp[here], in_proj[...]) + in_bias[...].astype(F32)
        key_input = (memory + table[here]).astype(BF)
        value_input = memory.astype(BF)
        ki[here] = key_input
        vi[here] = value_input
        k[here] = nn(key_input, cross_proj[1]).astype(BF)
        v[here] = (nn(value_input, cross_proj[2]) + row(cross_bias, 1)).astype(BF)


def forward_kernel(
    ids,
    mask,
    own,
    got1,
    got2,
    got3,
    pos_ref,
    self_proj,
    self_out,
    self_bias,
    cross_proj,
    cross_out,
    cross_bias,
    gains,
    shifts,
    k_ref,
    v_ref,
    x_out,
    cot_out,
    ai_out,
    sq_out,
    sk_out,
    sv_out,
    ps_out,
    sm_out,
    xhat1_out,
    rstd1_out,
    ci_out,
    cq_out,
    pc_out,
    cm_out,
    h2_out,
    xhat2_out,
    rstd2_out,
    scores,
    *,
    rows_used,
):
    pb = ids[0]
    width = pos_ref.shape[1]
    block = own.shape[0]
    for k, ref in enumerate((own, got1, got2, got3)):
        at = pl.multiple_of((pb ^ k) * block, block)
        x_out[pl.ds(at, block), :] = ref[:, :width]
        cot_out[pl.ds(at, block), :] = ref[:, width:]
    rows = x_out.shape[0]
    pos = pos_ref[...].astype(F32)
    x = x_out[...].astype(F32)
    ai = (x + pos).astype(BF)
    ai_out[...] = ai
    sq_out[...] = ((nn(ai, self_proj[0]) + row(self_bias, 0)) * 0.125).astype(BF)
    sk_out[...] = nn(ai, self_proj[1]).astype(BF)
    sv_out[...] = (nn(x_out[...], self_proj[2]) + row(self_bias, 1)).astype(BF)
    key_row = lax.broadcasted_iota(jnp.int32, (rows, 2 * rows), 0)
    spare = jnp.where(lax.rem(key_row, block) < rows_used, 0.0, FAR).astype(F32)
    for g in range(GROUPS):
        lanes = slice(g * LANES, (g + 1) * LANES)
        s = nt(sk_out[:, lanes], pair(sq_out[...], g)) + spare
        e = jnp.exp(s - jnp.max(s, 0, keepdims=True))
        p = (e * (1.0 / jnp.sum(e, 0, keepdims=True))).astype(BF)
        ps_out[g] = p
        sm_out[:, lanes] = unpair(tn(p, sv_out[:, lanes])).astype(BF)
    xhat, rstd = norm(x + nn(sm_out[...], self_out[...]) + row(self_bias, 2))
    xhat1_out[...] = xhat
    rstd1_out[...] = rstd
    h1 = xhat * row(gains, 0) + row(shifts, 0)
    ci = (h1 + pos).astype(BF)
    ci_out[...] = ci
    cq_out[...] = ((nn(ci, cross_proj[0]) + row(cross_bias, 0)) * 0.125).astype(BF)

    padded = k_ref.shape[0] // GROUPS
    used = rows_used * 12
    slot_row = lax.broadcasted_iota(jnp.int32, (padded, 2 * rows), 0)
    for g in range(GROUPS):
        lanes = slice(g * LANES, (g + 1) * LANES)
        queries = pair(cq_out[...], g)
        top = jnp.full((8, 2 * rows), FAR, F32)
        for j in range(GROUPS):
            here = slice(j * padded, (j + 1) * padded)
            live = jnp.where(mask[pb, j] > 0, 0.0, -1000000000.0).astype(F32)
            s = nt(k_ref[here, lanes], queries) + jnp.where(slot_row < used, live, FAR)
            scores[here] = s
            top = jnp.maximum(top, eights(s, jnp.max))
        top = jnp.max(top, 0, keepdims=True)
        total = jnp.zeros((8, 2 * rows), F32)
        for j in range(GROUPS):
            here = slice(j * padded, (j + 1) * padded)
            e = jnp.exp(scores[here] - top)
            scores[here] = e
            total = total + eights(e, jnp.sum)
        inverse = 1.0 / jnp.sum(total, 0, keepdims=True)
        for j in range(GROUPS):
            here = slice(j * padded, (j + 1) * padded)
            pc_out[g, here] = (scores[here] * inverse).astype(BF)
        cm_out[:, lanes] = unpair(tn(pc_out[g], v_ref[:, lanes])).astype(BF)
    xhat, rstd = norm(h1 + nn(cm_out[...], cross_out[...]) + row(cross_bias, 2))
    xhat2_out[...] = xhat
    rstd2_out[...] = rstd
    h2_out[...] = xhat * row(gains, 1) + row(shifts, 1)


def ffn_kernel(
    ids,
    h2_ref,
    cot_ref,
    xhat2_ref,
    rstd2_ref,
    w_up,
    b_up,
    w_down,
    b_down,
    gains,
    shifts,
    fx,
    fy,
    fdx,
    fdy,
    sx,
    sy,
    sdx,
    sdy,
    res_out,
    ops_out,
    g2_out,
    small_out,
    weights,
    pre_ref,
    sems,
):
    core = ids[1]
    width = h2_ref.shape[1]
    half = fdx.shape[0]
    full = fx.shape[0]
    copies = []
    for side, (rx, ry, rdx, rdy) in enumerate(((fx, fy, fdx, fdy), (sx, sy, sdx, sdy))):
        to = core if side == 0 else 1 - core
        copies.append(
            [
                pltpu.make_async_copy(rx, weights.at[to, 0], sems.at[side, 0]),
                pltpu.make_async_copy(ry, weights.at[to, 1], sems.at[side, 1]),
                pltpu.make_async_copy(
                    rdx, weights.at[to, 2, pl.ds(0, half)], sems.at[side, 2]
                ),
                pltpu.make_async_copy(
                    rdy, weights.at[to, 2, pl.ds(half, full - half)], sems.at[side, 3]
                ),
            ]
        )
    for one in copies:
        for copy in one:
            copy.start()
    h2 = h2_ref[...]
    h2b = h2.astype(BF)
    ops_out[:, :width] = h2b
    down = jnp.zeros(h2.shape, F32)
    waits = ([], [0], [1], [2, 3])
    for p in range(4):
        for index in waits[p]:
            copies[0][index].wait()
            copies[1][index].wait()
        up = w_up[...] if p == 0 else weights[0, p - 1, :width]
        bias = b_up[...] if p == 0 else weights[0, p - 1, width : width + 1]
        dn = w_down[...] if p == 0 else weights[1, p - 1, :width]
        pre = nn(h2b, up) + bias.astype(F32)
        pre_ref[p] = pre
        down = down + nt((pre * cdf(pre)).astype(BF), dn)
    xhat, rstd = norm(h2 + down + b_down[...].astype(F32))
    res_out[...] = (xhat * row(gains, 2) + row(shifts, 2)).astype(BF)
    g3, dgain3, dshift3 = norm_back(xhat, rstd, row(gains, 2), cot_ref[...].astype(F32))
    gb = g3.astype(BF)
    ops_out[:, width:] = gb
    gh = g3
    for p in range(4):
        up = w_up[...] if p == 0 else weights[0, p - 1, :width]
        dn = w_down[...] if p == 0 else weights[1, p - 1, :width]
        ga = nn(gb, dn).astype(BF).astype(F32)
        pre = pre_ref[p]
        gp = (ga * (cdf(pre) + pre * density(pre))).astype(BF)
        gh = gh + nt(gp, up)
    g2, dgain2, dshift2 = norm_back(xhat2_ref[...], rstd2_ref[...], row(gains, 1), gh)
    g2_out[...] = g2
    small_out[0:1] = dgain3
    small_out[1:2] = dshift3
    small_out[2:3] = dgain2
    small_out[3:4] = dshift2
    small_out[4:5] = column_sum(gb)
    small_out[5:6] = column_sum(g2.astype(BF))
    small_out[6:8] = jnp.zeros((2, width), F32)


def backward_kernel(
    ids,
    g2_ref,
    pc_ref,
    k_ref,
    v_ref,
    cq_ref,
    ci_ref,
    cm_ref,
    xhat1_ref,
    rstd1_ref,
    x_ref,
    ai_ref,
    sq_ref,
    sk_ref,
    sv_ref,
    ps_ref,
    sm_ref,
    self_proj,
    self_out,
    cross_proj,
    cross_out,
    gains,
    ds_out,
    gcm_out,
    gx_out,
    gpos_out,
    small_out,
    keep1,
    send1,
    keep2,
    send2,
    dp_ref,
    work,
    gq_ref,
    gk_ref,
    gv_ref,
):
    core = ids[1]
    width = x_ref.shape[1]
    rows = x_ref.shape[0]
    g2 = g2_ref[...]
    branch = g2.astype(BF)
    gcm_out[...] = nt(branch, cross_out[...]).astype(BF)
    padded = k_ref.shape[0] // GROUPS
    for g in range(GROUPS):
        lanes = slice(g * LANES, (g + 1) * LANES)
        grads = pair(gcm_out[...], g)
        total = jnp.zeros((8, 2 * rows), F32)
        for j in range(GROUPS):
            here = slice(j * padded, (j + 1) * padded)
            dp = nt(v_ref[here, lanes], grads).astype(BF)
            dp_ref[here] = dp
            total = total + eights(pc_ref[g, here].astype(F32) * dp.astype(F32), jnp.sum)
        total = jnp.sum(total, 0, keepdims=True)
        for j in range(GROUPS):
            here = slice(j * padded, (j + 1) * padded)
            ds_out[g, here] = (
                pc_ref[g, here].astype(F32) * (dp_ref[here].astype(F32) - total)
            ).astype(BF)
        gq_ref[:, lanes] = unpair(tn(ds_out[g], k_ref[:, lanes])).astype(BF) * 0.125
    gcq = gq_ref[...]
    gci = nt(gcq, cross_proj[0])
    small_out[0:1] = column_sum(gcq)
    put_halves(core, tn(ci_ref[...], gcq), 0, keep1, send1, work)
    put_halves(core, tn(cm_ref[...], branch), 8, keep1, send1, work)
    g1, dgain1, dshift1 = norm_back(xhat1_ref[...], rstd1_ref[...], row(gains, 0), g2 + gci)
    small_out[1:2] = dgain1
    small_out[2:3] = dshift1
    sbranch = g1.astype(BF)
    small_out[3:4] = column_sum(sbranch)
    put_halves(core, tn(sm_ref[...], sbranch), 4, keep1, send1, work)
    gsm = nt(sbranch, self_out[...]).astype(BF)
    for g in range(GROUPS):
        lanes = slice(g * LANES, (g + 1) * LANES)
        grads = pair(gsm, g)
        p = ps_ref[g]
        dp = nt(sv_ref[:, lanes], grads).astype(BF).astype(F32)
        pf = p.astype(F32)
        ds = (pf * (dp - jnp.sum(pf * dp, 0, keepdims=True))).astype(BF)
        gq_ref[:, lanes] = unpair(tn(ds, sk_ref[:, lanes])).astype(BF) * 0.125
        gk_ref[:, lanes] = nn(ds, pair(sq_ref[...], g)).astype(BF)
        gv_ref[:, lanes] = nn(p, grads).astype(BF)
    gq, gk, gv = gq_ref[...], gk_ref[...], gv_ref[...]
    gai = nt(gq, self_proj[0]) + nt(gk, self_proj[1])
    gx_out[...] = (g1 + gai + nt(gv, self_proj[2])).astype(BF)
    gpos_out[...] = gai + gci
    small_out[4:5] = column_sum(gq)
    small_out[5:6] = column_sum(gv)
    small_out[6:8] = jnp.zeros((2, width), F32)
    put_halves(core, tn(ai_ref[...], gq), 0, keep2, send2, work)
    put_halves(core, tn(ai_ref[...], gk), 4, keep2, send2, work)
    put_halves(core, tn(x_ref[...], gv), 8, keep2, send2, work)


def ffn_grad_kernel(
    ids, own, got1, got2, got3, w_up, b_up, w_down, keep, send, bup_out, work
):
    core = ids[1]
    width = w_up.shape[0]
    ops = jnp.concatenate([ref[...] for ref in (own, got1, got2, got3)], axis=0)
    inputs, branch = ops[:, :width], ops[:, width:]
    pre = nn(inputs, w_up[...]) + b_up[...].astype(F32)
    phi = cdf(pre)
    act = (pre * phi).astype(BF)
    gact = nn(branch, w_down[...]).astype(BF).astype(F32)
    gpre = (gact * (phi + pre * density(pre))).astype(BF)
    bup_out[...] = column_sum(gpre)
    blocks, size = keep.shape[1], keep.shape[2]
    for side, grad in enumerate((tn(inputs, gpre), tn(branch, act))):
        work[...] = grad
        for block in range(blocks):
            mine = pl.multiple_of((2 * block + core) * size, size)
            other = pl.multiple_of((2 * block + 1 - core) * size, size)
            keep[side, block] = work[pl.ds(mine, size), :].astype(BF)
            send[side, block] = work[pl.ds(other, size), :].astype(BF)


def memory_back_kernel(
    ids,
    ds_ref,
    pc_ref,
    cq_ref,
    gcm_ref,
    featp,
    ki,
    vi,
    cross_proj,
    in_proj,
    res_ref,
    gx_ref,
    gpos_ref,
    small_a,
    small_b,
    bup,
    rows_out,
    keep,
    send,
    gk_ref,
    gv_ref,
    gm_ref,
    work,
    small,
    *,
    rows_used,
):
    pb, core = ids[0], ids[1]
    width = featp.shape[1]
    rows = res_ref.shape[0]
    block = rows // GROUPS
    padded = featp.shape[0] // GROUPS
    pairs_q = [pair(cq_ref[...], g) for g in range(GROUPS)]
    pairs_g = [pair(gcm_ref[...], g) for g in range(GROUPS)]
    for j in range(GROUPS):
        here = slice(j * padded, (j + 1) * padded)
        for g in range(GROUPS):
            lanes = slice(g * LANES, (g + 1) * LANES)
            gk_ref[here, lanes] = nn(ds_ref[g, here], pairs_q[g]).astype(BF)
            gv_ref[here, lanes] = nn(pc_ref[g, here], pairs_g[g]).astype(BF)
        gm = (nt(gk_ref[here], cross_proj[1]) + nt(gv_ref[here], cross_proj[2])).astype(BF)
        gm_ref[here] = gm
        to = j ^ pb
        rows_out[to, 0:padded] = nt(gm, in_proj[...]).astype(BF)
        rows_out[to, padded : padded + block] = gx_ref[j * block : (j + 1) * block]
        rows_out[to, padded + block : padded + 2 * block] = res_ref[j * block : (j + 1) * block]
    put_halves(core, tn(ki[...], gk_ref[...]), 0, keep, send, work)
    put_halves(core, tn(vi[...], gv_ref[...]), 4, keep, send, work)
    put_halves(core, tn(featp[...], gm_ref[...]), 8, keep, send, work)

    small[...] = gpos_ref[...]
    extras = [
        row(small_b, 1),
        row(small_a, 2),
        row(small_a, 0),
        row(small_b, 2),
        row(small_a, 3),
        row(small_a, 1),
        row(small_b, 4),
        row(small_b, 5),
        row(small_b, 3),
        row(small_b, 0),
        column_sum(gv_ref[...]),
        row(small_a, 5),
        row(small_a, 4),
        column_sum(gm_ref[...]),
    ]
    for index, value in enumerate(extras):
        at = spare_row(index, block, rows_used)
        small[at : at + 1] = value
    units = bup.shape[1]
    for b in range(GROUPS):
        mine = jnp.where(pb == b, 1.0, 0.0).astype(F32)
        at = b * block + rows_used + 5
        small[at : at + 1] = bup[:, :width] * mine
        small[at + 1 : at + 2] = jnp.concatenate(
            [bup[:, width:] * mine, jnp.zeros((1, 2 * width - units), F32)], axis=1
        )
    for b in range(2):
        for side, ref in ((core, keep), (1 - core, send)):
            low = small[:, b * LANES : (b + 1) * LANES]
            high = small[:, (2 + b) * LANES : (3 + b) * LANES]
            ref[12, b * rows : (b + 1) * rows] = jnp.where(side == 0, low, high).astype(BF)


def spare_row(index, block, rows_used):
    return index // 5 * block + rows_used + index % 5


def finish_kernel(
    ids, own1, got1, own3, got3, cross_out_, self_out_, ccross_, in_, small_, *, rows
):
    core = ids[1]
    half = own1.shape[1]
    mine = pl.multiple_of(core * half, half)
    other = pl.multiple_of((1 - core) * half, half)

    def put(index, refs, own, got):
        for b in range(4):
            lanes = slice(b * LANES, (b + 1) * LANES)
            refs[pl.ds(mine, half), lanes] = own[index + b].astype(F32)
            refs[pl.ds(other, half), lanes] = got[index + b].astype(F32)

    put(0, cross_out_.at[0], own1, got1)
    put(4, self_out_, own1, got1)
    put(8, ccross_, own1, got1)
    put(0, cross_out_.at[1], own3, got3)
    put(4, cross_out_.at[2], own3, got3)
    put(8, in_, own3, got3)
    for b in range(2):
        here = slice(b * rows, (b + 1) * rows)
        first = own3[12, here].astype(F32)
        second = got3[12, here].astype(F32)
        small_[:, b * LANES : (b + 1) * LANES] = jnp.where(core == 0, first, second)
        small_[:, (2 + b) * LANES : (3 + b) * LANES] = jnp.where(core == 0, second, first)


def finish_self_kernel(ids, own, got, out):
    core = ids[1]
    half = own.shape[1]
    mine = pl.multiple_of(core * half, half)
    other = pl.multiple_of((1 - core) * half, half)
    for m in range(3):
        for b in range(4):
            lanes = slice(b * LANES, (b + 1) * LANES)
            out[m, pl.ds(mine, half), lanes] = own[m * 4 + b].astype(F32)
            out[m, pl.ds(other, half), lanes] = got[m * 4 + b].astype(F32)


def call(kernel, args, outs, scratch=(), smem=1, hbm=(), flops=0):
    specs = []
    for index in range(len(args)):
        space = pltpu.SMEM if index < smem else pl.ANY if index in hbm else pltpu.VMEM
        specs.append(pl.BlockSpec(memory_space=space))
    size = lambda shape, dtype: int(np.prod(shape)) * jnp.dtype(dtype).itemsize
    moved = sum(size(a.shape, a.dtype) for a in args) + sum(size(*o) for o in outs)
    return pl.pallas_call(
        kernel,
        out_shape=[jax.ShapeDtypeStruct(*o) for o in outs],
        in_specs=specs,
        out_specs=[pl.BlockSpec(memory_space=pltpu.VMEM)] * len(outs),
        scratch_shapes=list(scratch),
        compiler_params=pltpu.CompilerParams(vmem_limit_bytes=60 * 1024 * 1024),
        cost_estimate=pl.CostEstimate(flops=flops, bytes_accessed=moved, transcendentals=0),
    )(*args)


def swap(value, axis, bit):
    size = lax.axis_size(axis)
    return lax.ppermute(value, axis, [(i, i ^ bit) for i in range(size)])


def bit_of(axis, bit):
    return (lax.axis_index(axis) // bit) % 2


def plus(left, right):
    return (left.astype(F32) + right.astype(F32)).astype(BF)


def halve(value, axis, bit, dim):
    mine = bit_of(axis, bit)
    half = value.shape[dim] // 2
    keep = lax.dynamic_slice_in_dim(value, mine * half, half, dim)
    send = lax.dynamic_slice_in_dim(value, (1 - mine) * half, half, dim)
    return plus(keep, swap(send, axis, bit))


def double(value, axis, bit, dim):
    other = swap(value, axis, bit)
    mine = bit_of(axis, bit)
    return jnp.where(
        mine == 0,
        jnp.concatenate([value, other], dim),
        jnp.concatenate([other, value], dim),
    )


def sinusoid(count, model_width):
    places = np.arange(count).astype(np.float32)[:, None]
    column = np.arange(model_width)
    exponent = (column // 2 * 2).astype(np.float32) / np.float32(model_width)
    angle = places / np.float32(10000.0) ** exponent
    return np.where(column % 2 == 0, np.sin(angle), np.cos(angle)).astype(np.float32)


def on_device(
    tokens,
    query_pos,
    features,
    camera_mask,
    out_grad,
    self_proj,
    self_out,
    self_bias,
    cross_proj,
    cross_out,
    cross_bias,
    w_up,
    b_up,
    w_down,
    b_down,
    norm_gain,
    norm_bias,
    in_proj,
    in_bias,
):
    pb = lax.axis_index("pb")
    pb_size = lax.axis_size("pb")
    dp_size = lax.axis_size("dp")
    core = bit_of("dp", 1)
    ids = jnp.stack([pb, core]).astype(jnp.int32)
    width = tokens.shape[2]
    used = tokens.shape[1]
    block = -(-used // 16) * 16
    rows = block * pb_size
    mem = features.shape[1]
    part = mem // pb_size
    padded = -(-part // 16) * 16
    slots = padded * pb_size
    units = b_up.shape[0]
    half_row = lambda value: value.reshape(1, -1)

    tail = jnp.zeros((31, units), BF)
    mine = jnp.where(
        core == 0,
        jnp.concatenate([w_up, half_row(b_up), tail]),
        jnp.concatenate([w_down, half_row(b_up), tail]),
    )
    cut = mine.shape[0] // 2
    both = jnp.pad(
        jnp.concatenate([tokens, out_grad], -1), ((0, 0), (0, block - used), (0, 0))
    )
    send = [lax.dynamic_index_in_dim(both, pb ^ k, 0, keepdims=False) for k in range(pb_size)]
    got = [send[0]] + [swap(send[k], "pb", k) for k in range(1, pb_size)]
    fx = swap(mine, "pb", 1)
    fy = swap(mine, "pb", 2)
    fdx = swap(fy[:cut], "pb", 1)
    fdy = swap(fx[cut:], "pb", 2)
    sx, sy, sdx, sdy = [swap(value, "dp", 1) for value in (fx, fy, fdx, fdy)]

    pos = jnp.pad(
        query_pos.reshape(pb_size, used, width), ((0, 0), (0, block - used), (0, 0))
    ).reshape(rows, width)
    table = np.zeros((pb_size, padded, width), np.float32)
    table[:, :part] = sinusoid(mem, width).reshape(pb_size, part, width)
    table = jnp.asarray(table.reshape(slots, width))

    wide = (slots, width)
    featp, ki, vi, ck, cv = call(
        memory_kernel,
        [ids, features, table, in_proj, half_row(in_bias), cross_proj, cross_bias],
        [(wide, BF)] * 5,
        scratch=[pltpu.VMEM((mem, width), BF), pltpu.SemaphoreType.DMA],
        hbm=(1,),
        flops=6 * slots * width * width,
    )
    flat = (rows, width)
    scores = (GROUPS, slots, 2 * rows)
    (x, cot, ai, sq, sk, sv, ps, sm, xhat1, rstd1, ci, cq, pc, cm, h2, xhat2, rstd2) = call(
        functools.partial(forward_kernel, rows_used=used),
        [
            ids,
            camera_mask,
            *got,
            pos,
            self_proj,
            self_out,
            self_bias,
            cross_proj,
            cross_out,
            cross_bias,
            norm_gain,
            norm_bias,
            ck,
            cv,
        ],
        [
            (flat, BF),
            (flat, BF),
            (flat, BF),
            (flat, BF),
            (flat, BF),
            (flat, BF),
            ((GROUPS, rows, 2 * rows), BF),
            (flat, BF),
            (flat, F32),
            ((rows, 1), F32),
            (flat, BF),
            (flat, BF),
            (scores, BF),
            (flat, BF),
            (flat, F32),
            (flat, F32),
            ((rows, 1), F32),
        ],
        scratch=[pltpu.VMEM((slots, 2 * rows), F32)],
        smem=2,
        flops=12 * rows * width * width + 8 * rows * slots * width,
    )
    res, ops, g2, small_a = call(
        ffn_kernel,
        [
            ids,
            h2,
            cot,
            xhat2,
            rstd2,
            w_up,
            half_row(b_up),
            w_down,
            half_row(b_down),
            norm_gain,
            norm_bias,
            fx,
            fy,
            fdx,
            fdy,
            sx,
            sy,
            sdx,
            sdy,
        ],
        [(flat, BF), ((rows, 2 * width), BF), (flat, F32), ((8, width), F32)],
        scratch=[
            pltpu.VMEM((2, 3, mine.shape[0], units), BF),
            pltpu.VMEM((4, rows, units), F32),
            pltpu.SemaphoreType.DMA((2, 4)),
        ],
        hbm=tuple(range(11, 19)),
        flops=32 * rows * width * units,
    )
    others = [swap(ops, "pb", k) for k in range(1, pb_size)]
    halves = ((12, width // 2, LANES), BF)
    ds, gcm, gx, gpos, small_b, keep1, send1, keep2, send2 = call(
        backward_kernel,
        [
            ids,
            g2,
            pc,
            ck,
            cv,
            cq,
            ci,
            cm,
            xhat1,
            rstd1,
            x,
            ai,
            sq,
            sk,
            sv,
            ps,
            sm,
            self_proj,
            self_out,
            cross_proj,
            cross_out,
            norm_gain,
        ],
        [
            (scores, BF),
            (flat, BF),
            (flat, BF),
            (flat, F32),
            ((8, width), F32),
            halves,
            halves,
            halves,
            halves,
        ],
        scratch=[
            pltpu.VMEM((slots, 2 * rows), BF),
            pltpu.VMEM((width, width), F32),
            pltpu.VMEM(flat, BF),
            pltpu.VMEM(flat, BF),
            pltpu.VMEM(flat, BF),
        ],
        flops=24 * rows * width * width + 8 * rows * slots * width,
    )
    piece = width // dp_size
    fhalf = ((2, dp_size // 2, piece, units), BF)
    fkeep, fsend, bup = call(
        ffn_grad_kernel,
        [ids, ops, *others, w_up, half_row(b_up), w_down],
        [fhalf, fhalf, ((1, units), F32)],
        scratch=[pltpu.VMEM((width, units), F32)],
        flops=8 * pb_size * rows * width * units,
    )
    halves3 = ((13, width // 2, LANES), BF)
    rows_out, keep3, send3 = call(
        functools.partial(memory_back_kernel, rows_used=used),
        [ids, ds, pc, cq, gcm, featp, ki, vi, cross_proj, in_proj, res, gx, gpos, small_a, small_b, bup],
        [((pb_size, padded + 2 * block, width), BF), halves3, halves3],
        scratch=[
            pltpu.VMEM(wide, BF),
            pltpu.VMEM(wide, BF),
            pltpu.VMEM(wide, BF),
            pltpu.VMEM((width, width), F32),
            pltpu.VMEM(flat, F32),
        ],
        flops=12 * slots * width * width + 8 * rows * slots * width,
    )

    later = [("dp", 1 << i) for i in range(2, dp_size.bit_length() - 1)]
    first = [("pb", 1), ("pb", 2), ("dp", 2)]
    orders = [first[i:] + first[:i] + later for i in range(3)]
    parts = [
        plus(keep, swap(send, "dp", 1))
        for keep, send in ((keep1, send1), (keep2, send2), (keep3, send3))
    ]
    for step in range(len(first + later)):
        parts = [halve(value, *order[step], 1) for value, order in zip(parts, orders)]
    ffn = plus(fkeep, swap(fsend, "dp", 1))
    for axis, bit in reversed([first[2]] + later):
        ffn = halve(ffn, axis, bit, 1)
    for step in reversed(range(len(first + later))):
        parts = [double(value, *order[step], 1) for value, order in zip(parts, orders)]
    swapped = [swap(value, "dp", 1) for value in parts]
    matrix = ((width, width), F32)
    three = ((3, width, width), F32)
    (g_self_proj,) = call(finish_self_kernel, [ids, parts[1], swapped[1]], [three])
    g_cross_proj, g_self_out, g_cross_out, g_in_proj, small = call(
        functools.partial(finish_kernel, rows=rows),
        [ids, parts[0], swapped[0], parts[2], swapped[2]],
        [three, matrix, matrix, matrix, (flat, F32)],
    )

    arrived = [rows_out[0]] + [swap(rows_out[k], "pb", k) for k in range(1, pb_size)]
    arrived = jnp.stack(arrived)
    ordered = jnp.stack(
        [lax.dynamic_index_in_dim(arrived, pb ^ e, 0, keepdims=False) for e in range(pb_size)]
    )
    spare = lambda index, count=1: jnp.stack(
        [small[spare_row(i, block, used)] for i in range(index, index + count)]
    )
    bup_rows = [
        small[b * block + used + 5 : b * block + used + 7].reshape(-1)[:units]
        for b in range(pb_size)
    ]
    return (
        ordered[:, padded + block : padded + block + used],
        ordered[:, padded : padded + used],
        ordered[:, :part],
        small.reshape(pb_size, block, width)[:, :used].reshape(query_pos.shape),
        g_self_proj,
        g_self_out,
        spare(6, 3),
        g_cross_proj,
        g_cross_out,
        spare(9, 3),
        ffn[0].reshape(piece, units).astype(F32),
        jnp.concatenate(bup_rows),
        ffn[1].reshape(piece, units).astype(F32),
        spare(12)[0],
        spare(0, 3),
        spare(3, 3),
        g_in_proj,
        spare(13)[0],
    )


def solution(mesh):
    return jax.shard_map(
        on_device,
        mesh=mesh,
        in_specs=(
            P("dp", "pb", None),
            P(),
            P("dp", None, None),
            P("dp", None),
            P("dp", "pb", None),
            P(),
            P(),
            P(),
            P(),
            P(),
            P(),
            P(None, "pb"),
            P("pb"),
            P(None, "pb"),
            P(),
            P(),
            P(),
            P(),
            P(),
        ),
        out_specs=(
            P("dp", "pb", None),
            P("dp", "pb", None),
            P("dp", "pb", None),
            P(),
            P(),
            P(),
            P(),
            P(),
            P(),
            P(),
            P("dp", "pb"),
            P(),
            P("dp", "pb"),
            P(),
            P(),
            P(),
            P(),
            P(),
        ),
        check_vma=False,
    )
```

```python
import functools

import jax
import jax.numpy as jnp
import numpy as np
from jax import lax
from jax.experimental import pallas as pl
from jax.experimental.pallas import tpu as pltpu
from jax.sharding import PartitionSpec as P

BF = jnp.bfloat16
F32 = jnp.float32
HEADS = 8
LANES = 128
GROUPS = 4
FAR = -1e30


def dims(left, right, a, b):
    return lax.dot_general(left, right, (((a,), (b,)), ((), ())), preferred_element_type=F32)


def nn(left, right):
    return dims(left, right, 1, 0)


def nt(left, right):
    return dims(left, right, 1, 1)


def tn(left, right):
    return dims(left, right, 0, 0)


def lane_masks(dtype=BF):
    lane = lax.broadcasted_iota(jnp.int32, (1, LANES), 1)
    low = (lane < LANES // 2).astype(F32)
    return low.astype(dtype), (1.0 - low).astype(dtype)


def pair(value, group):
    part = value[:, group * LANES : (group + 1) * LANES]
    low, high = lane_masks()
    return jnp.concatenate([part * low, part * high], axis=0)


def unpair(value):
    rows = value.shape[0] // 2
    lane = lax.broadcasted_iota(jnp.int32, (rows, LANES), 1)
    return jnp.where(lane < LANES // 2, value[:rows], value[rows:])


def eights(value, op):
    return op(value.reshape(value.shape[0] // 8, 8, value.shape[1]), axis=0)


def norm(value):
    center = value - jnp.mean(value, -1, keepdims=True)
    rstd = lax.rsqrt(jnp.mean(center * center, -1, keepdims=True) + 1e-05)
    return center * rstd, rstd


def norm_back(xhat, rstd, gain, grad):
    scaled = grad * gain
    inner = jnp.mean(scaled, -1, keepdims=True) + xhat * jnp.mean(
        scaled * xhat, -1, keepdims=True
    )
    return (
        rstd * (scaled - inner),
        jnp.sum(grad * xhat, 0, keepdims=True),
        jnp.sum(grad, 0, keepdims=True),
    )


def column_sum(value):
    return jnp.sum(value.astype(F32), 0, keepdims=True)


def row(ref, index):
    return ref[index : index + 1, :].astype(F32)


def cdf(value):
    return 0.5 * (1.0 + lax.erf(value * np.float32(0.7071067811865476)))


def density(value):
    return jnp.exp(-0.5 * value * value) * np.float32(0.3989422804014327)


def put_halves(core, value, index, keep_ref, send_ref, scratch):
    half = value.shape[0] // 2
    scratch[...] = value
    mine = pl.multiple_of(core * half, half)
    other = pl.multiple_of((1 - core) * half, half)
    for block in range(value.shape[1] // LANES):
        lanes = slice(block * LANES, (block + 1) * LANES)
        keep_ref[index + block] = scratch[pl.ds(mine, half), lanes].astype(BF)
        send_ref[index + block] = scratch[pl.ds(other, half), lanes].astype(BF)


def start_kernel(
    ids, up, down, tokens, cots, misc, send0, send1, send2, send3, first, second, turned, sems, *, rows_used
):
    pb, core = ids[0], ids[1]
    cut = first.shape[0]
    for side, ref in enumerate((up, down)):

        @pl.when(core == side)
        def _():
            one = pltpu.make_async_copy(ref.at[pl.ds(0, cut)], first, sems.at[0])
            two = pltpu.make_async_copy(ref.at[pl.ds(cut, cut)], second, sems.at[1])
            one.start()
            two.start()
            one.wait()
            two.wait()

    rows, width2 = turned.shape
    width = width2 // 2
    block = rows // GROUPS
    count = tokens.shape[0]
    place = lax.broadcasted_iota(jnp.int32, (rows, count), 0)
    query = lax.broadcasted_iota(jnp.int32, (rows, count), 1)
    hit = query == lax.rem(place, block) * GROUPS + lax.div(place, block)
    used = lax.rem(place, block) < rows_used
    chosen = jnp.where(jnp.logical_and(hit, used), 1.0, 0.0).astype(BF)
    turned[:, :width] = nn(chosen, tokens[...])
    turned[:, width:] = nn(chosen, cots[...])
    for b in range(GROUPS):
        at = b * block + rows_used
        turned[at : at + 2, :width] = misc[2:4, :].astype(F32)
    for k, ref in enumerate((send0, send1, send2, send3)):
        at = pl.multiple_of((pb ^ k) * block, block)
        ref[...] = turned[pl.ds(at, block), :].astype(BF)


def memory_kernel(
    ids, feats, sines, cosines, waves, in_proj, misc, cross_proj, cross_bias, featp, ki, vi, k, v, buf, sems
):
    blocks = GROUPS
    slots = buf.shape[0]
    part = slots // blocks
    padded = featp.shape[0] // blocks
    copy = pltpu.make_async_copy(feats.at[ids[0]], buf, sems)
    copy.start()
    for j in range(blocks):
        featp[(j + 1) * padded - 16 : (j + 1) * padded] = jnp.zeros((16, featp.shape[1]), BF)
    copy.wait()
    bias = row(misc, 0)
    for j in range(blocks):
        here = slice(j * padded, (j + 1) * padded)
        featp[j * padded : j * padded + part] = buf[j * part : (j + 1) * part]
        memory = nn(featp[here], in_proj[...]) + bias
        places = cosines[...] * row(waves, j) + sines[...] * row(waves, blocks + j)
        key_input = (memory + places).astype(BF)
        value_input = memory.astype(BF)
        ki[here] = key_input
        vi[here] = value_input
        k[here] = nn(key_input, cross_proj[1]).astype(BF)
        v[here] = (nn(value_input, cross_proj[2]) + row(cross_bias, 1)).astype(BF)


def forward_kernel(
    ids,
    own,
    got1,
    got2,
    got3,
    query_pos,
    self_proj,
    self_out,
    self_bias,
    cross_proj,
    cross_out,
    cross_bias,
    gains,
    shifts,
    k_ref,
    v_ref,
    up_,
    down_,
    x_out,
    cot_out,
    ai_out,
    sq_out,
    sk_out,
    sv_out,
    ps_out,
    sm_out,
    xhat1_out,
    rstd1_out,
    ci_out,
    cq_out,
    pc_out,
    cm_out,
    h2_out,
    xhat2_out,
    rstd2_out,
    bups_out,
    scores,
    pos_ref,
    *,
    rows_used,
    mask_at,
):
    pb = ids[0]
    width = pos_ref.shape[1]
    block = own.shape[0]
    for k, ref in enumerate((own, got1, got2, got3)):
        at = pl.multiple_of((pb ^ k) * block, block)
        x_out[pl.ds(at, block), :] = ref[:, :width]
        cot_out[pl.ds(at, block), :] = ref[:, width:]
        bups_out[2 * k : 2 * k + 2] = ref[rows_used : rows_used + 2, :width].astype(F32)
    rows = x_out.shape[0]
    pos_ref[...] = jnp.zeros(pos_ref.shape, F32)
    for b in range(GROUPS):
        pos_ref[b * block : b * block + rows_used] = query_pos[
            b * rows_used : (b + 1) * rows_used
        ].astype(F32)
    pos = pos_ref[...]
    x = x_out[...].astype(F32)
    ai = (x + pos).astype(BF)
    ai_out[...] = ai
    sq_out[...] = ((nn(ai, self_proj[0]) + row(self_bias, 0)) * 0.125).astype(BF)
    sk_out[...] = nn(ai, self_proj[1]).astype(BF)
    sv_out[...] = (nn(x_out[...], self_proj[2]) + row(self_bias, 1)).astype(BF)
    key_row = lax.broadcasted_iota(jnp.int32, (rows, 2 * rows), 0)
    spare = jnp.where(lax.rem(key_row, block) < rows_used, 0.0, FAR).astype(F32)
    for g in range(GROUPS):
        lanes = slice(g * LANES, (g + 1) * LANES)
        s = nt(sk_out[:, lanes], pair(sq_out[...], g)) + spare
        e = jnp.exp(s - jnp.max(s, 0, keepdims=True))
        p = (e * (1.0 / jnp.sum(e, 0, keepdims=True))).astype(BF)
        ps_out[g] = p
        sm_out[:, lanes] = unpair(tn(p, sv_out[:, lanes])).astype(BF)
    xhat, rstd = norm(x + nn(sm_out[...], self_out[...]) + row(self_bias, 2))
    xhat1_out[...] = xhat
    rstd1_out[...] = rstd
    h1 = xhat * row(gains, 0) + row(shifts, 0)
    ci = (h1 + pos).astype(BF)
    ci_out[...] = ci
    cq_out[...] = ((nn(ci, cross_proj[0]) + row(cross_bias, 0)) * 0.125).astype(BF)

    padded = k_ref.shape[0] // GROUPS
    used = rows_used * 12
    slot_row = lax.broadcasted_iota(jnp.int32, (padded, 2 * rows), 0)
    for g in range(GROUPS):
        lanes = slice(g * LANES, (g + 1) * LANES)
        queries = pair(cq_out[...], g)
        top = jnp.full((8, 2 * rows), FAR, F32)
        for j in range(GROUPS):
            here = slice(j * padded, (j + 1) * padded)
            live = jnp.where(ids[mask_at + pb * GROUPS + j] > 0, 0.0, -1000000000.0).astype(F32)
            s = nt(k_ref[here, lanes], queries) + jnp.where(slot_row < used, live, FAR)
            scores[here] = s
            top = jnp.maximum(top, eights(s, jnp.max))
        top = jnp.max(top, 0, keepdims=True)
        total = jnp.zeros((8, 2 * rows), F32)
        for j in range(GROUPS):
            here = slice(j * padded, (j + 1) * padded)
            e = jnp.exp(scores[here] - top)
            scores[here] = e
            total = total + eights(e, jnp.sum)
        inverse = 1.0 / jnp.sum(total, 0, keepdims=True)
        for j in range(GROUPS):
            here = slice(j * padded, (j + 1) * padded)
            pc_out[g, here] = (scores[here] * inverse).astype(BF)
        cm_out[:, lanes] = unpair(tn(pc_out[g], v_ref[:, lanes])).astype(BF)
    xhat, rstd = norm(h1 + nn(cm_out[...], cross_out[...]) + row(cross_bias, 2))
    xhat2_out[...] = xhat
    rstd2_out[...] = rstd
    h2_out[...] = xhat * row(gains, 1) + row(shifts, 1)


def ffn_kernel(
    ids,
    h2_ref,
    cot_ref,
    xhat2_ref,
    rstd2_ref,
    bups,
    up_own,
    down_own,
    misc,
    gains,
    shifts,
    fx0,
    fx1,
    fy0,
    fy1,
    fd0,
    fd1,
    sx0,
    sx1,
    sy0,
    sy1,
    sd0,
    sd1,
    res_out,
    ops_out,
    g2_out,
    small_out,
    bup_out,
    weights,
    pre_ref,
    sems,
):
    core = ids[1]
    width = h2_ref.shape[1]
    units = up_own.shape[0]
    cut = units // 2
    copies = []
    for side, refs in enumerate(((fx0, fx1, fy0, fy1, fd0, fd1), (sx0, sx1, sy0, sy1, sd0, sd1))):
        to = core if side == 0 else 1 - core
        copies.append(
            [
                pltpu.make_async_copy(
                    ref, weights.at[to, n // 2, pl.ds(n % 2 * cut, cut)], sems.at[side, n]
                )
                for n, ref in enumerate(refs)
            ]
        )
    for one in copies:
        for copy in one:
            copy.start()
    h2 = h2_ref[...]
    h2b = h2.astype(BF)
    ops_out[:, :width] = h2b
    down = jnp.zeros(h2.shape, F32)
    for p in range(4):
        if p > 0:
            for one in copies:
                one[2 * p - 2].wait()
                one[2 * p - 1].wait()
        up = up_own[...] if p == 0 else weights[0, p - 1]
        dn = down_own[...] if p == 0 else weights[1, p - 1]
        bias = jnp.concatenate(
            [bups[2 * p : 2 * p + 1], bups[2 * p + 1 : 2 * p + 2, : units - width]], axis=1
        )
        pre = nt(h2b, up) + bias
        pre_ref[p] = pre
        down = down + nn((pre * cdf(pre)).astype(BF), dn)
    xhat, rstd = norm(h2 + down + row(misc, 1))
    res_out[...] = (xhat * row(gains, 2) + row(shifts, 2)).astype(BF)
    g3, dgain3, dshift3 = norm_back(xhat, rstd, row(gains, 2), cot_ref[...].astype(F32))
    gb = g3.astype(BF)
    ops_out[:, width:] = gb
    gh = g3
    for p in range(4):
        up = up_own[...] if p == 0 else weights[0, p - 1]
        dn = down_own[...] if p == 0 else weights[1, p - 1]
        ga = nt(gb, dn).astype(BF).astype(F32)
        pre = pre_ref[p]
        gp = (ga * (cdf(pre) + pre * density(pre))).astype(BF)
        total = column_sum(gp)
        bup_out[p] = jnp.concatenate(
            [total, jnp.zeros((1, 2 * width - units), F32)], axis=1
        )
        gh = gh + nn(gp, up)
    g2, dgain2, dshift2 = norm_back(xhat2_ref[...], rstd2_ref[...], row(gains, 1), gh)
    g2_out[...] = g2
    small_out[0:1] = dgain3
    small_out[1:2] = dshift3
    small_out[2:3] = dgain2
    small_out[3:4] = dshift2
    small_out[4:5] = column_sum(gb)
    small_out[5:6] = column_sum(g2.astype(BF))
    small_out[6:8] = jnp.zeros((2, width), F32)


def backward_kernel(
    ids,
    g2_ref,
    pc_ref,
    k_ref,
    v_ref,
    cq_ref,
    ci_ref,
    cm_ref,
    xhat1_ref,
    rstd1_ref,
    x_ref,
    ai_ref,
    sq_ref,
    sk_ref,
    sv_ref,
    ps_ref,
    sm_ref,
    self_proj,
    self_out,
    cross_proj,
    cross_out,
    gains,
    ds_out,
    gcm_out,
    gx_out,
    gpos_out,
    small_out,
    keep,
    send,
    dp_ref,
    work,
    gq_ref,
    gk_ref,
    gv_ref,
):
    core = ids[1]
    width = x_ref.shape[1]
    rows = x_ref.shape[0]
    g2 = g2_ref[...]
    branch = g2.astype(BF)
    gcm_out[...] = nt(branch, cross_out[...]).astype(BF)
    padded = k_ref.shape[0] // GROUPS
    for g in range(GROUPS):
        lanes = slice(g * LANES, (g + 1) * LANES)
        grads = pair(gcm_out[...], g)
        total = jnp.zeros((8, 2 * rows), F32)
        for j in range(GROUPS):
            here = slice(j * padded, (j + 1) * padded)
            dp = nt(v_ref[here, lanes], grads).astype(BF)
            dp_ref[here] = dp
            total = total + eights(pc_ref[g, here].astype(F32) * dp.astype(F32), jnp.sum)
        total = jnp.sum(total, 0, keepdims=True)
        for j in range(GROUPS):
            here = slice(j * padded, (j + 1) * padded)
            ds_out[g, here] = (
                pc_ref[g, here].astype(F32) * (dp_ref[here].astype(F32) - total)
            ).astype(BF)
        gq_ref[:, lanes] = unpair(tn(ds_out[g], k_ref[:, lanes])).astype(BF) * 0.125
    gcq = gq_ref[...]
    gci = nt(gcq, cross_proj[0])
    small_out[0:1] = column_sum(gcq)
    put_halves(core, tn(ci_ref[...], gcq), 0, keep, send, work)
    put_halves(core, tn(cm_ref[...], branch), 8, keep, send, work)
    g1, dgain1, dshift1 = norm_back(xhat1_ref[...], rstd1_ref[...], row(gains, 0), g2 + gci)
    small_out[1:2] = dgain1
    small_out[2:3] = dshift1
    sbranch = g1.astype(BF)
    small_out[3:4] = column_sum(sbranch)
    put_halves(core, tn(sm_ref[...], sbranch), 4, keep, send, work)
    gsm = nt(sbranch, self_out[...]).astype(BF)
    for g in range(GROUPS):
        lanes = slice(g * LANES, (g + 1) * LANES)
        grads = pair(gsm, g)
        p = ps_ref[g]
        dp = nt(sv_ref[:, lanes], grads).astype(BF).astype(F32)
        pf = p.astype(F32)
        ds = (pf * (dp - jnp.sum(pf * dp, 0, keepdims=True))).astype(BF)
        gq_ref[:, lanes] = unpair(tn(ds, sk_ref[:, lanes])).astype(BF) * 0.125
        gk_ref[:, lanes] = nn(ds, pair(sq_ref[...], g)).astype(BF)
        gv_ref[:, lanes] = nn(p, grads).astype(BF)
    gq, gk, gv = gq_ref[...], gk_ref[...], gv_ref[...]
    gai = nt(gq, self_proj[0]) + nt(gk, self_proj[1])
    gx_out[...] = (g1 + gai + nt(gv, self_proj[2])).astype(BF)
    gpos_out[...] = gai + gci
    small_out[4:5] = column_sum(gq)
    small_out[5:6] = column_sum(gv)
    small_out[6:8] = jnp.zeros((2, width), F32)
    put_halves(core, tn(ai_ref[...], gq), 12, keep, send, work)
    put_halves(core, tn(ai_ref[...], gk), 16, keep, send, work)
    put_halves(core, tn(x_ref[...], gv), 20, keep, send, work)


def ffn_grad_kernel(ids, own, got1, got2, got3, up_own, misc, down_own, keep, send, work):
    core = ids[1]
    units, width = up_own.shape
    ops = jnp.concatenate([ref[...] for ref in (own, got1, got2, got3)], axis=0)
    inputs, branch = ops[:, :width], ops[:, width:]
    bias = jnp.concatenate([row(misc, 2), row(misc, 3)[:, : units - width]], axis=1)
    pre = nt(inputs, up_own[...]) + bias
    phi = cdf(pre)
    act = (pre * phi).astype(BF)
    gact = nt(branch, down_own[...]).astype(BF).astype(F32)
    gpre = (gact * (phi + pre * density(pre))).astype(BF)
    blocks, size = keep.shape[1], keep.shape[2]
    for side, grad in enumerate((tn(inputs, gpre), tn(branch, act))):
        work[...] = grad
        for block in range(blocks):
            mine = pl.multiple_of((2 * block + core) * size, size)
            other = pl.multiple_of((2 * block + 1 - core) * size, size)
            keep[side, block] = work[pl.ds(mine, size), :].astype(BF)
            send[side, block] = work[pl.ds(other, size), :].astype(BF)


def ffn_fold_kernel(ids, keep, got, stay, go, *, bit):
    for side in range(keep.shape[0]):
        for block in range(stay.shape[1]):
            for ref, at in ((stay, 2 * block + ids[bit]), (go, 2 * block + 1 - ids[bit])):
                ref[side, block] = plus(keep[side, at], got[side, at])


def ffn_finish_kernel(ids, keep, got, up_grad, down_grad):
    for side, ref in enumerate((up_grad, down_grad)):
        ref[...] = keep[side, 0].astype(F32) + got[side, 0].astype(F32)


def memory_back_kernel(
    ids,
    ds_ref,
    pc_ref,
    cq_ref,
    gcm_ref,
    featp,
    ki,
    vi,
    cross_proj,
    in_proj,
    res_ref,
    gx_ref,
    gpos_ref,
    small_a,
    small_b,
    bup,
    rows0,
    rows1,
    rows2,
    rows3,
    keep,
    send,
    gk_ref,
    gv_ref,
    gm_ref,
    gf_ref,
    work,
    small,
    *,
    rows_used,
):
    pb, core = ids[0], ids[1]
    width = featp.shape[1]
    rows = res_ref.shape[0]
    block = rows // GROUPS
    padded = featp.shape[0] // GROUPS
    pairs_q = [pair(cq_ref[...], g) for g in range(GROUPS)]
    pairs_g = [pair(gcm_ref[...], g) for g in range(GROUPS)]
    for j in range(GROUPS):
        here = slice(j * padded, (j + 1) * padded)
        for g in range(GROUPS):
            lanes = slice(g * LANES, (g + 1) * LANES)
            gk_ref[here, lanes] = nn(ds_ref[g, here], pairs_q[g]).astype(BF)
            gv_ref[here, lanes] = nn(pc_ref[g, here], pairs_g[g]).astype(BF)
        gm = (nt(gk_ref[here], cross_proj[1]) + nt(gv_ref[here], cross_proj[2])).astype(BF)
        gm_ref[here] = gm
        gf_ref[j] = nt(gm, in_proj[...]).astype(BF)
    for k, ref in enumerate((rows0, rows1, rows2, rows3)):
        at = pl.multiple_of((pb ^ k) * block, block)
        ref[0:padded] = gf_ref[pb ^ k]
        ref[padded : padded + block] = gx_ref[pl.ds(at, block), :]
        ref[padded + block : padded + 2 * block] = res_ref[pl.ds(at, block), :]
    put_halves(core, tn(ki[...], gk_ref[...]), 0, keep, send, work)
    put_halves(core, tn(vi[...], gv_ref[...]), 4, keep, send, work)
    put_halves(core, tn(featp[...], gm_ref[...]), 8, keep, send, work)

    small[...] = gpos_ref[...]
    extras = [
        row(small_b, 1),
        row(small_a, 2),
        row(small_a, 0),
        row(small_b, 2),
        row(small_a, 3),
        row(small_a, 1),
        row(small_b, 4),
        row(small_b, 5),
        row(small_b, 3),
        row(small_b, 0),
        column_sum(gv_ref[...]),
        row(small_a, 5),
        row(small_a, 4),
        column_sum(gm_ref[...]),
    ]
    for index, value in enumerate(extras):
        at = spare_row(index, block, rows_used)
        small[at : at + 1] = value
    for b in range(GROUPS):
        at = b * block + rows_used + 5
        total = bup[b ^ pb]
        small[at : at + 1] = total[:, :width]
        small[at + 1 : at + 2] = total[:, width:]
    for b in range(2):
        for side, ref in ((core, keep), (1 - core, send)):
            low = small[:, b * LANES : (b + 1) * LANES]
            high = small[:, (2 + b) * LANES : (3 + b) * LANES]
            ref[12, b * rows : (b + 1) * rows] = jnp.where(side == 0, low, high).astype(BF)


def spare_row(index, block, rows_used):
    return index // 5 * block + rows_used + index % 5


def put_whole(core, out, index, own, got):
    half = own.shape[1]
    mine = pl.multiple_of(core * half, half)
    other = pl.multiple_of((1 - core) * half, half)
    for b in range(4):
        lanes = slice(b * LANES, (b + 1) * LANES)
        out[pl.ds(mine, half), lanes] = own[index + b].astype(F32)
        out[pl.ds(other, half), lanes] = got[index + b].astype(F32)


def finish_chain_kernel(ids, own1, got1, own2, got2, cross_q, self_out, cross_out, self_proj):
    core = ids[1]
    put_whole(core, cross_q, 0, own1, got1)
    put_whole(core, self_out, 4, own1, got1)
    put_whole(core, cross_out, 8, own1, got1)
    for m in range(3):
        put_whole(core, self_proj.at[m], 4 * m, own2, got2)


def finish_memory_kernel(
    ids, own, got, cross_q, cross_, in_, pos_, self_bias_, cross_bias_, bup_, bdown_, gain_, shift_, inb_, small, *, rows_used
):
    core = ids[1]
    cross_[0] = cross_q[...]
    put_whole(core, cross_.at[1], 0, own, got)
    put_whole(core, cross_.at[2], 4, own, got)
    put_whole(core, in_, 8, own, got)
    rows, width = small.shape
    block = rows // GROUPS
    for b in range(2):
        here = slice(b * rows, (b + 1) * rows)
        first = own[12, here].astype(F32)
        second = got[12, here].astype(F32)
        small[:, b * LANES : (b + 1) * LANES] = jnp.where(core == 0, first, second)
        small[:, (2 + b) * LANES : (3 + b) * LANES] = jnp.where(core == 0, second, first)
    for b in range(GROUPS):
        pos_[b * rows_used : (b + 1) * rows_used] = small[b * block : b * block + rows_used]
        at = b * block + rows_used + 5
        bup_[b : b + 1, :width] = small[at : at + 1]
        bup_[b : b + 1, width:] = small[at + 1 : at + 2]

    def spare(index):
        at = spare_row(index, block, rows_used)
        return small[at : at + 1]

    for ref, index in ((gain_, 0), (shift_, 3), (self_bias_, 6), (cross_bias_, 9)):
        for i in range(3):
            ref[i : i + 1] = spare(index + i)
    bdown_[...] = spare(12)
    inb_[...] = spare(13)


def order_kernel(ids, own, got1, got2, got3, out, grad, feats):
    pb = ids[0]
    part, used = feats.shape[1], out.shape[1]
    block = out.shape[1] // 16 * 16 + 16
    padded = own.shape[0] - 2 * block
    for k, ref in enumerate((own, got1, got2, got3)):
        feats[pb ^ k] = ref[0:part]
        grad[pb ^ k] = ref[padded : padded + used]
        out[pb ^ k] = ref[padded + block : padded + block + used]


class Far:
    def __init__(self, value, parts=None, emit=False):
        self.value, self.parts, self.emit = value, parts, emit


class Raw:
    def __init__(self, value):
        self.value = value


class Late:
    def __init__(self, ref, buffers, sems, parts):
        self.shape = ref.shape
        self.parts = parts
        self.buffers = buffers
        sources = [ref] if parts is None else [ref.at[part] for part in parts]
        self.copies = [
            pltpu.make_async_copy(source, buffer, sems.at[n])
            for n, (source, buffer) in enumerate(zip(sources, buffers))
        ]
        for copy in self.copies:
            copy.start()
        self.waiting = set(range(len(sources)))

    def ready(self, n):
        if n in self.waiting:
            self.waiting.discard(n)
            self.copies[n].wait()

    def __getitem__(self, index):
        if self.parts is None:
            self.ready(0)
            return self.buffers[0][index]
        n = self.parts.index(index)
        self.ready(n)
        return self.buffers[n][...]


def call(kernel, args, outs, scratch=(), limit=16, near=True):
    specs = [pl.BlockSpec(memory_space=pltpu.SMEM)]
    values, extra, emitted, plans = [args[0]], [], [], [None]
    outs = list(outs)
    for arg in args[1:]:
        if isinstance(arg, (Far, Raw)):
            value = arg.value
            specs.append(pl.BlockSpec(memory_space=pl.ANY))
            values.append(pltpu.with_memory_space_constraint(value, pltpu.HBM))
            if isinstance(arg, Raw):
                plans.append(None)
                continue
            count = 1 if arg.parts is None else len(arg.parts)
            if arg.emit:
                plans.append((None, len(emitted), len(extra), count, arg.parts))
                emitted.append((value.shape, value.dtype))
            else:
                plans.append((len(extra), None, len(extra) + count, count, arg.parts))
                shape = value.shape if arg.parts is None else value.shape[1:]
                extra += [pltpu.VMEM(shape, value.dtype)] * count
            extra.append(pltpu.SemaphoreType.DMA((count,)))
        else:
            specs.append(pl.BlockSpec(memory_space=pltpu.VMEM))
            values.append(pltpu.with_memory_space_constraint(arg, pltpu.VMEM))
            plans.append(None)

    def body(*refs):
        given, rest = list(refs[: len(args)]), refs[len(args) :]
        first, rest = rest[: len(outs)], rest[len(outs) :]
        copies, rest = rest[: len(emitted)], rest[len(emitted) :]
        own, late = rest[: len(scratch)], rest[len(scratch) :]
        waits = []
        for index, plan in enumerate(plans):
            if plan is None:
                continue
            at, place, sem, count, parts = plan
            if place is None:
                buffers = late[at : at + count]
            elif parts is None:
                buffers = [copies[place]]
            else:
                buffers = [copies[place].at[part] for part in parts]
            given[index] = Late(given[index], buffers, late[sem], parts)
            waits.append(given[index])
        kernel(*given, *first, *own)
        for one in waits:
            for n in sorted(one.waiting):
                one.ready(n)

    whole = [(o, near) for o in outs] + [(o, True) for o in emitted]
    return pl.pallas_call(
        body,
        out_shape=[pltpu.VMEM(*o) if here else jax.ShapeDtypeStruct(*o) for o, here in whole],
        in_specs=specs,
        out_specs=[pl.BlockSpec(memory_space=pltpu.VMEM)] * len(whole),
        scratch_shapes=list(scratch) + extra,
        compiler_params=pltpu.CompilerParams(vmem_limit_bytes=limit * 1024 * 1024),
        cost_estimate=pl.CostEstimate(flops=1, bytes_accessed=1, transcendentals=0),
    )(*values)


def swap(value, axis, bit):
    size = lax.axis_size(axis)
    return lax.ppermute(value, axis, [(i, i ^ bit) for i in range(size)])


def bit_of(axis, bit):
    return (lax.axis_index(axis) // bit) % 2


def plus(left, right):
    return (left.astype(F32) + right.astype(F32)).astype(BF)


def halve(keep, got, bit):
    half = keep.shape[1] // 2
    total = plus(keep, got)
    mine = lax.dynamic_slice_in_dim(total, bit * half, half, 1)
    other = lax.dynamic_slice_in_dim(total, (1 - bit) * half, half, 1)
    return mine, other


def fold(ids, groups):
    rows = groups[0][0][0][0].shape[1] // 2
    if rows % 16:
        result = []
        for pieces, bit in groups:
            done = [halve(keep[a:b], got[a:b], ids[bit]) for keep, got, a, b in pieces]
            result += [jnp.concatenate(side) for side in zip(*done)]
        return result
    args, outs = [], []
    for pieces, bit in groups:
        count = sum(b - a for _, _, a, b in pieces)
        outs += [((count, rows, LANES), BF)] * 2
        for keep, got, _, _ in pieces:
            args += [keep, got]

    def kernel(ids, *refs):
        given, made = list(refs[: len(args)]), list(refs[len(args) :])
        for pieces, bit in groups:
            stay, go = made.pop(0), made.pop(0)
            mine = pl.multiple_of(ids[bit] * rows, rows)
            other = pl.multiple_of((1 - ids[bit]) * rows, rows)
            at = 0
            for _, _, a, b in pieces:
                keep, got = given.pop(0), given.pop(0)
                for block in range(a, b):
                    for ref, start in ((stay, mine), (go, other)):
                        here = pl.ds(start, rows)
                        ref[at] = plus(keep[block, here], got[block, here])
                    at += 1

    return call(kernel, [ids, *args], outs, limit=4)


def add_up(ids, keep, got):
    if keep.shape[1] % 16:
        return plus(keep, got)

    def kernel(ids, keep, got, out):
        out[...] = plus(keep[...], got[...])

    return call(kernel, [ids, keep, got], [(keep.shape, BF)], limit=4)[0]


def join(ids, value, got, bit, cuts=None):
    blocks, rows, lanes = value.shape
    cuts = cuts or [(0, blocks)]
    if rows % 16:
        full = jnp.where(
            ids[bit] == 0, jnp.concatenate([value, got], 1), jnp.concatenate([got, value], 1)
        )
        return [full[a:b] for a, b in cuts]

    def kernel(ids, value, got, *outs):
        mine = pl.multiple_of(ids[bit] * rows, rows)
        other = pl.multiple_of((1 - ids[bit]) * rows, rows)
        for out, (a, b) in zip(outs, cuts):
            for block in range(a, b):
                out[block - a, pl.ds(mine, rows)] = value[block]
                out[block - a, pl.ds(other, rows)] = got[block]

    outs = [((b - a, 2 * rows, lanes), BF) for a, b in cuts]
    return call(kernel, [ids, value, got], outs, limit=4)


def on_device(
    tokens,
    query_pos,
    features,
    camera_mask,
    out_grad,
    self_proj,
    self_out,
    self_bias,
    cross_proj,
    cross_out,
    cross_bias,
    w_up,
    b_up,
    w_down,
    b_down,
    norm_gain,
    norm_bias,
    in_proj,
    in_bias,
):
    pb = lax.axis_index("pb")
    pb_size = lax.axis_size("pb")
    dp_size = lax.axis_size("dp")
    ways = [("dp", 1 << i) for i in range(1, dp_size.bit_length() - 1)]
    core_way, x_way, y_way = ("dp", 1), ("pb", 1), ("pb", 2)
    bits = [core_way, x_way, y_way] + ways
    ids = jnp.concatenate(
        [jnp.stack([pb] + [bit_of(*way) for way in bits]).astype(jnp.int32), camera_mask.reshape(-1)]
    )
    at_of = {way: 1 + n for n, way in enumerate(bits)}
    mask_at = 1 + len(bits)
    width = tokens.shape[2]
    used = tokens.shape[1]
    block = -(-used // 16) * 16
    rows = block * pb_size
    mem = features.shape[1]
    part = mem // pb_size
    padded = -(-part // 16) * 16
    slots = padded * pb_size
    units = b_up.shape[0]

    misc = jnp.concatenate([in_bias, b_down, b_up, jnp.zeros((2 * width - units,), BF)])
    misc = misc.reshape(4, width)
    up, down = w_up.T, w_down.T
    cut = units // 2
    turn = lambda value: value.transpose(1, 0, 2).reshape(-1, width)
    *send, mine0, mine1 = call(
        functools.partial(start_kernel, rows_used=used),
        [ids, Raw(up), Raw(down), turn(tokens), turn(out_grad), misc],
        [((block, 2 * width), BF)] * 4 + [((cut, width), BF)] * 2,
        scratch=[pltpu.VMEM((rows, 2 * width), F32), pltpu.SemaphoreType.DMA((2,))],
    )
    fx1 = swap(mine1, *x_way)
    fy0 = swap(mine0, *y_way)
    got = [send[0]] + [swap(send[k], "pb", k) for k in range(1, pb_size)]

    column = np.arange(width)
    rate = 1.0 / 10000.0 ** ((column // 2 * 2) / width)
    angle = np.arange(padded)[:, None] * rate
    start = np.arange(pb_size)[:, None] * part * rate
    even = column % 2 == 0
    waves = np.concatenate(
        [
            np.where(even, np.sin(start), np.cos(start)),
            np.where(even, np.cos(start), -np.sin(start)),
        ]
    )
    sines, cosines, waves = [
        jnp.asarray(value.astype(np.float32)) for value in (np.sin(angle), np.cos(angle), waves)
    ]

    wide = (slots, width)
    featp, ki, vi, ck, cv, in_proj, cross_proj = call(
        memory_kernel,
        [
            ids,
            Raw(features),
            Far(sines),
            Far(cosines),
            Far(waves),
            Far(in_proj, emit=True),
            misc,
            Far(cross_proj, (1, 2, 0), emit=True),
            Far(cross_bias),
        ],
        [(wide, BF)] * 5,
        scratch=[pltpu.VMEM((mem, width), BF), pltpu.SemaphoreType.DMA],
    )
    ck, fx1, fy0, mine0, mine1, *got = lax.optimization_barrier(
        (ck, fx1, fy0, mine0, mine1, *got)
    )
    fd0 = swap(fy0, *x_way)
    fd1 = swap(fx1, *y_way)
    fx0 = swap(mine0, *x_way)
    fy1 = swap(mine1, *y_way)
    flat = (rows, width)
    scores = (GROUPS, slots, 2 * rows)
    (x, cot, ai, sq, sk, sv, ps, sm, xhat1, rstd1, ci, cq, pc, cm, h2, xhat2, rstd2, bups, self_proj, self_out, cross_out, norm_gain, norm_bias, up, down) = call(
        functools.partial(forward_kernel, rows_used=used, mask_at=mask_at),
        [
            ids,
            *got,
            Far(query_pos),
            Far(self_proj, (0, 1, 2), emit=True),
            Far(self_out, emit=True),
            Far(self_bias),
            cross_proj,
            Far(cross_out, emit=True),
            Far(cross_bias),
            Far(norm_gain, emit=True),
            Far(norm_bias, emit=True),
            ck,
            cv,
            Far(up, emit=True),
            Far(down, emit=True),
        ],
        [
            (flat, BF),
            (flat, BF),
            (flat, BF),
            (flat, BF),
            (flat, BF),
            (flat, BF),
            ((GROUPS, rows, 2 * rows), BF),
            (flat, BF),
            (flat, F32),
            ((rows, 1), F32),
            (flat, BF),
            (flat, BF),
            (scores, BF),
            (flat, BF),
            (flat, F32),
            (flat, F32),
            ((rows, 1), F32),
            ((2 * pb_size, width), F32),
        ],
        scratch=[pltpu.VMEM((slots, 2 * rows), F32), pltpu.VMEM(flat, F32)],
    )
    fetched = [fx0, fx1, fy0, fy1, fd0, fd1]
    h2, *fetched = lax.optimization_barrier((h2, *fetched))
    swapped = [swap(value, *core_way) for value in fetched]
    res, ops, g2, small_a, bup = call(
        ffn_kernel,
        [
            ids,
            h2,
            cot,
            xhat2,
            rstd2,
            bups,
            up,
            down,
            misc,
            norm_gain,
            norm_bias,
            *[Raw(value) for value in fetched],
            *[Raw(value) for value in swapped],
        ],
        [
            (flat, BF),
            ((rows, 2 * width), BF),
            (flat, F32),
            ((8, width), F32),
            ((pb_size, 1, 2 * width), F32),
        ],
        scratch=[
            pltpu.VMEM((2, 3, units, width), BF),
            pltpu.VMEM((4, rows, units), F32),
            pltpu.SemaphoreType.DMA((2, 6)),
        ],
    )
    others = [swap(ops, "pb", k) for k in range(1, pb_size)]
    halves = ((24, width // 2, LANES), BF)
    ds, gcm, gx, gpos, small_b, keep12, send12 = call(
        backward_kernel,
        [
            ids,
            g2,
            pc,
            ck,
            cv,
            cq,
            ci,
            cm,
            xhat1,
            rstd1,
            x,
            ai,
            sq,
            sk,
            sv,
            ps,
            sm,
            self_proj,
            self_out,
            cross_proj,
            cross_out,
            norm_gain,
        ],
        [
            (scores, BF),
            (flat, BF),
            (flat, BF),
            (flat, F32),
            ((8, width), F32),
            halves,
            halves,
        ],
        scratch=[
            pltpu.VMEM((slots, 2 * rows), BF),
            pltpu.VMEM((width, width), F32),
            pltpu.VMEM(flat, BF),
            pltpu.VMEM(flat, BF),
            pltpu.VMEM(flat, BF),
        ],
    )
    ops, *others, send12 = lax.optimization_barrier((ops, *others, send12))
    halves3 = ((13, width // 2, LANES), BF)
    *rows_out, keep3, send3 = call(
        functools.partial(memory_back_kernel, rows_used=used),
        [
            ids,
            ds,
            pc,
            cq,
            gcm,
            featp,
            ki,
            vi,
            cross_proj,
            in_proj,
            res,
            gx,
            gpos,
            small_a,
            small_b,
            bup,
        ],
        [((padded + 2 * block, width), BF)] * 4 + [halves3, halves3],
        scratch=[
            pltpu.VMEM(wide, BF),
            pltpu.VMEM(wide, BF),
            pltpu.VMEM(wide, BF),
            pltpu.VMEM((pb_size, padded, width), BF),
            pltpu.VMEM((width, width), F32),
            pltpu.VMEM(flat, F32),
        ],
    )

    got12 = swap(send12, *core_way)
    ka, sa, kb, sb = fold(
        ids, [([(keep12, got12, 0, 12)], at_of[x_way]), ([(keep12, got12, 12, 24)], at_of[y_way])]
    )
    ra, rb = swap(sa, *x_way), swap(sb, *y_way)
    ra, rb, keep3, send3 = lax.optimization_barrier((ra, rb, keep3, send3))
    got3 = swap(send3, *core_way)
    ka, sa, kb, sb = fold(
        ids, [([(ka, ra, 0, 12)], at_of[y_way]), ([(kb, rb, 0, 12)], at_of[x_way])]
    )
    ra, rb = swap(sa, *y_way), swap(sb, *x_way)
    order3 = [ways[0], x_way, y_way] + ways[1:]
    kc, sc = fold(ids, [([(keep3, got3, 0, 13)], at_of[order3[0]])])
    rc = swap(sc, *order3[0])
    piece = width // dp_size
    fkeep, fsend = call(
        ffn_grad_kernel,
        [ids, ops, *others, up, misc, down],
        [((2, dp_size // 2, piece, units), BF)] * 2,
        scratch=[pltpu.VMEM((width, units), F32)],
    )
    ra, rb, rc, fsend, *rows_out = lax.optimization_barrier((ra, rb, rc, fsend, *rows_out))
    fgot = swap(fsend, *core_way)
    arrived = [rows_out[0]] + [swap(rows_out[k], "pb", k) for k in range(1, pb_size)]
    kab, sab = fold(ids, [([(ka, ra, 0, 12), (kb, rb, 0, 12)], at_of[ways[0]])])
    rab = swap(sab, *ways[0])
    left = list(ways[1:])
    left3 = order3[1:]
    back, back3 = [], []
    vab = vc = None
    after = list(reversed(ways))
    after3 = list(reversed(order3))
    ab_done = False
    pair_out = None
    c_out = None
    while c_out is None:
        if left:
            way = left.pop(0)
            kab, sab = fold(ids, [([(kab, rab, 0, 24)], at_of[way])])
            rab = swap(sab, *way)
        elif vab is None:
            vab = add_up(ids, kab, rab)
            way = after.pop(0)
            rab = swap(vab, *way)
            last = way
        elif after:
            (vab,) = join(ids, vab, rab, at_of[last])
            last = after.pop(0)
            rab = swap(vab, *last)
        elif pair_out is None:
            va, vb = join(ids, vab, rab, at_of[last], [(0, 12), (12, 24)])
            ra, rb = swap(va, *y_way), swap(vb, *x_way)
            pair_out = 1
        elif pair_out == 1:
            (va,) = join(ids, va, ra, at_of[y_way])
            (vb,) = join(ids, vb, rb, at_of[x_way])
            ra, rb = swap(va, *x_way), swap(vb, *y_way)
            pair_out = 2
        elif pair_out == 2:
            (va,) = join(ids, va, ra, at_of[x_way])
            (vb,) = join(ids, vb, rb, at_of[y_way])
            ra, rb = swap(va, *core_way), swap(vb, *core_way)
            pair_out = 3
        if left3:
            way = left3.pop(0)
            kc, sc = fold(ids, [([(kc, rc, 0, 13)], at_of[way])])
            rc = swap(sc, *way)
        elif vc is None:
            vc = add_up(ids, kc, rc)
            last3 = after3.pop(0)
            rc = swap(vc, *last3)
        elif after3:
            (vc,) = join(ids, vc, rc, at_of[last3])
            last3 = after3.pop(0)
            rc = swap(vc, *last3)
        else:
            (c_out,) = join(ids, vc, rc, at_of[last3])
        if ways and fkeep.shape[1] > 1:
            way = ways[(dp_size // 2).bit_length() - fkeep.shape[1].bit_length()]
            fkeep, fsend = call(
                functools.partial(ffn_fold_kernel, bit=at_of[way]),
                [ids, fkeep, fgot],
                [((2, fkeep.shape[1] // 2, piece, units), BF)] * 2,
                limit=4,
            )
            fgot = swap(fsend, *way)
        if c_out is None:
            names = [rab, rc, fgot] if pair_out is None else [ra, rb, rc, fgot]
            if pair_out == 1:
                names += arrived[1:]
            names = lax.optimization_barrier(tuple(names))
            if pair_out is None:
                rab, rc, fgot = names
            else:
                ra, rb, rc, fgot = names[:4]
            if pair_out == 1:
                arrived[1:] = names[4:]
                layer_out, grad_tokens, grad_features = call(
                    order_kernel,
                    [ids, *arrived],
                    [(tokens.shape, BF), (tokens.shape, BF), ((pb_size, part, width), BF)],
                    near=False,
                )
    ffn_up, ffn_down = call(
        ffn_finish_kernel, [ids, fkeep, fgot], [((piece, units), F32)] * 2, near=False
    )
    c = c_out
    matrix = ((width, width), F32)
    three = ((3, width, width), F32)
    g_cross_q, g_self_out, g_cross_out, g_self_proj = call(
        finish_chain_kernel, [ids, va, ra, vb, rb], [matrix, matrix, matrix, three], near=False
    )
    c_other = swap(c, "dp", 1)
    bias3 = ((3, width), F32)
    bias1 = ((1, width), F32)
    (
        g_cross_proj,
        g_in_proj,
        g_pos,
        g_self_bias,
        g_cross_bias,
        g_bup,
        g_bdown,
        g_gain,
        g_shift,
        g_inb,
    ) = call(
        functools.partial(finish_memory_kernel, rows_used=used),
        [ids, c, c_other, g_cross_q],
        [
            three,
            matrix,
            (query_pos.shape, F32),
            bias3,
            bias3,
            ((pb_size, 2 * width), F32),
            bias1,
            bias3,
            bias3,
            bias1,
        ],
        scratch=[pltpu.VMEM(flat, F32)],
        near=False,
    )

    return (
        layer_out,
        grad_tokens,
        grad_features,
        g_pos,
        g_self_proj,
        g_self_out,
        g_self_bias,
        g_cross_proj,
        g_cross_out,
        g_cross_bias,
        ffn_up,
        g_bup[:, :units].reshape(-1),
        ffn_down,
        g_bdown[0],
        g_gain,
        g_shift,
        g_in_proj,
        g_inb[0],
    )


def solution(mesh):
    return jax.shard_map(
        on_device,
        mesh=mesh,
        in_specs=(
            P("dp", "pb", None),
            P(),
            P("dp", None, None),
            P("dp", None),
            P("dp", "pb", None),
            P(),
            P(),
            P(),
            P(),
            P(),
            P(),
            P(None, "pb"),
            P("pb"),
            P(None, "pb"),
            P(),
            P(),
            P(),
            P(),
            P(),
        ),
        out_specs=(
            P("dp", "pb", None),
            P("dp", "pb", None),
            P("dp", "pb", None),
            P(),
            P(),
            P(),
            P(),
            P(),
            P(),
            P(),
            P("dp", "pb"),
            P(),
            P("dp", "pb"),
            P(),
            P(),
            P(),
            P(),
            P(),
        ),
        check_vma=False,
    )
```

```python
import functools

import jax
import jax.numpy as jnp
import numpy as np
from jax import lax
from jax.experimental import pallas as pl
from jax.experimental.pallas import tpu as pltpu
from jax.sharding import PartitionSpec as P

BF = jnp.bfloat16
F32 = jnp.float32
HEADS = 8
LANES = 128
GROUPS = 4
FAR = -1e30
RATE = 1.15e9
COST_P = 0.0
COST_Q = 1.0
COST_K = 2.6


def dims(left, right, a, b):
    return lax.dot_general(left, right, (((a,), (b,)), ((), ())), preferred_element_type=F32)


def nn(left, right):
    return dims(left, right, 1, 0)


def nt(left, right):
    return dims(left, right, 1, 1)


def tn(left, right):
    return dims(left, right, 0, 0)


def lane_masks(dtype=BF):
    lane = lax.broadcasted_iota(jnp.int32, (1, LANES), 1)
    low = (lane < LANES // 2).astype(F32)
    return low.astype(dtype), (1.0 - low).astype(dtype)


def pair(value, group):
    part = value[:, group * LANES : (group + 1) * LANES]
    low, high = lane_masks()
    return jnp.concatenate([part * low, part * high], axis=0)


def unpair(value):
    rows = value.shape[0] // 2
    lane = lax.broadcasted_iota(jnp.int32, (rows, LANES), 1)
    return jnp.where(lane < LANES // 2, value[:rows], value[rows:])


def eights(value, op):
    return op(value.reshape(value.shape[0] // 8, 8, value.shape[1]), axis=0)


def norm(value):
    center = value - jnp.mean(value, -1, keepdims=True)
    rstd = lax.rsqrt(jnp.mean(center * center, -1, keepdims=True) + 1e-05)
    return center * rstd, rstd


def norm_back(xhat, rstd, gain, grad):
    scaled = grad * gain
    inner = jnp.mean(scaled, -1, keepdims=True) + xhat * jnp.mean(
        scaled * xhat, -1, keepdims=True
    )
    return (
        rstd * (scaled - inner),
        jnp.sum(grad * xhat, 0, keepdims=True),
        jnp.sum(grad, 0, keepdims=True),
    )


def column_sum(value):
    return jnp.sum(value.astype(F32), 0, keepdims=True)


def row(ref, index):
    return ref[index : index + 1, :].astype(F32)


def cdf(value):
    return 0.5 * (1.0 + lax.erf(value * np.float32(0.7071067811865476)))


def density(value):
    return jnp.exp(-0.5 * value * value) * np.float32(0.3989422804014327)


class Chain:
    def __init__(self, refs):
        self.refs = refs

    def __setitem__(self, index, value):
        size = self.refs[0].shape[0]
        self.refs[index // size][index % size] = value


def put_halves(core, value, index, keep_ref, send_ref, scratch):
    half = value.shape[0] // 2
    scratch[...] = value
    mine = pl.multiple_of(core * half, half)
    other = pl.multiple_of((1 - core) * half, half)
    for block in range(value.shape[1] // LANES):
        lanes = slice(block * LANES, (block + 1) * LANES)
        keep_ref[index + block] = scratch[pl.ds(mine, half), lanes].astype(BF)
        send_ref[index + block] = scratch[pl.ds(other, half), lanes].astype(BF)


def pick_kernel(ids, up, down, *refs):
    outs, sems = refs[:4], refs[4]
    core = ids[1]
    units = up.shape[0]
    starts = (0, units - outs[1].shape[0], units - outs[2].shape[0], 0)
    for side, ref in enumerate((up, down)):

        @pl.when(core == side)
        def _():
            copies = []
            for n, (out, start) in enumerate(zip(outs, starts)):
                half = out.shape[0] // 2
                for m in range(2):
                    copies.append(
                        pltpu.make_async_copy(
                            ref.at[pl.ds(start + m * half, half)],
                            out.at[pl.ds(m * half, half)],
                            sems.at[2 * n + m],
                        )
                    )
            for copy in copies:
                copy.start()
            for copy in copies:
                copy.wait()


def start_kernel(
    ids, tokens, cots, misc, send0, send1, send2, send3, flat, turned, *, rows_used
):
    pb = ids[0]
    rows, width2 = turned.shape
    width = width2 // 2
    block = rows // GROUPS
    count = rows_used * GROUPS
    for q in range(rows_used):
        flat[q * GROUPS : (q + 1) * GROUPS, :width] = tokens[q].astype(F32)
        flat[q * GROUPS : (q + 1) * GROUPS, width:] = cots[q].astype(F32)
    place = lax.broadcasted_iota(jnp.int32, (rows, count), 0)
    query = lax.broadcasted_iota(jnp.int32, (rows, count), 1)
    hit = query == lax.rem(place, block) * GROUPS + lax.div(place, block)
    used = lax.rem(place, block) < rows_used
    chosen = jnp.where(jnp.logical_and(hit, used), 1.0, 0.0).astype(BF)
    turned[...] = nn(chosen, flat[...].astype(BF))
    for b in range(GROUPS):
        at = b * block + rows_used
        turned[at : at + 2, :width] = misc[2:4, :].astype(F32)
    for k, ref in enumerate((send0, send1, send2, send3)):
        at = pl.multiple_of((pb ^ k) * block, block)
        ref[...] = turned[pl.ds(at, block), :].astype(BF)


def memory_kernel(
    ids, feats, sines, cosines, waves, in_proj, misc, cross_proj, cross_bias, featp, ki, vi, k, v, buf, sems
):
    blocks = GROUPS
    slots = buf.shape[0]
    part = slots // blocks
    padded = featp.shape[0] // blocks
    copy = pltpu.make_async_copy(feats.at[ids[0]], buf, sems)
    copy.start()
    for j in range(blocks):
        featp[(j + 1) * padded - 16 : (j + 1) * padded] = jnp.zeros((16, featp.shape[1]), BF)
    copy.wait()
    bias = row(misc, 0)
    for j in range(blocks):
        here = slice(j * padded, (j + 1) * padded)
        featp[j * padded : j * padded + part] = buf[j * part : (j + 1) * part]
        memory = nn(featp[here], in_proj[...]) + bias
        places = cosines[...] * row(waves, j) + sines[...] * row(waves, blocks + j)
        key_input = (memory + places).astype(BF)
        value_input = memory.astype(BF)
        ki[here] = key_input
        vi[here] = value_input
        k[here] = nn(key_input, cross_proj[1]).astype(BF)
        v[here] = (nn(value_input, cross_proj[2]) + row(cross_bias, 1)).astype(BF)


def forward_kernel(
    ids,
    mask,
    own,
    got1,
    got2,
    got3,
    query_pos,
    self_proj,
    self_out,
    self_bias,
    cross_proj,
    cross_out,
    cross_bias,
    gains,
    shifts,
    k_ref,
    v_ref,
    up_,
    down_,
    x_out,
    cot_out,
    ai_out,
    sq_out,
    sk_out,
    sv_out,
    ps_out,
    sm_out,
    xhat1_out,
    rstd1_out,
    ci_out,
    cq_out,
    pc_out,
    cm_out,
    h2_out,
    xhat2_out,
    rstd2_out,
    bups_out,
    h2b_out,
    scores,
    pos_ref,
    *,
    rows_used,
):
    pb = ids[0]
    width = pos_ref.shape[1]
    block = own.shape[0]
    for k, ref in enumerate((own, got1, got2, got3)):
        at = pl.multiple_of((pb ^ k) * block, block)
        x_out[pl.ds(at, block), :] = ref[:, :width]
        cot_out[pl.ds(at, block), :] = ref[:, width:]
        bups_out[2 * k : 2 * k + 2] = ref[rows_used : rows_used + 2, :width].astype(F32)
    rows = x_out.shape[0]
    pos_ref[...] = jnp.zeros(pos_ref.shape, F32)
    for b in range(GROUPS):
        pos_ref[b * block : b * block + rows_used] = query_pos[
            b * rows_used : (b + 1) * rows_used
        ].astype(F32)
    pos = pos_ref[...]
    x = x_out[...].astype(F32)
    ai = (x + pos).astype(BF)
    ai_out[...] = ai
    sq_out[...] = ((nn(ai, self_proj[0]) + row(self_bias, 0)) * 0.125).astype(BF)
    sk_out[...] = nn(ai, self_proj[1]).astype(BF)
    sv_out[...] = (nn(x_out[...], self_proj[2]) + row(self_bias, 1)).astype(BF)
    key_row = lax.broadcasted_iota(jnp.int32, (rows, 2 * rows), 0)
    spare = jnp.where(lax.rem(key_row, block) < rows_used, 0.0, FAR).astype(F32)
    for g in range(GROUPS):
        lanes = slice(g * LANES, (g + 1) * LANES)
        s = nt(sk_out[:, lanes], pair(sq_out[...], g)) + spare
        e = jnp.exp(s - jnp.max(s, 0, keepdims=True))
        p = (e * (1.0 / jnp.sum(e, 0, keepdims=True))).astype(BF)
        ps_out[g] = p
        sm_out[:, lanes] = unpair(tn(p, sv_out[:, lanes])).astype(BF)
    xhat, rstd = norm(x + nn(sm_out[...], self_out[...]) + row(self_bias, 2))
    xhat1_out[...] = xhat
    rstd1_out[...] = rstd
    h1 = xhat * row(gains, 0) + row(shifts, 0)
    ci = (h1 + pos).astype(BF)
    ci_out[...] = ci
    cq_out[...] = ((nn(ci, cross_proj[0]) + row(cross_bias, 0)) * 0.125).astype(BF)

    padded = k_ref.shape[0] // GROUPS
    used = rows_used * 12
    slot_row = lax.broadcasted_iota(jnp.int32, (padded, 2 * rows), 0)
    for g in range(GROUPS):
        lanes = slice(g * LANES, (g + 1) * LANES)
        queries = pair(cq_out[...], g)
        top = jnp.full((8, 2 * rows), FAR, F32)
        for j in range(GROUPS):
            here = slice(j * padded, (j + 1) * padded)
            live = jnp.where(mask[pb, j] > 0, 0.0, -1000000000.0).astype(F32)
            s = nt(k_ref[here, lanes], queries) + jnp.where(slot_row < used, live, FAR)
            scores[here] = s
            top = jnp.maximum(top, eights(s, jnp.max))
        top = jnp.max(top, 0, keepdims=True)
        total = jnp.zeros((8, 2 * rows), F32)
        for j in range(GROUPS):
            here = slice(j * padded, (j + 1) * padded)
            e = jnp.exp(scores[here] - top)
            scores[here] = e
            total = total + eights(e, jnp.sum)
        inverse = 1.0 / jnp.sum(total, 0, keepdims=True)
        for j in range(GROUPS):
            here = slice(j * padded, (j + 1) * padded)
            pc_out[g, here] = (scores[here] * inverse).astype(BF)
        cm_out[:, lanes] = unpair(tn(pc_out[g], v_ref[:, lanes])).astype(BF)
    xhat, rstd = norm(h1 + nn(cm_out[...], cross_out[...]) + row(cross_bias, 2))
    xhat2_out[...] = xhat
    rstd2_out[...] = rstd
    h2 = xhat * row(gains, 1) + row(shifts, 1)
    h2_out[...] = h2
    h2b_out[...] = h2.astype(BF)


def ffn_first_kernel(
    ids, h2_ref, bups, up_own, down_own, fd0, fd1, sd0, sd1, down_out, pre_ref, weights, sems
):
    copies = gather_weights(ids[1], weights, sems, ((fd0, fd1), (sd0, sd1)))
    h2 = h2_ref[...]
    down = jnp.zeros(h2.shape, F32)
    for p in range(2):
        if p:
            for copy in copies:
                for one in copy:
                    one.wait()
        up = weights[0, 0] if p else up_own[...]
        dn = weights[1, 0] if p else down_own[...]
        pre = nt(h2, up) + bias_of(bups, 3 * p, up.shape[0])
        pre_ref[p] = pre
        down = down + nn((pre * cdf(pre)).astype(BF), dn)
    down_out[...] = down


def gather_weights(core, weights, sems, sides):
    units = weights.shape[2]
    copies = []
    for n in range(len(sides[0])):
        take = units // 2
        source, start = (0, 0) if n % 2 == 0 else (sides[0][n].shape[0] - take, take)
        copies.append(
            [
                pltpu.make_async_copy(
                    refs[n].at[pl.ds(source, take)],
                    weights.at[core if side == 0 else 1 - core, n // 2, pl.ds(start, take)],
                    sems.at[side, n],
                )
                for side, refs in enumerate(sides)
            ]
        )
        for one in copies[-1]:
            one.start()
    return copies


def bias_of(bups, p, units):
    width = bups.shape[1]
    return jnp.concatenate(
        [bups[2 * p : 2 * p + 1], bups[2 * p + 1 : 2 * p + 2, : units - width]], axis=1
    )


def ffn_second_kernel(
    ids,
    h2_ref,
    h2b_ref,
    cot_ref,
    xhat2_ref,
    rstd2_ref,
    bups,
    up_own,
    down_own,
    down_ref,
    pre_ref,
    far,
    misc,
    gains,
    shifts,
    fx0,
    fx1,
    fy0,
    fy1,
    sx0,
    sx1,
    sy0,
    sy1,
    res_out,
    ops_out,
    g2_out,
    small_out,
    bup_out,
    near,
    sems,
):
    copies = gather_weights(ids[1], near, sems, ((fx0, fx1, fy0, fy1), (sx0, sx1, sy0, sy1)))
    h2 = h2_ref[...]
    width = h2.shape[1]
    units = up_own.shape[0]
    h2b = h2b_ref[...]
    down = down_ref[...]
    pres = [pre_ref[0]]
    for p in range(2):
        for copy in copies[2 * p : 2 * p + 2]:
            for one in copy:
                one.wait()
        pre = nt(h2b, near[0, p]) + bias_of(bups, p + 1, units)
        pres.append(pre)
        down = down + nn((pre * cdf(pre)).astype(BF), near[1, p])
    pres.append(pre_ref[1])
    xhat, rstd = norm(h2 + down + row(misc, 1))
    res_out[...] = (xhat * row(gains, 2) + row(shifts, 2)).astype(BF)
    g3, dgain3, dshift3 = norm_back(xhat, rstd, row(gains, 2), cot_ref[...].astype(F32))
    gb = g3.astype(BF)
    ops_out[:, :width] = h2b
    ops_out[:, width:] = gb
    gh = g3
    for p, (up, dn) in enumerate(
        (
            (up_own[...], down_own[...]),
            (near[0, 0], near[1, 0]),
            (near[0, 1], near[1, 1]),
            (far[0, 0], far[1, 0]),
        )
    ):
        pre = pres[p]
        ga = nt(gb, dn).astype(BF).astype(F32)
        gp = (ga * (cdf(pre) + pre * density(pre))).astype(BF)
        bup_out[p] = jnp.concatenate(
            [column_sum(gp), jnp.zeros((1, 2 * width - units), F32)], axis=1
        )
        gh = gh + nn(gp, up)
    g2, dgain2, dshift2 = norm_back(xhat2_ref[...], rstd2_ref[...], row(gains, 1), gh)
    g2_out[...] = g2
    small_out[0:1] = dgain3
    small_out[1:2] = dshift3
    small_out[2:3] = dgain2
    small_out[3:4] = dshift2
    small_out[4:5] = column_sum(gb)
    small_out[5:6] = column_sum(g2.astype(BF))
    small_out[6:8] = jnp.zeros((2, width), F32)


def backward_kernel(
    ids,
    g2_ref,
    pc_ref,
    k_ref,
    v_ref,
    cq_ref,
    ci_ref,
    cm_ref,
    xhat1_ref,
    rstd1_ref,
    x_ref,
    ai_ref,
    sq_ref,
    sk_ref,
    sv_ref,
    ps_ref,
    sm_ref,
    self_proj,
    self_out,
    cross_proj,
    cross_out,
    gains,
    ds_out,
    gcm_out,
    gx_out,
    gpos_out,
    small_out,
    keep,
    send0,
    send1,
    send2,
    send3,
    dp_ref,
    work,
    gq_ref,
    gk_ref,
    gv_ref,
):
    core = ids[1]
    send = Chain((send0, send1, send2, send3))
    width = x_ref.shape[1]
    rows = x_ref.shape[0]
    g2 = g2_ref[...]
    branch = g2.astype(BF)
    gcm_out[...] = nt(branch, cross_out[...]).astype(BF)
    padded = k_ref.shape[0] // GROUPS
    for g in range(GROUPS):
        lanes = slice(g * LANES, (g + 1) * LANES)
        grads = pair(gcm_out[...], g)
        total = jnp.zeros((8, 2 * rows), F32)
        for j in range(GROUPS):
            here = slice(j * padded, (j + 1) * padded)
            dp = nt(v_ref[here, lanes], grads).astype(BF)
            dp_ref[here] = dp
            total = total + eights(pc_ref[g, here].astype(F32) * dp.astype(F32), jnp.sum)
        total = jnp.sum(total, 0, keepdims=True)
        for j in range(GROUPS):
            here = slice(j * padded, (j + 1) * padded)
            ds_out[g, here] = (
                pc_ref[g, here].astype(F32) * (dp_ref[here].astype(F32) - total)
            ).astype(BF)
        gq_ref[:, lanes] = unpair(tn(ds_out[g], k_ref[:, lanes])).astype(BF) * 0.125
    gcq = gq_ref[...]
    gci = nt(gcq, cross_proj[0])
    small_out[0:1] = column_sum(gcq)
    put_halves(core, tn(ci_ref[...], gcq), 0, keep, send, work)
    put_halves(core, tn(cm_ref[...], branch), 8, keep, send, work)
    g1, dgain1, dshift1 = norm_back(xhat1_ref[...], rstd1_ref[...], row(gains, 0), g2 + gci)
    small_out[1:2] = dgain1
    small_out[2:3] = dshift1
    sbranch = g1.astype(BF)
    small_out[3:4] = column_sum(sbranch)
    put_halves(core, tn(sm_ref[...], sbranch), 4, keep, send, work)
    gsm = nt(sbranch, self_out[...]).astype(BF)
    for g in range(GROUPS):
        lanes = slice(g * LANES, (g + 1) * LANES)
        grads = pair(gsm, g)
        p = ps_ref[g]
        dp = nt(sv_ref[:, lanes], grads).astype(BF).astype(F32)
        pf = p.astype(F32)
        ds = (pf * (dp - jnp.sum(pf * dp, 0, keepdims=True))).astype(BF)
        gq_ref[:, lanes] = unpair(tn(ds, sk_ref[:, lanes])).astype(BF) * 0.125
        gk_ref[:, lanes] = nn(ds, pair(sq_ref[...], g)).astype(BF)
        gv_ref[:, lanes] = nn(p, grads).astype(BF)
    gq, gk, gv = gq_ref[...], gk_ref[...], gv_ref[...]
    gai = nt(gq, self_proj[0]) + nt(gk, self_proj[1])
    gx_out[...] = (g1 + gai + nt(gv, self_proj[2])).astype(BF)
    gpos_out[...] = gai + gci
    small_out[4:5] = column_sum(gq)
    small_out[5:6] = column_sum(gv)
    small_out[6:8] = jnp.zeros((2, width), F32)
    put_halves(core, tn(ai_ref[...], gq), 12, keep, send, work)
    put_halves(core, tn(ai_ref[...], gk), 16, keep, send, work)
    put_halves(core, tn(x_ref[...], gv), 20, keep, send, work)


def ffn_grad_kernel(ids, *refs):
    up_own, misc, down_own, keep, send0, send1, work = refs[4:]
    core = ids[1]
    units, width = up_own.shape
    ops = jnp.concatenate([ref[...] for ref in refs[:4]], axis=0)
    inputs, branch = ops[:, :width], ops[:, width:]
    bias = jnp.concatenate([row(misc, 2), row(misc, 3)[:, : units - width]], axis=1)
    pre = nt(inputs, up_own[...]) + bias
    phi = cdf(pre)
    act = (pre * phi).astype(BF)
    gact = nt(branch, down_own[...]).astype(BF).astype(F32)
    gpre = (gact * (phi + pre * density(pre))).astype(BF)
    blocks, size = keep.shape[1], keep.shape[2]
    for side, grad in enumerate((tn(inputs, gpre), tn(branch, act))):
        work[...] = grad
        for block in range(blocks):
            mine = pl.multiple_of((2 * block + core) * size, size)
            other = pl.multiple_of((2 * block + 1 - core) * size, size)
            keep[side, block] = work[pl.ds(mine, size), :].astype(BF)
            (send0, send1)[side][block] = work[pl.ds(other, size), :].astype(BF)


def ffn_fold_kernel(ids, keep, got0, got1, stay, go0, go1, *, bit):
    for side, (got, go) in enumerate(((got0, go0), (got1, go1))):
        for block in range(stay.shape[1]):
            mine, other = 2 * block + ids[bit], 2 * block + 1 - ids[bit]
            go[block] = plus(keep[side, other], got[other])
            stay[side, block] = plus(keep[side, mine], got[mine])


def ffn_finish_kernel(ids, keep, got0, got1, up_grad, down_grad):
    up_grad[...] = keep[0, 0].astype(F32) + got0[0].astype(F32)
    down_grad[...] = keep[1, 0].astype(F32) + got1[0].astype(F32)


def memory_back_kernel(
    ids,
    ds_ref,
    pc_ref,
    cq_ref,
    gcm_ref,
    featp,
    ki,
    vi,
    cross_proj,
    in_proj,
    res_ref,
    gx_ref,
    gpos_ref,
    small_a,
    small_b,
    bup,
    held,
    rows0,
    rows1,
    rows2,
    rows3,
    keep,
    send,
    gk_ref,
    gv_ref,
    gm_ref,
    gf_ref,
    work,
    small,
    *,
    rows_used,
):
    pb, core = ids[0], ids[1]
    width = featp.shape[1]
    rows = res_ref.shape[0]
    block = rows // GROUPS
    padded = featp.shape[0] // GROUPS
    pairs_q = [pair(cq_ref[...], g) for g in range(GROUPS)]
    pairs_g = [pair(gcm_ref[...], g) for g in range(GROUPS)]
    for j in range(GROUPS):
        here = slice(j * padded, (j + 1) * padded)
        for g in range(GROUPS):
            lanes = slice(g * LANES, (g + 1) * LANES)
            gk_ref[here, lanes] = nn(ds_ref[g, here], pairs_q[g]).astype(BF)
            gv_ref[here, lanes] = nn(pc_ref[g, here], pairs_g[g]).astype(BF)
        gm = (nt(gk_ref[here], cross_proj[1]) + nt(gv_ref[here], cross_proj[2])).astype(BF)
        gm_ref[here] = gm
        gf_ref[j] = nt(gm, in_proj[...]).astype(BF)
    for k, ref in enumerate((rows0, rows1, rows2, rows3)):
        at = pl.multiple_of((pb ^ k) * block, block)
        ref[0:padded] = gf_ref[pb ^ k]
        ref[padded : padded + block] = gx_ref[pl.ds(at, block), :]
        ref[padded + block : padded + 2 * block] = res_ref[pl.ds(at, block), :]
    put_halves(core, tn(ki[...], gk_ref[...]), 0, keep, send, work)
    put_halves(core, tn(vi[...], gv_ref[...]), 4, keep, send, work)
    put_halves(core, tn(featp[...], gm_ref[...]), 8, keep, send, work)

    small[...] = gpos_ref[...]
    extras = [
        row(small_b, 1),
        row(small_a, 2),
        row(small_a, 0),
        row(small_b, 2),
        row(small_a, 3),
        row(small_a, 1),
        row(small_b, 4),
        row(small_b, 5),
        row(small_b, 3),
        row(small_b, 0),
        column_sum(gv_ref[...]),
        row(small_a, 5),
        row(small_a, 4),
        column_sum(gm_ref[...]),
    ]
    for index, value in enumerate(extras):
        at = spare_row(index, block, rows_used)
        small[at : at + 1] = value
    for b in range(GROUPS):
        at = b * block + rows_used + 5
        total = bup[b ^ pb]
        small[at : at + 1] = total[:, :width]
        small[at + 1 : at + 2] = total[:, width:]
    for b in range(2):
        for side, ref in ((core, keep), (1 - core, send)):
            low = small[:, b * LANES : (b + 1) * LANES]
            high = small[:, (2 + b) * LANES : (3 + b) * LANES]
            ref[12, b * rows : (b + 1) * rows] = jnp.where(side == 0, low, high).astype(BF)


def spare_row(index, block, rows_used):
    return index // 5 * block + rows_used + index % 5


def put_whole(core, out, index, own, got):
    half = own.shape[1]
    mine = pl.multiple_of(core * half, half)
    other = pl.multiple_of((1 - core) * half, half)
    for b in range(4):
        put_block(mine, other, half, out, b, own, got, index + b)


def put_block(mine, other, half, out, b, own, got, index):
    lanes = slice(b * LANES, (b + 1) * LANES)
    out[pl.ds(mine, half), lanes] = own[index].astype(F32)
    out[pl.ds(other, half), lanes] = got[index].astype(F32)


def finish_chain_kernel(ids, own1, got1, own2, got2, cross_q, self_out, cross_out, self_proj):
    core = ids[1]
    put_whole(core, cross_q, 0, own1, got1)
    put_whole(core, self_out, 4, own1, got1)
    put_whole(core, cross_out, 8, own1, got1)
    for m in range(3):
        put_whole(core, self_proj.at[m], 4 * m, own2, got2)


def finish_memory_kernel(
    ids, own1, got1, cross_q, cross_, in_, pos_, self_bias_, cross_bias_, bup_, bdown_, gain_, shift_, inb_, small, *, rows_used
):
    core = ids[1]
    cross_[0] = cross_q[...]
    half = own1.shape[1]
    mine = pl.multiple_of(core * half, half)
    other = pl.multiple_of((1 - core) * half, half)
    for index in range(12):
        out = (cross_.at[1], cross_.at[2], in_)[index // 4]
        put_block(mine, other, half, out, index % 4, own1, got1, index)
    rows, width = small.shape
    block = rows // GROUPS
    for b in range(2):
        here = slice(b * rows, (b + 1) * rows)
        first = own1[12, here].astype(F32)
        second = got1[12, here].astype(F32)
        small[:, b * LANES : (b + 1) * LANES] = jnp.where(core == 0, first, second)
        small[:, (2 + b) * LANES : (3 + b) * LANES] = jnp.where(core == 0, second, first)
    for b in range(GROUPS):
        pos_[b * rows_used : (b + 1) * rows_used] = small[b * block : b * block + rows_used]
        at = b * block + rows_used + 5
        bup_[b : b + 1, :width] = small[at : at + 1]
        bup_[b : b + 1, width:] = small[at + 1 : at + 2]

    def spare(index):
        at = spare_row(index, block, rows_used)
        return small[at : at + 1]

    for ref, index in ((gain_, 0), (shift_, 3), (self_bias_, 6), (cross_bias_, 9)):
        for i in range(3):
            ref[i : i + 1] = spare(index + i)
    bdown_[...] = spare(12)
    inb_[...] = spare(13)


def hold_kernel(ids, got1, got2, got3, branch, out):
    out[...] = got1[:16, :LANES] + got2[:16, :LANES] + got3[:16, :LANES] + branch[:16, :LANES]


def order_kernel(ids, own, got1, got2, got3, out, grad, feats, *, block):
    pb = ids[0]
    part, used = feats.shape[1], out.shape[1]
    padded = own.shape[0] - 2 * block
    for k, ref in enumerate((own, got1, got2, got3)):
        feats[pb ^ k] = ref[0:part]
        grad[pb ^ k] = ref[padded : padded + used]
        out[pb ^ k] = ref[padded + block : padded + block + used]


class Far:
    def __init__(self, value, parts=None, emit=False):
        self.value, self.parts, self.emit = value, parts, emit


class Raw:
    def __init__(self, value):
        self.value = value


class Late:
    def __init__(self, ref, buffers, sems, parts):
        self.shape = ref.shape
        self.parts = parts
        self.buffers = buffers
        sources = [ref] if parts is None else [ref.at[part] for part in parts]
        self.copies = [
            pltpu.make_async_copy(source, buffer, sems.at[n])
            for n, (source, buffer) in enumerate(zip(sources, buffers))
        ]
        for copy in self.copies:
            copy.start()
        self.waiting = set(range(len(sources)))

    def ready(self, n):
        if n in self.waiting:
            self.waiting.discard(n)
            self.copies[n].wait()

    def __getitem__(self, index):
        if self.parts is None:
            self.ready(0)
            return self.buffers[0][index]
        n = self.parts.index(index)
        self.ready(n)
        return self.buffers[n][...]


class Places:
    def __getitem__(self, index):
        if index == 0:
            return lax.axis_index("pb")
        axis, bit = BITS[index - 1]
        return lax.rem(lax.div(lax.axis_index(axis), bit), 2)


CORE, X_WAY, Y_WAY = ("dp", 1), ("pb", 1), ("pb", 2)
BITS = [CORE, X_WAY, Y_WAY] + [("dp", 2 << n) for n in range(16)]


def place_of(way):
    return 1 + BITS.index(way)


class Order:
    def __init__(self):
        self.token = None

    def after(self, values):
        if self.token is None:
            return list(values)
        return list(lax.optimization_barrier((*values, self.token)))[:-1]


def call(order, kernel, args, outs, scratch=(), limit=16, near=True, micros=0.6, through=()):
    through = order.after(through)
    bare = order.after([arg.value if isinstance(arg, (Far, Raw)) else arg for arg in args])
    args = [
        Far(value, arg.parts, arg.emit)
        if isinstance(arg, Far)
        else Raw(value)
        if isinstance(arg, Raw)
        else value
        for value, arg in zip(bare, args)
    ]
    specs, values, extra, emitted, plans = [], [], [], [], []
    outs = list(outs)
    for arg in args:
        if isinstance(arg, (Far, Raw)):
            value = arg.value
            specs.append(pl.BlockSpec(memory_space=pl.ANY))
            values.append(pltpu.with_memory_space_constraint(value, pltpu.HBM))
            if isinstance(arg, Raw):
                plans.append(None)
                continue
            count = 1 if arg.parts is None else len(arg.parts)
            if arg.emit:
                plans.append((None, len(emitted), len(extra), count, arg.parts))
                emitted.append((value.shape, value.dtype))
            else:
                plans.append((len(extra), None, len(extra) + count, count, arg.parts))
                shape = value.shape if arg.parts is None else value.shape[1:]
                extra += [pltpu.VMEM(shape, value.dtype)] * count
            extra.append(pltpu.SemaphoreType.DMA((count,)))
        elif jnp.issubdtype(arg.dtype, jnp.integer):
            specs.append(pl.BlockSpec(memory_space=pltpu.SMEM))
            values.append(arg)
            plans.append(None)
        else:
            specs.append(pl.BlockSpec(memory_space=pltpu.VMEM))
            values.append(pltpu.with_memory_space_constraint(arg, pltpu.VMEM))
            plans.append(None)

    def body(*refs):
        given, rest = list(refs[: len(args)]), refs[len(args) + len(through) :]
        first, rest = rest[: len(outs)], rest[len(outs) :]
        copies, rest = rest[: len(emitted)], rest[len(emitted) + len(through) :]
        own, late = rest[: len(scratch)], rest[len(scratch) :]
        waits = []
        for index, plan in enumerate(plans):
            if plan is None:
                continue
            at, place, sem, count, parts = plan
            if place is None:
                buffers = late[at : at + count]
            elif parts is None:
                buffers = [copies[place]]
            else:
                buffers = [copies[place].at[part] for part in parts]
            given[index] = Late(given[index], buffers, late[sem], parts)
            waits.append(given[index])
        kernel(Places(), *given, *first, *own)
        for one in waits:
            for n in sorted(one.waiting):
                one.ready(n)

    whole = [(o, near) for o in outs] + [(o, True) for o in emitted]
    result = pl.pallas_call(
        body,
        out_shape=[pltpu.VMEM(*o) if here else jax.ShapeDtypeStruct(*o) for o, here in whole]
        + [jax.ShapeDtypeStruct(value.shape, value.dtype) for value in through],
        in_specs=specs + [pl.BlockSpec(memory_space=pl.ANY)] * len(through),
        out_specs=[pl.BlockSpec(memory_space=pltpu.VMEM)] * len(whole)
        + [pl.BlockSpec(memory_space=pl.ANY)] * len(through),
        input_output_aliases={len(args) + n: len(whole) + n for n in range(len(through))},
        scratch_shapes=list(scratch) + extra,
        compiler_params=pltpu.CompilerParams(vmem_limit_bytes=limit * 1024 * 1024),
        cost_estimate=pl.CostEstimate(
            flops=int(micros * RATE) + 1, bytes_accessed=int(micros * 3.7e6) + 1, transcendentals=0
        ),
    )(*values, *through)
    order.token = result[0]
    return result


def swap(value, axis, bit):
    size = lax.axis_size(axis)
    return lax.ppermute(value, axis, [(i, i ^ bit) for i in range(size)])


def bit_of(axis, bit):
    return (lax.axis_index(axis) // bit) % 2


def plus(left, right):
    return (left.astype(F32) + right.astype(F32)).astype(BF)


def bit_of(way):
    axis, bit = way
    return (lax.axis_index(axis) // bit) % 2


def halve(keep, got, bit):
    half = keep.shape[1] // 2
    total = plus(keep, got)
    mine = lax.dynamic_slice_in_dim(total, bit * half, half, 1)
    other = lax.dynamic_slice_in_dim(total, (1 - bit) * half, half, 1)
    return mine, other


def fold(order, groups, micros=0.6):
    rows = groups[0][0][0][0].shape[1] // 2
    if rows % 16:
        result = []
        for pieces, way in groups:
            done = [
                halve(keep[a:b], got[a - m : b - m], bit_of(way)) for keep, got, a, b, m in pieces
            ]
            result += [jnp.concatenate(side) for side in zip(*done)]
        return result
    args, outs = [], []
    for pieces, way in groups:
        count = sum(b - a for _, _, a, b, _ in pieces)
        outs += [((count, rows, LANES), BF)] * 2
        for keep, got, _, _, _ in pieces:
            args += [keep, got]

    def kernel(ids, *refs):
        given, made = list(refs[: len(args)]), list(refs[len(args) :])
        for pieces, way in groups:
            stay, go = made.pop(0), made.pop(0)
            bit = ids[place_of(way)]
            mine = pl.multiple_of(bit * rows, rows)
            other = pl.multiple_of((1 - bit) * rows, rows)
            at = 0
            for _, _, a, b, m in pieces:
                keep, got = given.pop(0), given.pop(0)
                for block in range(a, b):
                    for ref, start in ((go, other), (stay, mine)):
                        here = pl.ds(start, rows)
                        ref[at] = plus(keep[block, here], got[block - m, here])
                    at += 1

    return call(order, kernel, args, outs, limit=4, micros=micros)


def add_up(order, pieces, micros=0.6):
    if pieces[0][0].shape[1] % 16:
        return jnp.concatenate([plus(keep, got) for keep, got in pieces])

    def kernel(ids, *refs):
        at = 0
        for keep, got in zip(refs[0:-1:2], refs[1:-1:2]):
            refs[-1][at : at + keep.shape[0]] = plus(keep[...], got[...])
            at += keep.shape[0]

    count = sum(keep.shape[0] for keep, _ in pieces)
    shape = (count,) + pieces[0][0].shape[1:]
    args = [ref for piece in pieces for ref in piece]
    return call(order, kernel, args, [(shape, BF)], limit=4, micros=micros)[0]


def join(order, pieces, micros=0.6, through=()):
    if pieces[0][0].shape[1] % 16:
        result = []
        for value, got, way, cuts in pieces:
            full = jnp.where(
                bit_of(way) == 0, jnp.concatenate([value, got], 1), jnp.concatenate([got, value], 1)
            )
            result += [full[a:b] for a, b in cuts]
        return result + list(through)
    outs = []
    for value, _, _, cuts in pieces:
        outs += [((b - a, 2 * value.shape[1], LANES), BF) for a, b in cuts]

    def kernel(ids, *refs):
        given, made = list(refs[: 2 * len(pieces)]), list(refs[2 * len(pieces) :])
        for _, _, way, cuts in pieces:
            value, got = given.pop(0), given.pop(0)
            rows = value.shape[1]
            bit = ids[place_of(way)]
            mine = pl.multiple_of(bit * rows, rows)
            other = pl.multiple_of((1 - bit) * rows, rows)
            for a, b in cuts:
                out = made.pop(0)
                for block in range(a, b):
                    out[block - a, pl.ds(mine, rows)] = value[block]
                    out[block - a, pl.ds(other, rows)] = got[block]

    args = [ref for value, got, _, _ in pieces for ref in (value, got)]
    return call(order, kernel, args, outs, limit=4, micros=micros, through=through)


def on_device(
    tokens,
    query_pos,
    features,
    camera_mask,
    out_grad,
    self_proj,
    self_out,
    self_bias,
    cross_proj,
    cross_out,
    cross_bias,
    w_up,
    b_up,
    w_down,
    b_down,
    norm_gain,
    norm_bias,
    in_proj,
    in_bias,
):
    order = Order()
    pb_size = lax.axis_size("pb")
    dp_size = lax.axis_size("dp")
    ways = [("dp", 1 << i) for i in range(1, dp_size.bit_length() - 1)]
    width = tokens.shape[2]
    used = tokens.shape[1]
    block = -(-used // 16) * 16
    rows = block * pb_size
    mem = features.shape[1]
    part = mem // pb_size
    padded = -(-part // 16) * 16
    slots = padded * pb_size
    units = b_up.shape[0]

    up, down = w_up.T, w_down.T
    cut = units // 2
    low, high, after, before = call(
        order,
        pick_kernel,
        [Raw(up), Raw(down)],
        [((cut, width), BF)] * 2 + [((cut + 16, width), BF)] * 2,
        micros=1.4,
        scratch=[pltpu.SemaphoreType.DMA((8,))],
        limit=4,
    )
    fy0 = swap(low, *Y_WAY)
    fx1 = swap(high, *X_WAY)
    misc = (
        jnp.pad(in_bias[None], ((0, 3), (0, 0)))
        + jnp.pad(b_down[None], ((1, 2), (0, 0)))
        + jnp.pad(jnp.pad(b_up, (0, 2 * width - units)).reshape(2, width), ((2, 0), (0, 0)))
    )
    turn = lambda value: value.transpose(1, 0, 2)
    send = call(
        order,
        functools.partial(start_kernel, rows_used=used),
        [turn(tokens), turn(out_grad), misc],
        [((block, 2 * width), BF)] * 4,
        scratch=[
            pltpu.VMEM((used * pb_size, 2 * width), F32),
            pltpu.VMEM((rows, 2 * width), F32),
        ],
    )
    got = [send[0]] + [swap(send[k], "pb", k) for k in range(1, pb_size)]
    column = np.arange(width)
    rate = 1.0 / 10000.0 ** ((column // 2 * 2) / width)
    angle = np.arange(padded)[:, None] * rate
    start = np.arange(pb_size)[:, None] * part * rate
    even = column % 2 == 0
    waves = np.concatenate(
        [
            np.where(even, np.sin(start), np.cos(start)),
            np.where(even, np.cos(start), -np.sin(start)),
        ]
    )
    sines, cosines, waves = [
        jnp.asarray(value.astype(np.float32)) for value in (np.sin(angle), np.cos(angle), waves)
    ]

    wide = (slots, width)
    featp, ki, vi, ck, cv, in_proj, cross_proj = call(
        order,
        memory_kernel,
        [
            Raw(features),
            Far(sines),
            Far(cosines),
            Far(waves),
            Far(in_proj, emit=True),
            misc,
            Far(cross_proj, (1, 2, 0), emit=True),
            Far(cross_bias),
        ],
        [(wide, BF)] * 5,
        micros=0.0,
        scratch=[pltpu.VMEM((mem, width), BF), pltpu.SemaphoreType.DMA],
    )
    fx1, fy0, after, before = order.after((fx1, fy0, after, before))
    fx0 = swap(before, *X_WAY)
    fy1 = swap(after, *Y_WAY)
    fx1, fy0, *got = order.after((fx1, fy0, *got))
    fd0 = swap(fy0, *X_WAY)
    fd1 = swap(fx1, *Y_WAY)
    sx1, sy0 = swap(fx1, *CORE), swap(fy0, *CORE)
    got[0], sx1, sy0 = lax.optimization_barrier((got[0], sx1, sy0))
    flat = (rows, width)
    scores = (GROUPS, slots, 2 * rows)
    (x, cot, ai, sq, sk, sv, ps, sm, xhat1, rstd1, ci, cq, pc, cm, h2, xhat2, rstd2, bups, h2b, self_proj, self_out, cross_out, norm_gain, norm_bias, up, down) = call(
        order,
        functools.partial(forward_kernel, rows_used=used),
        [
            camera_mask,
            *got,
            Far(query_pos),
            Far(self_proj, (0, 1, 2), emit=True),
            Far(self_out, emit=True),
            Far(self_bias),
            cross_proj,
            Far(cross_out, emit=True),
            Far(cross_bias),
            Far(norm_gain, emit=True),
            Far(norm_bias, emit=True),
            ck,
            cv,
            Far(up, emit=True),
            Far(down, emit=True),
        ],
        [
            (flat, BF),
            (flat, BF),
            (flat, BF),
            (flat, BF),
            (flat, BF),
            (flat, BF),
            ((GROUPS, rows, 2 * rows), BF),
            (flat, BF),
            (flat, F32),
            ((rows, 1), F32),
            (flat, BF),
            (flat, BF),
            (scores, BF),
            (flat, BF),
            (flat, F32),
            (flat, F32),
            ((rows, 1), F32),
            ((2 * pb_size, width), F32),
            (flat, BF),
        ],
        micros=8.0,
        scratch=[pltpu.VMEM((slots, 2 * rows), F32), pltpu.VMEM(flat, F32)],
    )
    fd0, fd1 = order.after((fd0, fd1))
    sd0, sd1 = swap(fd0, *CORE), swap(fd1, *CORE)
    down_part, pre, far_weights = call(
        order,
        ffn_first_kernel,
        [h2b, bups, up, down, Raw(fd0), Raw(fd1), Raw(sd0), Raw(sd1)],
        [(flat, F32), ((2, rows, units), F32), ((2, 1, units, width), BF)],
        micros=0.0,
        scratch=[pltpu.SemaphoreType.DMA((2, 2))],
    )
    fx0, fy1 = order.after((fx0, fy1))
    sx0, sy1 = swap(fx0, *CORE), swap(fy1, *CORE)
    near = [fx0, fx1, fy0, fy1, sx0, sx1, sy0, sy1]
    res, ops, g2, small_a, bup = call(
        order,
        ffn_second_kernel,
        [
            h2,
            h2b,
            cot,
            xhat2,
            rstd2,
            bups,
            up,
            down,
            down_part,
            pre,
            far_weights,
            misc,
            norm_gain,
            norm_bias,
            *[Raw(value) for value in near],
        ],
        [
            (flat, BF),
            ((rows, 2 * width), BF),
            (flat, F32),
            ((8, width), F32),
            ((pb_size, 1, 2 * width), F32),
        ],
        micros=6.0,
        scratch=[pltpu.VMEM((2, 2, units, width), BF), pltpu.SemaphoreType.DMA((2, 4))],
    )
    others = [swap(ops, "pb", k) for k in range(1, pb_size)]
    halves = ((24, width // 2, LANES), BF)
    ds, gcm, gx, gpos, small_b, keep12, *sends12 = call(
        order,
        backward_kernel,
        [
            g2,
            pc,
            ck,
            cv,
            cq,
            ci,
            cm,
            xhat1,
            rstd1,
            x,
            ai,
            sq,
            sk,
            sv,
            ps,
            sm,
            self_proj,
            self_out,
            cross_proj,
            cross_out,
            norm_gain,
        ],
        [
            (scores, BF),
            (flat, BF),
            (flat, BF),
            (flat, F32),
            ((8, width), F32),
            halves,
        ]
        + [((6, width // 2, LANES), BF)] * 4,
        micros=7.8,
        scratch=[
            pltpu.VMEM((slots, 2 * rows), BF),
            pltpu.VMEM((width, width), F32),
            pltpu.VMEM(flat, BF),
            pltpu.VMEM(flat, BF),
            pltpu.VMEM(flat, BF),
        ],
    )
    got12 = [swap(send, *CORE) for send in sends12]
    piece = width // dp_size
    (held,) = call(order, hold_kernel, [*others, gcm], [((16, LANES), BF)], limit=2, micros=2.0)
    ka, sa, kb, sb = fold(
        order,
        [
            ([(keep12, got12[0], 0, 6, 0), (keep12, got12[1], 6, 12, 6)], X_WAY),
            ([(keep12, got12[2], 12, 18, 12), (keep12, got12[3], 18, 24, 18)], Y_WAY),
        ],
    )
    ra, rb = swap(sa, *X_WAY), swap(sb, *Y_WAY)

    def ffn_fold(keep, gots, micros):
        way = ways[(dp_size // 2).bit_length() - keep.shape[1].bit_length()]
        half = keep.shape[1] // 2
        keep, *sends = call(
            order,
            functools.partial(ffn_fold_kernel, bit=place_of(way)),
            [keep, *gots],
            [((2, half, piece, units), BF)] + [((half, piece, units), BF)] * 2,
            limit=4,
            micros=micros,
        )
        return keep, [swap(send, *way) for send in sends]

    halves3 = ((13, width // 2, LANES), BF)
    *rows_out, keep3, send3 = call(
        order,
        functools.partial(memory_back_kernel, rows_used=used),
        [
            ds,
            pc,
            cq,
            gcm,
            featp,
            ki,
            vi,
            cross_proj,
            in_proj,
            res,
            gx,
            gpos,
            small_a,
            small_b,
            bup,
            held,
        ],
        [((padded + 2 * block, width), BF)] * 4 + [halves3, halves3],
        micros=6.4,
        scratch=[
            pltpu.VMEM(wide, BF),
            pltpu.VMEM(wide, BF),
            pltpu.VMEM(wide, BF),
            pltpu.VMEM((pb_size, padded, width), BF),
            pltpu.VMEM((width, width), F32),
            pltpu.VMEM(flat, F32),
        ],
    )

    fkeep, *fsends = call(
        order,
        ffn_grad_kernel,
        [ops, *others, up, misc, down],
        [((2, dp_size // 2, piece, units), BF)] + [((dp_size // 2, piece, units), BF)] * 2,
        micros=2.8,
        scratch=[pltpu.VMEM((width, units), F32)],
    )
    fgots = [swap(send, *CORE) for send in fsends]
    ra, rb, send3 = lax.optimization_barrier((ra, rb, send3))
    got3 = swap(send3, *CORE)
    z_way, far_ways = ways[0], ways[1:]
    ka, sa, kb, sb = fold(
        order, [([(ka, ra, 0, 12, 0)], Y_WAY), ([(kb, rb, 0, 12, 0)], X_WAY)], 0.3
    )
    ra, rb = swap(sa, *Y_WAY), swap(sb, *X_WAY)
    kc, sc = fold(order, [([(keep3, got3, 0, 13, 0)], z_way)], 0.3)
    rc = swap(sc, *z_way)
    kab, sab = fold(order, [([(ka, ra, 0, 12, 0), (kb, rb, 0, 12, 0)], z_way)], 2.7)
    rab = swap(sab, *z_way)
    fkeep, fgots = ffn_fold(fkeep, fgots, 0.0)
    kc, sc = fold(order, [([(kc, rc, 0, 13, 0)], X_WAY)], 0.3)
    rc = swap(sc, *X_WAY)
    vab = add_up(order, [(kab, rab)], 0.6)
    for way in far_ways[:-1]:
        rab = swap(vab, *way)
        vab = add_up(order, [(vab, rab)], 0.3)
    rab = swap(vab, *far_ways[-1])
    kc, sc = fold(order, [([(kc, rc, 0, 13, 0)], Y_WAY)], 0.3)
    rc = swap(sc, *Y_WAY)
    arrived = [rows_out[0]] + [swap(rows_out[k], "pb", k) for k in range(1, pb_size)]
    while fkeep.shape[1] > 1:
        fkeep, fgots = ffn_fold(fkeep, fgots, 0.0)
    vc = add_up(order, [(kc, rc)], 0.3)
    for way in far_ways[:-1]:
        rc = swap(vc, *way)
        vc = add_up(order, [(vc, rc)], 0.3)
    rc = swap(vc, *far_ways[-1])
    vab = add_up(order, [(vab, rab)], 0.3)
    rab = swap(vab, *z_way)
    vc = add_up(order, [(vc, rc)], 1.2)
    rc = swap(vc, *Y_WAY)
    rab, *arrived[1:3] = lax.optimization_barrier((rab, *arrived[1:3]))
    va, vb = join(order, [(vab, rab, z_way, [(0, 12), (12, 24)])], 0.3)
    ra, rb = swap(va, *Y_WAY), swap(vb, *X_WAY)
    (vc,) = join(order, [(vc, rc, Y_WAY, [(0, 13)])], 1.2)
    rc = swap(vc, *X_WAY)
    ra, arrived[3] = lax.optimization_barrier((ra, arrived[3]))
    va, vb = join(order, [(va, ra, Y_WAY, [(0, 12)]), (vb, rb, X_WAY, [(0, 12)])], 0.5)
    ra, rb = swap(va, *X_WAY), swap(vb, *Y_WAY)
    (vc,) = join(order, [(vc, rc, X_WAY, [(0, 13)])], 2.4)
    rc = swap(vc, *z_way)
    exchanged = call(
        order,
        functools.partial(order_kernel, block=block),
        arrived,
        [(tokens.shape, BF), (tokens.shape, BF), ((pb_size, part, width), BF)],
        micros=0.3,
    )
    exchanged = [turn(value) for value in exchanged]
    ffn_up, ffn_down = call(
        order, ffn_finish_kernel, [fkeep, *fgots], [((piece, units), F32)] * 2, near=False
    )
    va, vb, *exchanged = join(
        order, [(va, ra, X_WAY, [(0, 12)]), (vb, rb, Y_WAY, [(0, 12)])], 0.6, exchanged
    )
    layer_out, grad_tokens, grad_features = [turn(value) for value in exchanged]
    ra, rb = swap(va, *CORE), swap(vb, *CORE)
    (vc,) = join(order, [(vc, rc, z_way, [(0, 13)])], 4.0)
    rc = swap(vc, *CORE)
    matrix = ((width, width), F32)
    three = ((3, width, width), F32)
    g_cross_q, g_self_out, g_cross_out, g_self_proj = call(
        order,
        finish_chain_kernel,
        [va, ra, vb, rb],
        [matrix, matrix, matrix, three],
        near=False,
    )
    bias3 = ((3, width), F32)
    bias1 = ((1, width), F32)
    (
        g_cross_proj,
        g_in_proj,
        g_pos,
        g_self_bias,
        g_cross_bias,
        g_bup,
        g_bdown,
        g_gain,
        g_shift,
        g_inb,
    ) = call(
        order,
        functools.partial(finish_memory_kernel, rows_used=used),
        [vc, rc, g_cross_q],
        [
            three,
            matrix,
            (query_pos.shape, F32),
            bias3,
            bias3,
            ((pb_size, 2 * width), F32),
            bias1,
            bias3,
            bias3,
            bias1,
        ],
        scratch=[pltpu.VMEM(flat, F32)],
        near=False,
    )

    return (
        layer_out,
        grad_tokens,
        grad_features,
        g_pos,
        g_self_proj,
        g_self_out,
        g_self_bias,
        g_cross_proj,
        g_cross_out,
        g_cross_bias,
        ffn_up,
        g_bup[:, :units].reshape(-1),
        ffn_down,
        g_bdown[0],
        g_gain,
        g_shift,
        g_in_proj,
        g_inb[0],
    )


def solution(mesh):
    return jax.shard_map(
        on_device,
        mesh=mesh,
        in_specs=(
            P("dp", "pb", None),
            P(),
            P("dp", None, None),
            P("dp", None),
            P("dp", "pb", None),
            P(),
            P(),
            P(),
            P(),
            P(),
            P(),
            P(None, "pb"),
            P("pb"),
            P(None, "pb"),
            P(),
            P(),
            P(),
            P(),
            P(),
        ),
        out_specs=(
            P("dp", "pb", None),
            P("dp", "pb", None),
            P("dp", "pb", None),
            P(),
            P(),
            P(),
            P(),
            P(),
            P(),
            P(),
            P("dp", "pb"),
            P(),
            P("dp", "pb"),
            P(),
            P(),
            P(),
            P(),
            P(),
        ),
        check_vma=False,
    )
```

```python
import functools

import jax
import jax.numpy as jnp
import numpy as np
from jax import lax
from jax.experimental import pallas as pl
from jax.experimental.pallas import tpu as pltpu
from jax.sharding import PartitionSpec as P

BF = jnp.bfloat16
F32 = jnp.float32
HEADS = 8
LANES = 128
GROUPS = 4
FAR = -1e30
START_COSTS = (0.0, 8.0, 0.0, 6.0, 7.8, 2.0)
RATE = 1.15e9
STEPS = (
    ("memory", 5.0),
    ("ffn", 0.5),
    ("features", 0.3),
    ("ab2", 0.3),
    ("c1", 0.3),
    ("ab3", 2.7),
    ("ffn1", 0.0),
    ("c2", 0.3),
    ("ab4", 0.6),
    ("c3", 0.3),
    ("ffn2", 0.0),
    ("c4", 0.3),
    ("ab5", 0.3),
    ("c5", 1.2),
    ("ab6", 0.3),
    ("c6", 1.2),
    ("ab7", 0.5),
    ("c7", 2.4),
    ("order", 0.3),
    ("ffn3", 0.6),
    ("ab8", 0.6),
    ("own", 0.0),
    ("c8", 4.0),
    ("c_own", 0.0),
    ("finish", 1.5),
)
NEAR_AT, FAR_AT = "ab5", "ab6"


def dims(left, right, a, b):
    return lax.dot_general(left, right, (((a,), (b,)), ((), ())), preferred_element_type=F32)


def nn(left, right):
    return dims(left, right, 1, 0)


def nt(left, right):
    return dims(left, right, 1, 1)


def tn(left, right):
    return dims(left, right, 0, 0)


def lane_masks(dtype=BF):
    lane = lax.broadcasted_iota(jnp.int32, (1, LANES), 1)
    low = (lane < LANES // 2).astype(F32)
    return low.astype(dtype), (1.0 - low).astype(dtype)


def pair(value, group):
    part = value[:, group * LANES : (group + 1) * LANES]
    low, high = lane_masks()
    return jnp.concatenate([part * low, part * high], axis=0)


def unpair(value):
    rows = value.shape[0] // 2
    lane = lax.broadcasted_iota(jnp.int32, (rows, LANES), 1)
    return jnp.where(lane < LANES // 2, value[:rows], value[rows:])


def row_totals(mix, grad, group):
    lanes = slice(group * LANES, (group + 1) * LANES)
    product = (mix[:, lanes].astype(F32) * grad[:, lanes].astype(F32)).astype(BF)
    low, high = lane_masks()
    heads = jnp.concatenate([low, high, jnp.zeros((14, LANES), BF)], axis=0)
    sums = nt(heads, product)
    return jnp.concatenate([sums[0:1], sums[1:2]], axis=1)


def eights(value, op):
    return op(value.reshape(value.shape[0] // 8, 8, value.shape[1]), axis=0)


def norm(value):
    center = value - jnp.mean(value, -1, keepdims=True)
    rstd = lax.rsqrt(jnp.mean(center * center, -1, keepdims=True) + 1e-05)
    return center * rstd, rstd


def norm_back(xhat, rstd, gain, grad):
    scaled = grad * gain
    inner = jnp.mean(scaled, -1, keepdims=True) + xhat * jnp.mean(
        scaled * xhat, -1, keepdims=True
    )
    return (
        rstd * (scaled - inner),
        jnp.sum(grad * xhat, 0, keepdims=True),
        jnp.sum(grad, 0, keepdims=True),
    )


def column_sum(value):
    return jnp.sum(value.astype(F32), 0, keepdims=True)


def row(ref, index):
    return ref[index : index + 1, :].astype(F32)


def cdf(value):
    return 0.5 * (1.0 + lax.erf(value * np.float32(0.7071067811865476)))


def density(value):
    return jnp.exp(-0.5 * value * value) * np.float32(0.3989422804014327)


class Chain:
    def __init__(self, refs):
        self.refs = refs

    def __setitem__(self, index, value):
        size = self.refs[0].shape[0]
        self.refs[index // size][index % size] = value


def put_halves(core, value, index, keep_ref, send_ref, scratch):
    half = value.shape[0] // 2
    scratch[...] = value
    mine = pl.multiple_of(core * half, half)
    other = pl.multiple_of((1 - core) * half, half)
    for block in range(value.shape[1] // LANES):
        lanes = slice(block * LANES, (block + 1) * LANES)
        keep_ref[index + block] = scratch[pl.ds(mine, half), lanes].astype(BF)
        send_ref[index + block] = scratch[pl.ds(other, half), lanes].astype(BF)


def pick_kernel(ids, up, down, up_half, down_half, up_wide, down_wide, sems):
    core = ids[1]
    copies = []
    for ref, half, wide in ((up, up_half, up_wide), (down, down_half, down_wide)):
        for out in (half, wide):
            start = core * (ref.shape[0] - out.shape[0])
            size = out.shape[0] // 2
            for m in range(2):
                copies.append(
                    pltpu.make_async_copy(
                        ref.at[pl.ds(pl.multiple_of(start + m * size, 16), size)],
                        out.at[pl.ds(m * size, size)],
                        sems.at[len(copies)],
                    )
                )
    for copy in copies:
        copy.start()
    for copy in copies:
        copy.wait()


def start_kernel(
    ids, tokens, cots, misc, send0, send1, send2, send3, flat, turned, *, rows_used
):
    pb = ids[0]
    rows, width2 = turned.shape
    width = width2 // 2
    block = rows // GROUPS
    count = rows_used * GROUPS
    for q in range(rows_used):
        flat[q * GROUPS : (q + 1) * GROUPS, :width] = tokens[q].astype(F32)
        flat[q * GROUPS : (q + 1) * GROUPS, width:] = cots[q].astype(F32)
    place = lax.broadcasted_iota(jnp.int32, (rows, count), 0)
    query = lax.broadcasted_iota(jnp.int32, (rows, count), 1)
    hit = query == lax.rem(place, block) * GROUPS + lax.div(place, block)
    used = lax.rem(place, block) < rows_used
    chosen = jnp.where(jnp.logical_and(hit, used), 1.0, 0.0).astype(BF)
    turned[...] = nn(chosen, flat[...].astype(BF))
    for b in range(GROUPS):
        at = b * block + rows_used
        turned[at : at + 2, :width] = misc[2:4, :].astype(F32)
    for k, ref in enumerate((send0, send1, send2, send3)):
        at = pl.multiple_of((pb ^ k) * block, block)
        ref[...] = turned[pl.ds(at, block), :].astype(BF)


def memory_kernel(
    ids, feats, sines, cosines, waves, in_proj, misc, cross_proj, cross_bias, featp, ki, vi, k, v, buf, sems
):
    blocks = GROUPS
    slots = buf.shape[0]
    part = slots // blocks
    padded = featp.shape[0] // blocks
    copy = pltpu.make_async_copy(feats.at[ids[0]], buf, sems)
    copy.start()
    for j in range(blocks):
        featp[(j + 1) * padded - 16 : (j + 1) * padded] = jnp.zeros((16, featp.shape[1]), BF)
    copy.wait()
    bias = row(misc, 0)
    for j in range(blocks):
        here = slice(j * padded, (j + 1) * padded)
        featp[j * padded : j * padded + part] = buf[j * part : (j + 1) * part]
        memory = nn(featp[here], in_proj[...]) + bias
        places = cosines[...] * row(waves, j) + sines[...] * row(waves, blocks + j)
        key_input = (memory + places).astype(BF)
        value_input = memory.astype(BF)
        ki[here] = key_input
        vi[here] = value_input
        k[here] = nn(key_input, cross_proj[1]).astype(BF)
        v[here] = (nn(value_input, cross_proj[2]) + row(cross_bias, 1)).astype(BF)


def forward_kernel(
    ids,
    mask,
    own,
    got1,
    got2,
    got3,
    query_pos,
    self_proj,
    self_out,
    self_bias,
    cross_proj,
    cross_out,
    cross_bias,
    gains,
    shifts,
    k_ref,
    v_ref,
    up_,
    down_,
    x_out,
    cot_out,
    ai_out,
    sq_out,
    sk_out,
    sv_out,
    ps_out,
    sm_out,
    xhat1_out,
    rstd1_out,
    ci_out,
    cq_out,
    pc_out,
    cm_out,
    h2_out,
    xhat2_out,
    rstd2_out,
    bups_out,
    h2b_out,
    scores,
    pos_ref,
    *,
    rows_used,
):
    pb = ids[0]
    width = pos_ref.shape[1]
    block = own.shape[0]
    for k, ref in enumerate((own, got1, got2, got3)):
        at = pl.multiple_of((pb ^ k) * block, block)
        x_out[pl.ds(at, block), :] = ref[:, :width]
        cot_out[pl.ds(at, block), :] = ref[:, width:]
        bups_out[2 * k : 2 * k + 2] = ref[rows_used : rows_used + 2, :width].astype(F32)
    rows = x_out.shape[0]
    pos_ref[...] = jnp.zeros(pos_ref.shape, F32)
    for b in range(GROUPS):
        pos_ref[b * block : b * block + rows_used] = query_pos[
            b * rows_used : (b + 1) * rows_used
        ].astype(F32)
    pos = pos_ref[...]
    x = x_out[...].astype(F32)
    ai = (x + pos).astype(BF)
    ai_out[...] = ai
    sq_out[...] = ((nn(ai, self_proj[0]) + row(self_bias, 0)) * 0.125).astype(BF)
    sk_out[...] = nn(ai, self_proj[1]).astype(BF)
    sv_out[...] = (nn(x_out[...], self_proj[2]) + row(self_bias, 1)).astype(BF)
    key_row = lax.broadcasted_iota(jnp.int32, (rows, 2 * rows), 0)
    spare = jnp.where(lax.rem(key_row, block) < rows_used, 0.0, FAR).astype(F32)
    for g in range(GROUPS):
        lanes = slice(g * LANES, (g + 1) * LANES)
        s = nt(sk_out[:, lanes], pair(sq_out[...], g)) + spare
        e = jnp.exp(s - jnp.max(s, 0, keepdims=True))
        p = (e * (1.0 / jnp.sum(e, 0, keepdims=True))).astype(BF)
        ps_out[g] = p
        sm_out[:, lanes] = unpair(tn(p, sv_out[:, lanes])).astype(BF)
    xhat, rstd = norm(x + nn(sm_out[...], self_out[...]) + row(self_bias, 2))
    xhat1_out[...] = xhat
    rstd1_out[...] = rstd
    h1 = xhat * row(gains, 0) + row(shifts, 0)
    ci = (h1 + pos).astype(BF)
    ci_out[...] = ci
    cq_out[...] = ((nn(ci, cross_proj[0]) + row(cross_bias, 0)) * 0.125).astype(BF)

    padded = k_ref.shape[0] // GROUPS
    used = rows_used * 12
    slot_row = lax.broadcasted_iota(jnp.int32, (padded, 2 * rows), 0)
    for g in range(GROUPS):
        lanes = slice(g * LANES, (g + 1) * LANES)
        queries = pair(cq_out[...], g)
        top = jnp.full((8, 2 * rows), FAR, F32)
        for j in range(GROUPS):
            here = slice(j * padded, (j + 1) * padded)
            live = jnp.where(mask[pb, j] > 0, 0.0, -1000000000.0).astype(F32)
            s = nt(k_ref[here, lanes], queries) + jnp.where(slot_row < used, live, FAR)
            scores[here] = s
            top = jnp.maximum(top, eights(s, jnp.max))
        top = jnp.max(top, 0, keepdims=True)
        total = jnp.zeros((8, 2 * rows), F32)
        for j in range(GROUPS):
            here = slice(j * padded, (j + 1) * padded)
            e = jnp.exp(scores[here] - top)
            scores[here] = e
            total = total + eights(e, jnp.sum)
        inverse = 1.0 / jnp.sum(total, 0, keepdims=True)
        for j in range(GROUPS):
            here = slice(j * padded, (j + 1) * padded)
            pc_out[g, here] = (scores[here] * inverse).astype(BF)
        cm_out[:, lanes] = unpair(tn(pc_out[g], v_ref[:, lanes])).astype(BF)
    xhat, rstd = norm(h1 + nn(cm_out[...], cross_out[...]) + row(cross_bias, 2))
    xhat2_out[...] = xhat
    rstd2_out[...] = rstd
    h2 = xhat * row(gains, 1) + row(shifts, 1)
    h2_out[...] = h2
    h2b_out[...] = h2.astype(BF)


def part_of(ref, cut, core):
    spare = ref.shape[0] - cut
    return ref[pl.ds(pl.multiple_of(core * spare, 16), cut), :]


def bias_of(bups, p, units):
    width = bups.shape[1]
    return jnp.concatenate(
        [bups[2 * p : 2 * p + 1], bups[2 * p + 1 : 2 * p + 2, : units - width]], axis=1
    )


def bias_halves(bups, p, units, core):
    whole = bias_of(bups, p, units)
    low, high = whole[:, : units // 2], whole[:, units // 2 :]
    return jnp.where(core == 0, low, high), jnp.where(core == 0, high, low)


def ffn_first_kernel(
    ids, h2_ref, bups, up_own, down_own, up_f, down_f, up_s, down_s, down_out, pre_own, pre_far
):
    core = ids[1]
    h2 = h2_ref[...]
    units = up_own.shape[0]
    pre = nt(h2, up_own[...]) + bias_of(bups, 0, units)
    pre_own[...] = pre
    down = nn((pre * cdf(pre)).astype(BF), down_own[...])
    biases = bias_halves(bups, 3, units, core)
    for n, (up, dn) in enumerate(((up_f, down_f), (up_s, down_s))):
        pre = nt(h2, up[...]) + biases[n]
        pre_far[n] = pre
        down = down + nn((pre * cdf(pre)).astype(BF), dn[...])
    down_out[...] = down


def ffn_second_kernel(
    ids,
    h2_ref,
    h2b_ref,
    cot_ref,
    xhat2_ref,
    rstd2_ref,
    bups,
    up_own,
    down_own,
    down_ref,
    pre_own,
    pre_far,
    misc,
    gains,
    shifts,
    xu_f,
    xd_f,
    yu_f,
    yd_f,
    du_f,
    dd_f,
    xu_s,
    xd_s,
    yu_s,
    yd_s,
    du_s,
    dd_s,
    res_out,
    ops_out,
    g2_out,
    small_out,
    bup_out,
    pre_near,
):
    core = ids[1]
    units = up_own.shape[0]
    cut = units // 2
    width = h2_ref.shape[1]
    near = (
        (xu_f, xd_f, core),
        (xu_s, xd_s, 1 - core),
        (yu_f, yd_f, core),
        (yu_s, yd_s, 1 - core),
    )
    h2b = h2b_ref[...]
    down = down_ref[...]
    for n, (up, dn, place) in enumerate(near):
        pre = nt(h2b, part_of(up, cut, place)) + bias_halves(bups, n // 2 + 1, units, core)[n % 2]
        pre_near[n] = pre
        down = down + nn((pre * cdf(pre)).astype(BF), part_of(dn, cut, place))
    xhat, rstd = norm(h2_ref[...] + down + row(misc, 1))
    res_out[...] = (xhat * row(gains, 2) + row(shifts, 2)).astype(BF)
    g3, dgain3, dshift3 = norm_back(xhat, rstd, row(gains, 2), cot_ref[...].astype(F32))
    gb = g3.astype(BF)
    ops_out[:, :width] = h2b
    ops_out[:, width:] = gb

    def unit_grads(pre, dn):
        ga = nt(gb, dn).astype(BF).astype(F32)
        return (ga * (cdf(pre) + pre * density(pre))).astype(BF)

    tail = jnp.zeros((1, 2 * width - units), F32)
    gp = unit_grads(pre_own[...], down_own[...])
    bup_out[0] = jnp.concatenate([column_sum(gp), tail], axis=1)
    gh = g3 + nn(gp, up_own[...])
    blocks = list(near) + [(du_f, dd_f, core), (du_s, dd_s, 1 - core)]
    for p in range(3):
        sums = []
        for n in (2 * p, 2 * p + 1):
            up, dn, place = blocks[n]
            gp = unit_grads(pre_near[n] if n < 4 else pre_far[n - 4], part_of(dn, cut, place))
            sums.append(column_sum(gp))
            gh = gh + nn(gp, part_of(up, cut, place))
        low = jnp.where(core == 0, sums[0], sums[1])
        high = jnp.where(core == 0, sums[1], sums[0])
        bup_out[p + 1] = jnp.concatenate([low, high, tail], axis=1)
    g2, dgain2, dshift2 = norm_back(xhat2_ref[...], rstd2_ref[...], row(gains, 1), gh)
    g2_out[...] = g2
    small_out[0:1] = dgain3
    small_out[1:2] = dshift3
    small_out[2:3] = dgain2
    small_out[3:4] = dshift2
    small_out[4:5] = column_sum(gb)
    small_out[5:6] = column_sum(g2.astype(BF))
    small_out[6:8] = jnp.zeros((2, width), F32)


def backward_kernel(
    ids,
    g2_ref,
    pc_ref,
    k_ref,
    v_ref,
    cq_ref,
    ci_ref,
    cm_ref,
    xhat1_ref,
    rstd1_ref,
    x_ref,
    ai_ref,
    sq_ref,
    sk_ref,
    sv_ref,
    ps_ref,
    sm_ref,
    self_proj,
    self_out,
    cross_proj,
    cross_out,
    gains,
    ds_out,
    gcm_out,
    gx_out,
    gpos_out,
    small_out,
    keep,
    send0,
    send1,
    send2,
    send3,
    work,
    gq_ref,
    gk_ref,
    gv_ref,
):
    core = ids[1]
    send = Chain((send0, send1, send2, send3))
    width = x_ref.shape[1]
    rows = x_ref.shape[0]
    g2 = g2_ref[...]
    branch = g2.astype(BF)
    gcm_out[...] = nt(branch, cross_out[...]).astype(BF)
    padded = k_ref.shape[0] // GROUPS
    gcm = gcm_out[...]
    for g in range(GROUPS):
        lanes = slice(g * LANES, (g + 1) * LANES)
        grads = pair(gcm, g)
        total = row_totals(cm_ref[...], gcm, g)
        for j in range(GROUPS):
            here = slice(j * padded, (j + 1) * padded)
            dp = nt(v_ref[here, lanes], grads)
            ds_out[g, here] = (pc_ref[g, here].astype(F32) * (dp - total)).astype(BF)
        gq_ref[:, lanes] = unpair(tn(ds_out[g], k_ref[:, lanes])).astype(BF) * 0.125
    gcq = gq_ref[...]
    gci = nt(gcq, cross_proj[0])
    small_out[0:1] = column_sum(gcq)
    put_halves(core, tn(ci_ref[...], gcq), 0, keep, send, work)
    put_halves(core, tn(cm_ref[...], branch), 8, keep, send, work)
    g1, dgain1, dshift1 = norm_back(xhat1_ref[...], rstd1_ref[...], row(gains, 0), g2 + gci)
    small_out[1:2] = dgain1
    small_out[2:3] = dshift1
    sbranch = g1.astype(BF)
    small_out[3:4] = column_sum(sbranch)
    put_halves(core, tn(sm_ref[...], sbranch), 4, keep, send, work)
    gsm = nt(sbranch, self_out[...]).astype(BF)
    for g in range(GROUPS):
        lanes = slice(g * LANES, (g + 1) * LANES)
        grads = pair(gsm, g)
        p = ps_ref[g]
        dp = nt(sv_ref[:, lanes], grads)
        ds = (p.astype(F32) * (dp - row_totals(sm_ref[...], gsm, g))).astype(BF)
        gq_ref[:, lanes] = unpair(tn(ds, sk_ref[:, lanes])).astype(BF) * 0.125
        gk_ref[:, lanes] = nn(ds, pair(sq_ref[...], g)).astype(BF)
        gv_ref[:, lanes] = nn(p, grads).astype(BF)
    gq, gk, gv = gq_ref[...], gk_ref[...], gv_ref[...]
    gai = nt(gq, self_proj[0]) + nt(gk, self_proj[1])
    gx_out[...] = (g1 + gai + nt(gv, self_proj[2])).astype(BF)
    gpos_out[...] = gai + gci
    small_out[4:5] = column_sum(gq)
    small_out[5:6] = column_sum(gv)
    small_out[6:8] = jnp.zeros((2, width), F32)
    put_halves(core, tn(ai_ref[...], gq), 12, keep, send, work)
    put_halves(core, tn(ai_ref[...], gk), 16, keep, send, work)
    put_halves(core, tn(x_ref[...], gv), 20, keep, send, work)


def ffn_grad_kernel(ids, *refs):
    up_own, misc, down_own, keep, send0, send1, work = refs[4:]
    core = ids[1]
    units, width = up_own.shape
    ops = jnp.concatenate([ref[...] for ref in refs[:4]], axis=0)
    inputs, branch = ops[:, :width], ops[:, width:]
    bias = jnp.concatenate([row(misc, 2), row(misc, 3)[:, : units - width]], axis=1)
    pre = nt(inputs, up_own[...]) + bias
    phi = cdf(pre)
    act = (pre * phi).astype(BF)
    gact = nt(branch, down_own[...]).astype(BF).astype(F32)
    gpre = (gact * (phi + pre * density(pre))).astype(BF)
    blocks, size = keep.shape[1], keep.shape[2]
    for side, grad in enumerate((tn(inputs, gpre), tn(branch, act))):
        work[...] = grad
        for block in range(blocks):
            mine = pl.multiple_of((2 * block + core) * size, size)
            other = pl.multiple_of((2 * block + 1 - core) * size, size)
            keep[side, block] = work[pl.ds(mine, size), :].astype(BF)
            (send0, send1)[side][block] = work[pl.ds(other, size), :].astype(BF)


def ffn_fold_kernel(ids, keep, got0, got1, stay, go0, go1, *, bit):
    for side, (got, go) in enumerate(((got0, go0), (got1, go1))):
        for block in range(stay.shape[1]):
            mine, other = 2 * block + ids[bit], 2 * block + 1 - ids[bit]
            go[block] = plus(keep[side, other], got[other])
            stay[side, block] = plus(keep[side, mine], got[mine])


def ffn_finish_kernel(ids, keep, got0, got1, up_grad, down_grad):
    up_grad[...] = keep[0, 0].astype(F32) + got0[0].astype(F32)
    down_grad[...] = keep[1, 0].astype(F32) + got1[0].astype(F32)


def memory_back_kernel(
    ids,
    ds_ref,
    pc_ref,
    cq_ref,
    gcm_ref,
    featp,
    ki,
    vi,
    cross_proj,
    gpos_ref,
    small_a,
    small_b,
    bup,
    held,
    gm_ref,
    keep,
    send,
    gk_ref,
    gv_ref,
    work,
    small,
    *,
    rows_used,
):
    pb, core = ids[0], ids[1]
    width = featp.shape[1]
    rows = gpos_ref.shape[0]
    block = rows // GROUPS
    padded = featp.shape[0] // GROUPS
    pairs_q = [pair(cq_ref[...], g) for g in range(GROUPS)]
    pairs_g = [pair(gcm_ref[...], g) for g in range(GROUPS)]
    for j in range(GROUPS):
        here = slice(j * padded, (j + 1) * padded)
        for g in range(GROUPS):
            lanes = slice(g * LANES, (g + 1) * LANES)
            gk_ref[here, lanes] = nn(ds_ref[g, here], pairs_q[g]).astype(BF)
            gv_ref[here, lanes] = nn(pc_ref[g, here], pairs_g[g]).astype(BF)
        gm = (nt(gk_ref[here], cross_proj[1]) + nt(gv_ref[here], cross_proj[2])).astype(BF)
        gm_ref[here] = gm
    put_halves(core, tn(ki[...], gk_ref[...]), 0, keep, send, work)
    put_halves(core, tn(vi[...], gv_ref[...]), 4, keep, send, work)
    put_halves(core, tn(featp[...], gm_ref[...]), 8, keep, send, work)

    small[...] = gpos_ref[...]
    extras = [
        row(small_b, 1),
        row(small_a, 2),
        row(small_a, 0),
        row(small_b, 2),
        row(small_a, 3),
        row(small_a, 1),
        row(small_b, 4),
        row(small_b, 5),
        row(small_b, 3),
        row(small_b, 0),
        column_sum(gv_ref[...]),
        row(small_a, 5),
        row(small_a, 4),
        column_sum(gm_ref[...]),
    ]
    for index, value in enumerate(extras):
        at = spare_row(index, block, rows_used)
        small[at : at + 1] = value
    for b in range(GROUPS):
        at = b * block + rows_used + 5
        total = bup[b ^ pb]
        small[at : at + 1] = total[:, :width]
        small[at + 1 : at + 2] = total[:, width:]
    for b in range(2):
        for side, ref in ((core, keep), (1 - core, send)):
            low = small[:, b * LANES : (b + 1) * LANES]
            high = small[:, (2 + b) * LANES : (3 + b) * LANES]
            ref[12, b * rows : (b + 1) * rows] = jnp.where(side == 0, low, high).astype(BF)


def feature_grad_kernel(ids, gm_ref, in_proj, res_ref, gx_ref, rows0, rows1, rows2, rows3, gf_ref):
    pb = ids[0]
    padded = gf_ref.shape[1]
    block = res_ref.shape[0] // GROUPS
    for j in range(GROUPS):
        gf_ref[j] = nt(gm_ref[j * padded : (j + 1) * padded], in_proj[...]).astype(BF)
    for k, ref in enumerate((rows0, rows1, rows2, rows3)):
        at = pl.multiple_of((pb ^ k) * block, block)
        ref[0:padded] = gf_ref[pb ^ k]
        ref[padded : padded + block] = gx_ref[pl.ds(at, block), :]
        ref[padded + block : padded + 2 * block] = res_ref[pl.ds(at, block), :]


def spare_row(index, block, rows_used):
    return index // 5 * block + rows_used + index % 5


def write_rows(core, refs, places, work, sems):
    half = work.shape[1]
    rows = pl.ds(pl.multiple_of(core * half, half), half)
    copies = []
    for n, (ref, first, matrix) in enumerate(places):
        for b in range(4):
            work[n, :, b * LANES : (b + 1) * LANES] = refs[ref][first + b].astype(F32)
        copies.append(pltpu.make_async_copy(work.at[n], matrix.at[rows], sems.at[n]))
        copies[-1].start()
    return copies


def chain_places(cross, self_out, cross_out, self_proj):
    return [
        (0, 0, cross.at[0]),
        (0, 4, self_out),
        (0, 8, cross_out),
        (1, 0, self_proj.at[0]),
        (1, 4, self_proj.at[1]),
        (1, 8, self_proj.at[2]),
    ]


def chain_own_kernel(ids, va, vb, cross, self_out, cross_out, self_proj, work, sems):
    places = chain_places(cross, self_out, cross_out, self_proj)
    for copy in write_rows(ids[1], (va, vb), places, work, sems):
        copy.wait()


def chain_other_kernel(
    ids, ra, rb, in0, in1, in2, in3, cross, self_out, cross_out, self_proj, work, sems
):
    places = chain_places(cross, self_out, cross_out, self_proj)
    for copy in write_rows(1 - ids[1], (ra, rb), places, work, sems):
        copy.wait()


def memory_places(cross, in_):
    return [(0, 0, cross.at[1]), (0, 4, cross.at[2]), (0, 8, in_)]


def memory_own_kernel(ids, vc, cross_in, cross, in_, work, sems):
    for copy in write_rows(ids[1], (vc,), memory_places(cross, in_), work, sems):
        copy.wait()


def memory_other_kernel(
    ids,
    rc,
    vc,
    cross_in,
    in_in,
    pos_,
    self_bias_,
    cross_bias_,
    bup_,
    bdown_,
    gain_,
    shift_,
    inb_,
    cross,
    in_,
    work,
    sems,
    small,
    tiles,
    *,
    rows_used,
    units,
):
    core = ids[1]
    copies = write_rows(1 - core, (rc,), memory_places(cross, in_), work, sems)
    rows, width = small.shape
    block = rows // GROUPS
    for b in range(2):
        here = slice(b * rows, (b + 1) * rows)
        first = vc[12, here].astype(F32)
        second = rc[12, here].astype(F32)
        small[:, b * LANES : (b + 1) * LANES] = jnp.where(core == 0, first, second)
        small[:, (2 + b) * LANES : (3 + b) * LANES] = jnp.where(core == 0, second, first)
    lane = lax.broadcasted_iota(jnp.int32, (8, LANES), 1)
    tiles[...] = jnp.zeros(tiles.shape, F32)
    for b in range(GROUPS):
        pos_[b * rows_used : (b + 1) * rows_used] = small[b * block : b * block + rows_used]
        at = b * block + rows_used + 5
        first, shift = b * units // LANES, b * units % LANES
        both = [
            small[at + n : at + n + 1, m * LANES : (m + 1) * LANES]
            for n in range(2)
            for m in range(4)
        ]
        part = jnp.concatenate(both, axis=0)
        if shift:
            part = pltpu.roll(part, shift, 1)
        tiles[first : first + 8] += jnp.where(lane >= shift, part, 0.0)
        tiles[first + 1 : first + 9] += jnp.where(lane < shift, part, 0.0)
    bup_[...] = tiles[: bup_.shape[0]]

    def spare(index):
        at = spare_row(index, block, rows_used)
        return small[at : at + 1]

    for ref, index in ((gain_, 0), (shift_, 3), (self_bias_, 6), (cross_bias_, 9)):
        for i in range(3):
            ref[i : i + 1] = spare(index + i)
    bdown_[...] = spare(12)
    inb_[...] = spare(13)
    for copy in copies:
        copy.wait()


def hold_kernel(ids, got1, got2, got3, branch, out):
    out[...] = got1[:16, :LANES] + got2[:16, :LANES] + got3[:16, :LANES] + branch[:16, :LANES]


def order_kernel(ids, own, got1, got2, got3, out, grad, feats, *, block):
    pb = ids[0]
    part, used = feats.shape[1], out.shape[1]
    padded = own.shape[0] - 2 * block
    for k, ref in enumerate((own, got1, got2, got3)):
        feats[pb ^ k] = ref[0:part]
        grad[pb ^ k] = ref[padded : padded + used]
        out[pb ^ k] = ref[padded + block : padded + block + used]


class Far:
    def __init__(self, value, parts=None, emit=False):
        self.value, self.parts, self.emit = value, parts, emit


class Raw:
    def __init__(self, value):
        self.value = value


class Late:
    def __init__(self, ref, buffers, sems, parts):
        self.shape = ref.shape
        self.parts = parts
        self.buffers = buffers
        sources = [ref] if parts is None else [ref.at[part] for part in parts]
        self.copies = [
            pltpu.make_async_copy(source, buffer, sems.at[n])
            for n, (source, buffer) in enumerate(zip(sources, buffers))
        ]
        for copy in self.copies:
            copy.start()
        self.waiting = set(range(len(sources)))

    def ready(self, n):
        if n in self.waiting:
            self.waiting.discard(n)
            self.copies[n].wait()

    def __getitem__(self, index):
        if self.parts is None:
            self.ready(0)
            return self.buffers[0][index]
        n = self.parts.index(index)
        self.ready(n)
        return self.buffers[n][...]


class Places:
    def __getitem__(self, index):
        if index == 0:
            return lax.axis_index("pb")
        axis, bit = BITS[index - 1]
        return lax.rem(lax.div(lax.axis_index(axis), bit), 2)


CORE, X_WAY, Y_WAY = ("dp", 1), ("pb", 1), ("pb", 2)
BITS = [CORE, X_WAY, Y_WAY] + [("dp", 2 << n) for n in range(16)]


def place_of(way):
    return 1 + BITS.index(way)


class Order:
    def __init__(self):
        self.token = None

    def after(self, values):
        if self.token is None:
            return list(values)
        return list(lax.optimization_barrier((*values, self.token)))[:-1]


def call(
    order, kernel, args, outs, scratch=(), limit=16, near=True, micros=0.6, through=(), raw=(), alias=()
):
    through = order.after(through)
    bare = order.after([arg.value if isinstance(arg, (Far, Raw)) else arg for arg in args])
    args = [
        Far(value, arg.parts, arg.emit)
        if isinstance(arg, Far)
        else Raw(value)
        if isinstance(arg, Raw)
        else value
        for value, arg in zip(bare, args)
    ]
    specs, values, extra, emitted, plans = [], [], [], [], []
    outs, raw = list(outs), list(raw)
    for arg in args:
        if isinstance(arg, (Far, Raw)):
            value = arg.value
            specs.append(pl.BlockSpec(memory_space=pl.ANY))
            values.append(pltpu.with_memory_space_constraint(value, pltpu.HBM))
            if isinstance(arg, Raw):
                plans.append(None)
                continue
            count = 1 if arg.parts is None else len(arg.parts)
            if arg.emit:
                plans.append((None, len(emitted), len(extra), count, arg.parts))
                emitted.append((value.shape, value.dtype))
            else:
                plans.append((len(extra), None, len(extra) + count, count, arg.parts))
                shape = value.shape if arg.parts is None else value.shape[1:]
                extra += [pltpu.VMEM(shape, value.dtype)] * count
            extra.append(pltpu.SemaphoreType.DMA((count,)))
        elif jnp.issubdtype(arg.dtype, jnp.integer):
            specs.append(pl.BlockSpec(memory_space=pltpu.SMEM))
            values.append(arg)
            plans.append(None)
        else:
            specs.append(pl.BlockSpec(memory_space=pltpu.VMEM))
            values.append(pltpu.with_memory_space_constraint(arg, pltpu.VMEM))
            plans.append(None)

    def body(*refs):
        given, rest = list(refs[: len(args)]), refs[len(args) + len(through) :]
        first, rest = rest[: len(outs) + len(raw)], rest[len(outs) + len(raw) :]
        copies, rest = rest[: len(emitted)], rest[len(emitted) + len(through) :]
        own, late = rest[: len(scratch)], rest[len(scratch) :]
        waits = []
        for index, plan in enumerate(plans):
            if plan is None:
                continue
            at, place, sem, count, parts = plan
            if place is None:
                buffers = late[at : at + count]
            elif parts is None:
                buffers = [copies[place]]
            else:
                buffers = [copies[place].at[part] for part in parts]
            given[index] = Late(given[index], buffers, late[sem], parts)
            waits.append(given[index])
        kernel(Places(), *given, *first, *own)
        for one in waits:
            for n in sorted(one.waiting):
                one.ready(n)

    whole = [(o, near) for o in outs] + [(o, False) for o in raw] + [(o, True) for o in emitted]
    spaces = [pltpu.VMEM] * len(outs) + [pl.ANY] * len(raw) + [pltpu.VMEM] * len(emitted)
    result = pl.pallas_call(
        body,
        out_shape=[pltpu.VMEM(*o) if here else jax.ShapeDtypeStruct(*o) for o, here in whole]
        + [jax.ShapeDtypeStruct(value.shape, value.dtype) for value in through],
        in_specs=specs + [pl.BlockSpec(memory_space=pl.ANY)] * len(through),
        out_specs=[pl.BlockSpec(memory_space=space) for space in spaces]
        + [pl.BlockSpec(memory_space=pl.ANY)] * len(through),
        input_output_aliases={len(args) + n: len(whole) + n for n in range(len(through))} | dict(alias),
        scratch_shapes=list(scratch) + extra,
        compiler_params=pltpu.CompilerParams(vmem_limit_bytes=limit * 1024 * 1024),
        cost_estimate=pl.CostEstimate(
            flops=int(micros * RATE) + 1, bytes_accessed=int(micros * 3.7e6) + 1, transcendentals=0
        ),
    )(*values, *through)
    order.token = result[0]
    return result


def swap(value, axis, bit):
    size = lax.axis_size(axis)
    return lax.ppermute(value, axis, [(i, i ^ bit) for i in range(size)])


def bit_of(axis, bit):
    return (lax.axis_index(axis) // bit) % 2


def plus(left, right):
    return (left.astype(F32) + right.astype(F32)).astype(BF)


def bit_of(way):
    axis, bit = way
    return (lax.axis_index(axis) // bit) % 2


def halve(keep, got, bit):
    half = keep.shape[1] // 2
    total = plus(keep, got)
    mine = lax.dynamic_slice_in_dim(total, bit * half, half, 1)
    other = lax.dynamic_slice_in_dim(total, (1 - bit) * half, half, 1)
    return mine, other


def fold(order, groups, micros=0.6):
    rows = groups[0][0][0][0].shape[1] // 2
    if rows % 16:
        result = []
        for pieces, way in groups:
            done = [
                halve(keep[a:b], got[a - m : b - m], bit_of(way)) for keep, got, a, b, m in pieces
            ]
            result += [jnp.concatenate(side) for side in zip(*done)]
        return result
    args, outs = [], []
    for pieces, way in groups:
        count = sum(b - a for _, _, a, b, _ in pieces)
        outs += [((count, rows, LANES), BF)] * 2
        for keep, got, _, _, _ in pieces:
            args += [keep, got]

    def kernel(ids, *refs):
        given, made = list(refs[: len(args)]), list(refs[len(args) :])
        for pieces, way in groups:
            stay, go = made.pop(0), made.pop(0)
            bit = ids[place_of(way)]
            mine = pl.multiple_of(bit * rows, rows)
            other = pl.multiple_of((1 - bit) * rows, rows)
            at = 0
            for _, _, a, b, m in pieces:
                keep, got = given.pop(0), given.pop(0)
                for block in range(a, b):
                    for ref, start in ((go, other), (stay, mine)):
                        here = pl.ds(start, rows)
                        ref[at] = plus(keep[block, here], got[block - m, here])
                    at += 1

    return call(order, kernel, args, outs, limit=4, micros=micros)


def add_up(order, pieces, micros=0.6):
    if pieces[0][0].shape[1] % 16:
        return jnp.concatenate([plus(keep, got) for keep, got in pieces])

    def kernel(ids, *refs):
        at = 0
        for keep, got in zip(refs[0:-1:2], refs[1:-1:2]):
            refs[-1][at : at + keep.shape[0]] = plus(keep[...], got[...])
            at += keep.shape[0]

    count = sum(keep.shape[0] for keep, _ in pieces)
    shape = (count,) + pieces[0][0].shape[1:]
    args = [ref for piece in pieces for ref in piece]
    return call(order, kernel, args, [(shape, BF)], limit=4, micros=micros)[0]


def join(order, pieces, micros=0.6, through=()):
    if pieces[0][0].shape[1] % 16:
        result = []
        for value, got, way, cuts in pieces:
            full = jnp.where(
                bit_of(way) == 0, jnp.concatenate([value, got], 1), jnp.concatenate([got, value], 1)
            )
            result += [full[a:b] for a, b in cuts]
        return result + list(through)
    outs = []
    for value, _, _, cuts in pieces:
        outs += [((b - a, 2 * value.shape[1], LANES), BF) for a, b in cuts]

    def kernel(ids, *refs):
        given, made = list(refs[: 2 * len(pieces)]), list(refs[2 * len(pieces) :])
        for _, _, way, cuts in pieces:
            value, got = given.pop(0), given.pop(0)
            rows = value.shape[1]
            bit = ids[place_of(way)]
            mine = pl.multiple_of(bit * rows, rows)
            other = pl.multiple_of((1 - bit) * rows, rows)
            for a, b in cuts:
                out = made.pop(0)
                for block in range(a, b):
                    out[block - a, pl.ds(mine, rows)] = value[block]
                    out[block - a, pl.ds(other, rows)] = got[block]

    args = [ref for value, got, _, _ in pieces for ref in (value, got)]
    return call(order, kernel, args, outs, limit=4, micros=micros, through=through)


def on_device(
    tokens,
    query_pos,
    features,
    camera_mask,
    out_grad,
    self_proj,
    self_out,
    self_bias,
    cross_proj,
    cross_out,
    cross_bias,
    w_up,
    b_up,
    w_down,
    b_down,
    norm_gain,
    norm_bias,
    in_proj,
    in_bias,
):
    order = Order()
    pb_size = lax.axis_size("pb")
    dp_size = lax.axis_size("dp")
    ways = [("dp", 1 << i) for i in range(1, dp_size.bit_length() - 1)]
    width = tokens.shape[2]
    used = tokens.shape[1]
    block = -(-used // 16) * 16
    rows = block * pb_size
    mem = features.shape[1]
    part = mem // pb_size
    padded = -(-part // 16) * 16
    slots = padded * pb_size
    units = b_up.shape[0]

    up, down = w_up.T, w_down.T
    cut = units // 2
    up_half, down_half, up_wide, down_wide = call(
        order,
        pick_kernel,
        [Raw(up), Raw(down)],
        [((cut, width), BF)] * 2 + [((cut + 16, width), BF)] * 2,
        micros=1.4,
        scratch=[pltpu.SemaphoreType.DMA((8,))],
        limit=4,
    )
    fy0 = swap(up_half, *Y_WAY)
    fx1 = swap(down_half, *X_WAY)
    misc = (
        jnp.pad(in_bias[None], ((0, 3), (0, 0)))
        + jnp.pad(b_down[None], ((1, 2), (0, 0)))
        + jnp.pad(jnp.pad(b_up, (0, 2 * width - units)).reshape(2, width), ((2, 0), (0, 0)))
    )
    turn = lambda value: value.transpose(1, 0, 2)
    send = call(
        order,
        functools.partial(start_kernel, rows_used=used),
        [turn(tokens), turn(out_grad), misc],
        [((block, 2 * width), BF)] * 4,
        scratch=[
            pltpu.VMEM((used * pb_size, 2 * width), F32),
            pltpu.VMEM((rows, 2 * width), F32),
        ],
    )
    got = [send[0]] + [swap(send[k], "pb", k) for k in range(1, pb_size)]
    column = np.arange(width)
    rate = 1.0 / 10000.0 ** ((column // 2 * 2) / width)
    angle = np.arange(padded)[:, None] * rate
    start = np.arange(pb_size)[:, None] * part * rate
    even = column % 2 == 0
    waves = np.concatenate(
        [
            np.where(even, np.sin(start), np.cos(start)),
            np.where(even, np.cos(start), -np.sin(start)),
        ]
    )
    sines, cosines, waves = [
        jnp.asarray(value.astype(np.float32)) for value in (np.sin(angle), np.cos(angle), waves)
    ]

    wide = (slots, width)
    featp, ki, vi, ck, cv, in_proj, cross_proj = call(
        order,
        memory_kernel,
        [
            Raw(features),
            Far(sines),
            Far(cosines),
            Far(waves),
            Far(in_proj, emit=True),
            misc,
            Far(cross_proj, (1, 2, 0), emit=True),
            Far(cross_bias),
        ],
        [(wide, BF)] * 5,
        micros=START_COSTS[0],
        scratch=[pltpu.VMEM((mem, width), BF), pltpu.SemaphoreType.DMA],
    )
    fx1, fy0, up_wide, down_wide = order.after((fx1, fy0, up_wide, down_wide))
    fx0 = swap(up_wide, *X_WAY)
    fy1 = swap(down_wide, *Y_WAY)
    fx1, fy0, *got = order.after((fx1, fy0, *got))
    fd0 = swap(fy0, *X_WAY)
    fd1 = swap(fx1, *Y_WAY)
    sx1, sy0 = swap(fx1, *CORE), swap(fy0, *CORE)
    got[0], sx1, sy0 = lax.optimization_barrier((got[0], sx1, sy0))
    flat = (rows, width)
    scores = (GROUPS, slots, 2 * rows)
    (x, cot, ai, sq, sk, sv, ps, sm, xhat1, rstd1, ci, cq, pc, cm, h2, xhat2, rstd2, bups, h2b, self_proj, self_out, cross_out, norm_gain, norm_bias, up, down) = call(
        order,
        functools.partial(forward_kernel, rows_used=used),
        [
            camera_mask,
            *got,
            Far(query_pos),
            Far(self_proj, (0, 1, 2), emit=True),
            Far(self_out, emit=True),
            Far(self_bias),
            cross_proj,
            Far(cross_out, emit=True),
            Far(cross_bias),
            Far(norm_gain, emit=True),
            Far(norm_bias, emit=True),
            ck,
            cv,
            Far(up, emit=True),
            Far(down, emit=True),
        ],
        [
            (flat, BF),
            (flat, BF),
            (flat, BF),
            (flat, BF),
            (flat, BF),
            (flat, BF),
            ((GROUPS, rows, 2 * rows), BF),
            (flat, BF),
            (flat, F32),
            ((rows, 1), F32),
            (flat, BF),
            (flat, BF),
            (scores, BF),
            (flat, BF),
            (flat, F32),
            (flat, F32),
            ((rows, 1), F32),
            ((2 * pb_size, width), F32),
            (flat, BF),
        ],
        micros=START_COSTS[1],
        scratch=[pltpu.VMEM((slots, 2 * rows), F32), pltpu.VMEM(flat, F32)],
    )
    fd0, fd1 = order.after((fd0, fd1))
    sd0, sd1 = swap(fd0, *CORE), swap(fd1, *CORE)
    down_part, pre_own, pre_far = call(
        order,
        ffn_first_kernel,
        [h2b, bups, up, down, fd0, fd1, sd0, sd1],
        [(flat, F32), ((rows, units), F32), ((2, rows, cut), F32)],
        micros=START_COSTS[2],
    )
    fx0, fy1 = order.after((fx0, fy1))
    sx0, sy1 = swap(fx0, *CORE), swap(fy1, *CORE)
    pieces = [fx0, fx1, fy0, fy1, fd0, fd1, sx0, sx1, sy0, sy1, sd0, sd1]
    res, ops, g2, small_a, bup = call(
        order,
        ffn_second_kernel,
        [
            h2,
            h2b,
            cot,
            xhat2,
            rstd2,
            bups,
            up,
            down,
            down_part,
            pre_own,
            pre_far,
            misc,
            norm_gain,
            norm_bias,
            *pieces,
        ],
        [
            (flat, BF),
            ((rows, 2 * width), BF),
            (flat, F32),
            ((8, width), F32),
            ((pb_size, 1, 2 * width), F32),
        ],
        micros=START_COSTS[3],
        scratch=[pltpu.VMEM((4, rows, cut), F32)],
    )
    others = [swap(ops, "pb", k) for k in range(1, pb_size)]
    halves = ((24, width // 2, LANES), BF)
    ds, gcm, gx, gpos, small_b, keep12, *sends12 = call(
        order,
        backward_kernel,
        [
            g2,
            pc,
            ck,
            cv,
            cq,
            ci,
            cm,
            xhat1,
            rstd1,
            x,
            ai,
            sq,
            sk,
            sv,
            ps,
            sm,
            self_proj,
            self_out,
            cross_proj,
            cross_out,
            norm_gain,
        ],
        [
            (scores, BF),
            (flat, BF),
            (flat, BF),
            (flat, F32),
            ((8, width), F32),
            halves,
        ]
        + [((6, width // 2, LANES), BF)] * 4,
        micros=START_COSTS[4],
        scratch=[
            pltpu.VMEM((width, width), F32),
            pltpu.VMEM(flat, BF),
            pltpu.VMEM(flat, BF),
            pltpu.VMEM(flat, BF),
        ],
    )
    got12 = [swap(send, *CORE) for send in sends12]
    piece = width // dp_size
    (held,) = call(order, hold_kernel, [*others, gcm], [((16, LANES), BF)], limit=2, micros=START_COSTS[5])
    ka, sa, kb, sb = fold(
        order,
        [
            ([(keep12, got12[0], 0, 6, 0), (keep12, got12[1], 6, 12, 6)], X_WAY),
            ([(keep12, got12[2], 12, 18, 12), (keep12, got12[3], 18, 24, 18)], Y_WAY),
        ],
    )
    ra, rb = swap(sa, *X_WAY), swap(sb, *Y_WAY)

    def ffn_fold(keep, gots, micros):
        way = ways[(dp_size // 2).bit_length() - keep.shape[1].bit_length()]
        half = keep.shape[1] // 2
        keep, *sends = call(
            order,
            functools.partial(ffn_fold_kernel, bit=place_of(way)),
            [keep, *gots],
            [((2, half, piece, units), BF)] + [((half, piece, units), BF)] * 2,
            limit=4,
            micros=micros,
        )
        return keep, [swap(send, *way) for send in sends]

    halves3 = ((13, width // 2, LANES), BF)
    z_way, far_ways = ways[0], ways[1:]
    matrix = ((width, width), F32)
    three = ((3, width, width), F32)
    st = {"ra": ra, "rb": rb}

    def ffn_fold(micros):
        keep = st["fkeep"]
        way = ways[(dp_size // 2).bit_length() - keep.shape[1].bit_length()]
        half = keep.shape[1] // 2
        st["fkeep"], *sends = call(
            order,
            functools.partial(ffn_fold_kernel, bit=place_of(way)),
            [keep, *st["fgots"]],
            [((2, half, piece, units), BF)] + [((half, piece, units), BF)] * 2,
            limit=4,
            micros=micros,
        )
        st["fgots"] = [swap(send, *way) for send in sends]

    def memory(micros):
        st["gm"], st["keep3"], st["send3"] = call(
            order,
            functools.partial(memory_back_kernel, rows_used=used),
            [ds, pc, cq, gcm, featp, ki, vi, cross_proj, gpos, small_a, small_b, bup, held],
            [(wide, BF), halves3, halves3],
            micros=micros,
            scratch=[
                pltpu.VMEM(wide, BF),
                pltpu.VMEM(wide, BF),
                pltpu.VMEM((width, width), F32),
                pltpu.VMEM(flat, F32),
            ],
        )

    def ffn(micros):
        st["fkeep"], *sends = call(
            order,
            ffn_grad_kernel,
            [ops, *others, up, misc, down],
            [((2, dp_size // 2, piece, units), BF)] + [((dp_size // 2, piece, units), BF)] * 2,
            micros=micros,
            scratch=[pltpu.VMEM((width, units), F32)],
        )
        st["fgots"] = [swap(send, *CORE) for send in sends]

    def ffn_last(micros):
        st["ffn"] = call(
            order,
            ffn_finish_kernel,
            [st["fkeep"], *st["fgots"]],
            [((piece, units), F32)] * 2,
            near=False,
            micros=micros,
        )

    def features_step(micros):
        rows_out = call(
            order,
            feature_grad_kernel,
            [st["gm"], in_proj, res, gx],
            [((padded + 2 * block, width), BF)] * 4,
            micros=micros,
            scratch=[pltpu.VMEM((pb_size, padded, width), BF)],
        )
        st["arrived"] = [rows_out[0]] + [swap(rows_out[k], "pb", k) for k in range(1, pb_size)]

    def ab2(micros):
        ra, rb, send3 = order.after([st["ra"], st["rb"], st["send3"]])
        st["got3"] = swap(send3, *CORE)
        st["ka"], sa, st["kb"], sb = fold(
            order,
            [([(ka, ra, 0, 12, 0)], Y_WAY), ([(kb, rb, 0, 12, 0)], X_WAY)],
            micros,
        )
        st["ra"], st["rb"] = swap(sa, *Y_WAY), swap(sb, *X_WAY)

    def ab3(micros):
        st["kab"], send = fold(
            order, [([(st["ka"], st["ra"], 0, 12, 0), (st["kb"], st["rb"], 0, 12, 0)], z_way)], micros
        )
        st["rab"] = swap(send, *z_way)

    def exchange(name, keep, got, micros):
        total = add_up(order, [(keep, got)], micros)
        for way in far_ways[:-1]:
            total = add_up(order, [(total, swap(total, *way))], micros)
        st["v" + name] = total
        st["r" + name] = swap(total, *far_ways[-1])

    def ab4(micros):
        exchange("ab", st["kab"], st["rab"], micros)

    def ab5(micros):
        st["vab"] = add_up(order, [(st["vab"], st["rab"])], micros)
        st["rab"] = swap(st["vab"], *z_way)

    def ab6(micros):
        va, vb = join(order, [(st["vab"], st["rab"], z_way, [(0, 12), (12, 24)])], micros)
        st["va"], st["vb"] = va, vb
        st["ra"], st["rb"] = swap(va, *Y_WAY), swap(vb, *X_WAY)

    def ab7(micros):
        va, vb = join(
            order,
            [(st["va"], st["ra"], Y_WAY, [(0, 12)]), (st["vb"], st["rb"], X_WAY, [(0, 12)])],
            micros,
        )
        st["va"], st["vb"] = va, vb
        st["ra"], st["rb"] = swap(va, *X_WAY), swap(vb, *Y_WAY)

    def ab8(micros):
        va, vb, *st["exchanged"] = join(
            order,
            [(st["va"], st["ra"], X_WAY, [(0, 12)]), (st["vb"], st["rb"], Y_WAY, [(0, 12)])],
            micros,
            st["exchanged"],
        )
        st["va"], st["vb"] = va, vb
        st["ra"], st["rb"] = swap(va, *CORE), swap(vb, *CORE)

    def c_fold(way, first=False):
        def run(micros):
            keep, got = (st["keep3"], st["got3"]) if first else (st["kc"], st["rc"])
            st["kc"], send = fold(order, [([(keep, got, 0, 13, 0)], way)], micros)
            st["rc"] = swap(send, *way)

        return run

    def c4(micros):
        exchange("c", st["kc"], st["rc"], micros)

    def c5(micros):
        st["vc"] = add_up(order, [(st["vc"], st["rc"])], micros)
        st["rc"] = swap(st["vc"], *Y_WAY)

    def c_join(way, onward):
        def run(micros):
            (st["vc"],) = join(order, [(st["vc"], st["rc"], way, [(0, 13)])], micros)
            st["rc"] = swap(st["vc"], *onward)

        return run

    def order_rows(micros):
        exchanged = call(
            order,
            functools.partial(order_kernel, block=block),
            st["arrived"],
            [(tokens.shape, BF), (tokens.shape, BF), ((pb_size, part, width), BF)],
            micros=micros,
        )
        st["exchanged"] = [turn(value) for value in exchanged]

    half = width // 2
    six = [pltpu.VMEM((6, half, width), F32), pltpu.SemaphoreType.DMA((6,))]
    chain = [three, matrix, matrix, three]

    def own(micros):
        st["chain"] = call(
            order, chain_own_kernel, [st["va"], st["vb"]], [], raw=chain, scratch=six, micros=micros
        )

    def finish(micros):
        st["chain"] = call(
            order,
            chain_other_kernel,
            [st["ra"], st["rb"], *[Raw(value) for value in st["chain"]]],
            [],
            raw=chain,
            alias=[(2 + n, n) for n in range(4)],
            scratch=six,
            micros=micros,
        )

    def c_own(micros):
        cross, *rest = st["chain"]
        cross, st["in_proj"] = call(
            order,
            memory_own_kernel,
            [st["vc"], Raw(cross)],
            [],
            raw=[three, matrix],
            alias=[(1, 0)],
            scratch=[pltpu.VMEM((3, half, width), F32), pltpu.SemaphoreType.DMA((3,))],
            micros=micros,
        )
        st["chain"] = [cross, *rest]

    steps = {
        "memory": memory,
        "ffn": ffn,
        "ffn1": ffn_fold,
        "ffn2": lambda micros: [ffn_fold(micros) for _ in far_ways],
        "ffn3": ffn_last,
        "features": features_step,
        "ab2": ab2,
        "ab3": ab3,
        "ab4": ab4,
        "ab5": ab5,
        "ab6": ab6,
        "ab7": ab7,
        "ab8": ab8,
        "c1": c_fold(z_way, True),
        "c2": c_fold(X_WAY),
        "c3": c_fold(Y_WAY),
        "c4": c4,
        "c5": c5,
        "c6": c_join(Y_WAY, X_WAY),
        "c7": c_join(X_WAY, z_way),
        "c8": c_join(z_way, CORE),
        "order": order_rows,
        "finish": finish,
        "own": own,
        "c_own": c_own,
    }
    waits = {"ab5": ("rab",), "ab6": ("rab",), "ab7": ("ra",), "c5": ("rc",), "c6": ("rc",), "ab8": ("ra",)}
    for name, micros in STEPS:
        for at, rows_from in ((NEAR_AT, (1, 2)), (FAR_AT, (3,))):
            if name == at:
                key = waits[name][0]
                st[key], *rows_here = lax.optimization_barrier(
                    (st[key], *[st["arrived"][k] for k in rows_from])
                )
                for k, value in zip(rows_from, rows_here):
                    st["arrived"][k] = value
        steps[name](micros)
    ffn_up, ffn_down = st["ffn"]
    cross_grad, g_self_out, g_cross_out, g_self_proj = st["chain"]
    layer_out, grad_tokens, grad_features = [turn(value) for value in st["exchanged"]]
    bias3 = ((3, width), F32)
    bias1 = ((1, width), F32)
    (
        g_pos,
        g_self_bias,
        g_cross_bias,
        g_bup,
        g_bdown,
        g_gain,
        g_shift,
        g_inb,
        g_cross_proj,
        g_in_proj,
    ) = call(
        order,
        functools.partial(memory_other_kernel, rows_used=used, units=units),
        [st["rc"], st["vc"], Raw(cross_grad), Raw(st["in_proj"])],
        [
            (query_pos.shape, F32),
            bias3,
            bias3,
            ((-(-pb_size * units // LANES), LANES), F32),
            bias1,
            bias3,
            bias3,
            bias1,
        ],
        raw=[three, matrix],
        alias=[(2, 8), (3, 9)],
        scratch=[
            pltpu.VMEM((3, half, width), F32),
            pltpu.SemaphoreType.DMA((3,)),
            pltpu.VMEM(flat, F32),
            pltpu.VMEM((40, LANES), F32),
        ],
        near=False,
    )

    return (
        layer_out,
        grad_tokens,
        grad_features,
        g_pos,
        g_self_proj,
        g_self_out,
        g_self_bias,
        g_cross_proj,
        g_cross_out,
        g_cross_bias,
        ffn_up,
        g_bup.reshape(-1)[: pb_size * units],
        ffn_down,
        g_bdown[0],
        g_gain,
        g_shift,
        g_in_proj,
        g_inb[0],
    )


def solution(mesh):
    return jax.shard_map(
        on_device,
        mesh=mesh,
        in_specs=(
            P("dp", "pb", None),
            P(),
            P("dp", None, None),
            P("dp", None),
            P("dp", "pb", None),
            P(),
            P(),
            P(),
            P(),
            P(),
            P(),
            P(None, "pb"),
            P("pb"),
            P(None, "pb"),
            P(),
            P(),
            P(),
            P(),
            P(),
        ),
        out_specs=(
            P("dp", "pb", None),
            P("dp", "pb", None),
            P("dp", "pb", None),
            P(),
            P(),
            P(),
            P(),
            P(),
            P(),
            P(),
            P("dp", "pb"),
            P(),
            P("dp", "pb"),
            P(),
            P(),
            P(),
            P(),
            P(),
        ),
        check_vma=False,
    )
```

```python
import functools

import jax
import jax.numpy as jnp
import numpy as np
from jax import lax
from jax.experimental import pallas as pl
from jax.experimental.pallas import tpu as pltpu
from jax.sharding import PartitionSpec as P

BF = jnp.bfloat16
F32 = jnp.float32
HEADS = 8
LANES = 128
GROUPS = 4
FAR = -1e30
START_COSTS = (0.0, 8.0, 0.0, 6.0, 7.8, 6.2)
RATE = 1.15e9
STEPS = (
    ("memory", 5.0),
    ("ffn", 0.5),
    ("features", 0.3),
    ("ab2", 0.3),
    ("c1", 0.3),
    ("ab3", 2.7),
    ("ffn1", 0.0),
    ("c2", 0.3),
    ("ab4", 0.6),
    ("c3", 0.3),
    ("ffn2", 0.0),
    ("c4", 0.3),
    ("ab5", 0.3),
    ("c5", 1.2),
    ("ab6", 0.3),
    ("c6", 1.2),
    ("ab7", 0.5),
    ("c7", 2.4),
    ("order", 0.3),
    ("ffn3", 0.6),
    ("ab8", 0.6),
    ("own", 0.0),
    ("c8", 4.0),
    ("c_own", 0.0),
    ("finish", 1.5),
)
NEAR_AT, FAR_AT = "ab5", "ab6"


def dims(left, right, a, b):
    return lax.dot_general(left, right, (((a,), (b,)), ((), ())), preferred_element_type=F32)


def nn(left, right):
    return dims(left, right, 1, 0)


def nt(left, right):
    return dims(left, right, 1, 1)


def tn(left, right):
    return dims(left, right, 0, 0)


def lane_masks(dtype=BF):
    lane = lax.broadcasted_iota(jnp.int32, (1, LANES), 1)
    low = (lane < LANES // 2).astype(F32)
    return low.astype(dtype), (1.0 - low).astype(dtype)


def pair(value, group):
    part = value[:, group * LANES : (group + 1) * LANES]
    low, high = lane_masks()
    return jnp.concatenate([part * low, part * high], axis=0)


def unpair(value):
    rows = value.shape[0] // 2
    lane = lax.broadcasted_iota(jnp.int32, (rows, LANES), 1)
    return jnp.where(lane < LANES // 2, value[:rows], value[rows:])


def row_totals(mix, grad, group):
    lanes = slice(group * LANES, (group + 1) * LANES)
    product = (mix[:, lanes].astype(F32) * grad[:, lanes].astype(F32)).astype(BF)
    low, high = lane_masks()
    heads = jnp.concatenate([low, high, jnp.zeros((14, LANES), BF)], axis=0)
    sums = nt(heads, product)
    return jnp.concatenate([sums[0:1], sums[1:2]], axis=1)


def eights(value, op):
    return op(value.reshape(value.shape[0] // 8, 8, value.shape[1]), axis=0)


def norm(value):
    center = value - jnp.mean(value, -1, keepdims=True)
    rstd = lax.rsqrt(jnp.mean(center * center, -1, keepdims=True) + 1e-05)
    return center * rstd, rstd


def norm_back(xhat, rstd, gain, grad):
    scaled = grad * gain
    inner = jnp.mean(scaled, -1, keepdims=True) + xhat * jnp.mean(
        scaled * xhat, -1, keepdims=True
    )
    return (
        rstd * (scaled - inner),
        jnp.sum(grad * xhat, 0, keepdims=True),
        jnp.sum(grad, 0, keepdims=True),
    )


def column_sum(value):
    return jnp.sum(value.astype(F32), 0, keepdims=True)


def row(ref, index):
    return ref[index : index + 1, :].astype(F32)


def cdf(value):
    return 0.5 * (1.0 + lax.erf(value * np.float32(0.7071067811865476)))


def density(value):
    return jnp.exp(-0.5 * value * value) * np.float32(0.3989422804014327)


class Chain:
    def __init__(self, refs):
        self.refs = refs

    def __setitem__(self, index, value):
        size = self.refs[0].shape[0]
        self.refs[index // size][index % size] = value


def put_halves(core, left_ref, grad, index, keep_ref, send_ref):
    half = left_ref.shape[1] // 2
    for ref, place in ((send_ref, 1 - core), (keep_ref, core)):
        columns = pl.ds(pl.multiple_of(place * half, LANES), half)
        value = tn(left_ref[:, columns], grad).astype(BF)
        for block in range(value.shape[1] // LANES):
            ref[index + block] = value[:, block * LANES : (block + 1) * LANES]


def pick_kernel(ids, up, down, up_part, down_part, sems):
    core = ids[1]
    copies = []
    for ref, out in ((up, up_part), (down, down_part)):
        start = core * (ref.shape[0] - out.shape[0])
        size = out.shape[0] // 2
        for m in range(2):
            copies.append(
                pltpu.make_async_copy(
                    ref.at[pl.ds(pl.multiple_of(start + m * size, 16), size)],
                    out.at[pl.ds(m * size, size)],
                    sems.at[len(copies)],
                )
            )
    for copy in copies:
        copy.start()
    for copy in copies:
        copy.wait()


def start_kernel(
    ids, tokens, cots, misc, send0, send1, send2, send3, flat, turned, *, rows_used
):
    pb = ids[0]
    rows, width2 = turned.shape
    width = width2 // 2
    block = rows // GROUPS
    count = rows_used * GROUPS
    for q in range(rows_used):
        flat[q * GROUPS : (q + 1) * GROUPS, :width] = tokens[q].astype(F32)
        flat[q * GROUPS : (q + 1) * GROUPS, width:] = cots[q].astype(F32)
    place = lax.broadcasted_iota(jnp.int32, (rows, count), 0)
    query = lax.broadcasted_iota(jnp.int32, (rows, count), 1)
    hit = query == lax.rem(place, block) * GROUPS + lax.div(place, block)
    used = lax.rem(place, block) < rows_used
    chosen = jnp.where(jnp.logical_and(hit, used), 1.0, 0.0).astype(BF)
    turned[...] = nn(chosen, flat[...].astype(BF))
    for b in range(GROUPS):
        at = b * block + rows_used
        turned[at : at + 2, :width] = misc[2:4, :].astype(F32)
    for k, ref in enumerate((send0, send1, send2, send3)):
        at = pl.multiple_of((pb ^ k) * block, block)
        ref[...] = turned[pl.ds(at, block), :].astype(BF)


def memory_kernel(
    ids, feats, sines, cosines, waves, in_proj, misc, cross_proj, cross_bias, featp, ki, vi, k, v, buf, sems
):
    blocks = GROUPS
    slots = buf.shape[0]
    part = slots // blocks
    padded = featp.shape[0] // blocks
    copy = pltpu.make_async_copy(feats.at[ids[0]], buf, sems)
    copy.start()
    for j in range(blocks):
        featp[(j + 1) * padded - 16 : (j + 1) * padded] = jnp.zeros((16, featp.shape[1]), BF)
    copy.wait()
    bias = row(misc, 0)
    for j in range(blocks):
        here = slice(j * padded, (j + 1) * padded)
        featp[j * padded : j * padded + part] = buf[j * part : (j + 1) * part]
        memory = nn(featp[here], in_proj[...]) + bias
        places = cosines[...] * row(waves, j) + sines[...] * row(waves, blocks + j)
        key_input = (memory + places).astype(BF)
        value_input = memory.astype(BF)
        ki[here] = key_input
        vi[here] = value_input
        k[here] = nn(key_input, cross_proj[1]).astype(BF)
        v[here] = (nn(value_input, cross_proj[2]) + row(cross_bias, 1)).astype(BF)


def forward_kernel(
    ids,
    mask,
    own,
    got1,
    got2,
    got3,
    query_pos,
    self_proj,
    self_out,
    self_bias,
    cross_proj,
    cross_out,
    cross_bias,
    gains,
    shifts,
    k_ref,
    v_ref,
    up_,
    down_,
    x_out,
    cot_out,
    ai_out,
    sq_out,
    sk_out,
    sv_out,
    ps_out,
    sm_out,
    xhat1_out,
    rstd1_out,
    ci_out,
    cq_out,
    pc_out,
    cm_out,
    h2_out,
    xhat2_out,
    rstd2_out,
    bups_out,
    h2b_out,
    scores,
    pos_ref,
    *,
    rows_used,
):
    pb = ids[0]
    width = pos_ref.shape[1]
    block = own.shape[0]
    for k, ref in enumerate((own, got1, got2, got3)):
        at = pl.multiple_of((pb ^ k) * block, block)
        x_out[pl.ds(at, block), :] = ref[:, :width]
        cot_out[pl.ds(at, block), :] = ref[:, width:]
        bups_out[2 * k : 2 * k + 2] = ref[rows_used : rows_used + 2, :width].astype(F32)
    rows = x_out.shape[0]
    pos_ref[...] = jnp.zeros(pos_ref.shape, F32)
    for b in range(GROUPS):
        pos_ref[b * block : b * block + rows_used] = query_pos[
            b * rows_used : (b + 1) * rows_used
        ].astype(F32)
    pos = pos_ref[...]
    x = x_out[...].astype(F32)
    ai = (x + pos).astype(BF)
    ai_out[...] = ai
    sq_out[...] = ((nn(ai, self_proj[0]) + row(self_bias, 0)) * 0.125).astype(BF)
    sk_out[...] = nn(ai, self_proj[1]).astype(BF)
    sv_out[...] = (nn(x_out[...], self_proj[2]) + row(self_bias, 1)).astype(BF)
    key_row = lax.broadcasted_iota(jnp.int32, (rows, 2 * rows), 0)
    spare = jnp.where(lax.rem(key_row, block) < rows_used, 0.0, FAR).astype(F32)
    for g in range(GROUPS):
        lanes = slice(g * LANES, (g + 1) * LANES)
        s = nt(sk_out[:, lanes], pair(sq_out[...], g)) + spare
        e = jnp.exp(s - jnp.max(s, 0, keepdims=True))
        p = (e * (1.0 / jnp.sum(e, 0, keepdims=True))).astype(BF)
        ps_out[g] = p
        sm_out[:, lanes] = unpair(tn(p, sv_out[:, lanes])).astype(BF)
    xhat, rstd = norm(x + nn(sm_out[...], self_out[...]) + row(self_bias, 2))
    xhat1_out[...] = xhat
    rstd1_out[...] = rstd
    h1 = xhat * row(gains, 0) + row(shifts, 0)
    ci = (h1 + pos).astype(BF)
    ci_out[...] = ci
    cq_out[...] = ((nn(ci, cross_proj[0]) + row(cross_bias, 0)) * 0.125).astype(BF)

    padded = k_ref.shape[0] // GROUPS
    used = rows_used * 12
    slot_row = lax.broadcasted_iota(jnp.int32, (padded, 2 * rows), 0)
    for g in range(GROUPS):
        lanes = slice(g * LANES, (g + 1) * LANES)
        queries = pair(cq_out[...], g)
        top = jnp.full((8, 2 * rows), FAR, F32)
        for j in range(GROUPS):
            here = slice(j * padded, (j + 1) * padded)
            live = jnp.where(mask[pb, j] > 0, 0.0, -1000000000.0).astype(F32)
            s = nt(k_ref[here, lanes], queries) + jnp.where(slot_row < used, live, FAR)
            scores[here] = s
            top = jnp.maximum(top, eights(s, jnp.max))
        top = jnp.max(top, 0, keepdims=True)
        total = jnp.zeros((8, 2 * rows), F32)
        for j in range(GROUPS):
            here = slice(j * padded, (j + 1) * padded)
            e = jnp.exp(scores[here] - top)
            scores[here] = e
            total = total + eights(e, jnp.sum)
        inverse = 1.0 / jnp.sum(total, 0, keepdims=True)
        for j in range(GROUPS):
            here = slice(j * padded, (j + 1) * padded)
            pc_out[g, here] = (scores[here] * inverse).astype(BF)
        cm_out[:, lanes] = unpair(tn(pc_out[g], v_ref[:, lanes])).astype(BF)
    xhat, rstd = norm(h1 + nn(cm_out[...], cross_out[...]) + row(cross_bias, 2))
    xhat2_out[...] = xhat
    rstd2_out[...] = rstd
    h2 = xhat * row(gains, 1) + row(shifts, 1)
    h2_out[...] = h2
    h2b_out[...] = h2.astype(BF)


def part_of(ref, cut, core):
    spare = ref.shape[0] - cut
    return ref[pl.ds(pl.multiple_of(core * spare, 16), cut), :]


def bias_of(bups, p, units):
    width = bups.shape[1]
    return jnp.concatenate(
        [bups[2 * p : 2 * p + 1], bups[2 * p + 1 : 2 * p + 2, : units - width]], axis=1
    )


def bias_halves(bups, p, units, core):
    whole = bias_of(bups, p, units)
    low, high = whole[:, : units // 2], whole[:, units // 2 :]
    return jnp.where(core == 0, low, high), jnp.where(core == 0, high, low)


def ffn_first_kernel(
    ids, h2_ref, bups, up_own, down_own, up_f, down_f, up_s, down_s, down_out, pre_own, pre_far
):
    core = ids[1]
    h2 = h2_ref[...]
    units = up_own.shape[0]
    pre = nt(h2, up_own[...]) + bias_of(bups, 0, units)
    pre_own[...] = pre
    down = nn((pre * cdf(pre)).astype(BF), down_own[...])
    biases = bias_halves(bups, 3, units, core)
    for n, (up, dn) in enumerate(((up_f, down_f), (up_s, down_s))):
        pre = nt(h2, up[...]) + biases[n]
        pre_far[n] = pre
        down = down + nn((pre * cdf(pre)).astype(BF), dn[...])
    down_out[...] = down


def ffn_second_kernel(
    ids,
    h2_ref,
    h2b_ref,
    cot_ref,
    xhat2_ref,
    rstd2_ref,
    bups,
    up_own,
    down_own,
    down_ref,
    pre_own,
    pre_far,
    misc,
    gains,
    shifts,
    xu_f,
    xd_f,
    yu_f,
    yd_f,
    du_f,
    dd_f,
    xu_s,
    xd_s,
    yu_s,
    yd_s,
    du_s,
    dd_s,
    res_out,
    ops_out,
    g2_out,
    small_out,
    bup_out,
    pre_near,
    dense,
    *,
    rows_used,
):
    core = ids[1]
    units = up_own.shape[0]
    cut = units // 2
    width = h2_ref.shape[1]
    near = (
        (xu_f, xd_f, core),
        (xu_s, xd_s, 1 - core),
        (yu_f, yd_f, core),
        (yu_s, yd_s, 1 - core),
    )
    h2b = h2b_ref[...]
    down = down_ref[...]
    for n, (up, dn, place) in enumerate(near):
        pre = nt(h2b, part_of(up, cut, place)) + bias_halves(bups, n // 2 + 1, units, core)[n % 2]
        pre_near[n] = pre
        down = down + nn((pre * cdf(pre)).astype(BF), part_of(dn, cut, place))
    xhat, rstd = norm(h2_ref[...] + down + row(misc, 1))
    res_out[...] = (xhat * row(gains, 2) + row(shifts, 2)).astype(BF)
    g3, dgain3, dshift3 = norm_back(xhat, rstd, row(gains, 2), cot_ref[...].astype(F32))
    gb = g3.astype(BF)
    block = h2b.shape[0] // GROUPS
    dense[...] = jnp.zeros(dense.shape, F32)
    for b in range(GROUPS):
        here = slice(b * block, b * block + rows_used)
        there = slice(b * rows_used, (b + 1) * rows_used)
        dense[there, :width] = h2b[here].astype(F32)
        dense[there, width:] = gb[here].astype(F32)
    ops_out[...] = dense[...].astype(BF)

    def unit_grads(pre, dn):
        ga = nt(gb, dn).astype(BF).astype(F32)
        return (ga * (cdf(pre) + pre * density(pre))).astype(BF)

    tail = jnp.zeros((1, 2 * width - units), F32)
    gp = unit_grads(pre_own[...], down_own[...])
    bup_out[0] = jnp.concatenate([column_sum(gp), tail], axis=1)
    gh = g3 + nn(gp, up_own[...])
    blocks = list(near) + [(du_f, dd_f, core), (du_s, dd_s, 1 - core)]
    for p in range(3):
        sums = []
        for n in (2 * p, 2 * p + 1):
            up, dn, place = blocks[n]
            gp = unit_grads(pre_near[n] if n < 4 else pre_far[n - 4], part_of(dn, cut, place))
            sums.append(column_sum(gp))
            gh = gh + nn(gp, part_of(up, cut, place))
        low = jnp.where(core == 0, sums[0], sums[1])
        high = jnp.where(core == 0, sums[1], sums[0])
        bup_out[p + 1] = jnp.concatenate([low, high, tail], axis=1)
    g2, dgain2, dshift2 = norm_back(xhat2_ref[...], rstd2_ref[...], row(gains, 1), gh)
    g2_out[...] = g2
    small_out[0:1] = dgain3
    small_out[1:2] = dshift3
    small_out[2:3] = dgain2
    small_out[3:4] = dshift2
    small_out[4:5] = column_sum(gb)
    small_out[5:6] = column_sum(g2.astype(BF))
    small_out[6:8] = jnp.zeros((2, width), F32)


def backward_kernel(
    ids,
    g2_ref,
    pc_ref,
    k_ref,
    v_ref,
    cq_ref,
    ci_ref,
    cm_ref,
    xhat1_ref,
    rstd1_ref,
    x_ref,
    ai_ref,
    sq_ref,
    sk_ref,
    sv_ref,
    ps_ref,
    sm_ref,
    self_proj,
    self_out,
    cross_proj,
    cross_out,
    gains,
    ds_out,
    gcm_out,
    gx_out,
    gpos_out,
    small_out,
    keep,
    send0,
    send1,
    work,
    gq_ref,
    gk_ref,
    gv_ref,
):
    core = ids[1]
    send = Chain((send0, send1))
    width = x_ref.shape[1]
    rows = x_ref.shape[0]
    g2 = g2_ref[...]
    branch = g2.astype(BF)
    gcm_out[...] = nt(branch, cross_out[...]).astype(BF)
    padded = k_ref.shape[0] // GROUPS
    gcm = gcm_out[...]
    for g in range(GROUPS):
        lanes = slice(g * LANES, (g + 1) * LANES)
        grads = pair(gcm, g)
        total = row_totals(cm_ref[...], gcm, g)
        for j in range(GROUPS):
            here = slice(j * padded, (j + 1) * padded)
            dp = nt(v_ref[here, lanes], grads)
            ds_out[g, here] = (pc_ref[g, here].astype(F32) * (dp - total)).astype(BF)
        gq_ref[:, lanes] = unpair(tn(ds_out[g], k_ref[:, lanes])).astype(BF) * 0.125
    gcq = gq_ref[...]
    gci = nt(gcq, cross_proj[0])
    small_out[0:1] = column_sum(gcq)
    put_halves(core, ci_ref, gcq, 0, keep, send)
    put_halves(core, cm_ref, branch, 8, keep, send)
    g1, dgain1, dshift1 = norm_back(xhat1_ref[...], rstd1_ref[...], row(gains, 0), g2 + gci)
    small_out[1:2] = dgain1
    small_out[2:3] = dshift1
    sbranch = g1.astype(BF)
    small_out[3:4] = column_sum(sbranch)
    put_halves(core, sm_ref, sbranch, 4, keep, send)
    gsm = nt(sbranch, self_out[...]).astype(BF)
    for g in range(GROUPS):
        lanes = slice(g * LANES, (g + 1) * LANES)
        grads = pair(gsm, g)
        p = ps_ref[g]
        dp = nt(sv_ref[:, lanes], grads)
        ds = (p.astype(F32) * (dp - row_totals(sm_ref[...], gsm, g))).astype(BF)
        gq_ref[:, lanes] = unpair(tn(ds, sk_ref[:, lanes])).astype(BF) * 0.125
        gk_ref[:, lanes] = nn(ds, pair(sq_ref[...], g)).astype(BF)
        gv_ref[:, lanes] = nn(p, grads).astype(BF)
    gq, gk, gv = gq_ref[...], gk_ref[...], gv_ref[...]
    gai = nt(gq, self_proj[0]) + nt(gk, self_proj[1])
    gx_out[...] = (g1 + gai + nt(gv, self_proj[2])).astype(BF)
    gpos_out[...] = gai + gci
    small_out[4:5] = column_sum(gq)
    small_out[5:6] = column_sum(gv)
    small_out[6:8] = jnp.zeros((2, width), F32)
    put_halves(core, ai_ref, gq, 12, keep, send)
    put_halves(core, ai_ref, gk, 16, keep, send)
    put_halves(core, x_ref, gv, 20, keep, send)


def ffn_grad_kernel(ids, *refs):
    up_own, misc, down_own, keep, send0, send1, work = refs[4:]
    core = ids[1]
    units, width = up_own.shape
    ops = jnp.concatenate([ref[...] for ref in refs[:4]], axis=0)
    inputs, branch = ops[:, :width], ops[:, width:]
    bias = jnp.concatenate([row(misc, 2), row(misc, 3)[:, : units - width]], axis=1)
    pre = nt(inputs, up_own[...]) + bias
    phi = cdf(pre)
    act = (pre * phi).astype(BF)
    gact = nt(branch, down_own[...]).astype(BF).astype(F32)
    gpre = (gact * (phi + pre * density(pre))).astype(BF)
    blocks, size = keep.shape[1], keep.shape[2]
    for side, grad in enumerate((tn(inputs, gpre), tn(branch, act))):
        work[...] = grad
        for block in range(blocks):
            mine = pl.multiple_of((2 * block + core) * size, size)
            other = pl.multiple_of((2 * block + 1 - core) * size, size)
            keep[side, block] = work[pl.ds(mine, size), :].astype(BF)
            (send0, send1)[side][block] = work[pl.ds(other, size), :].astype(BF)


def ffn_fold_kernel(ids, keep, got0, got1, stay, go0, go1, *, bit):
    for side, (got, go) in enumerate(((got0, go0), (got1, go1))):
        for block in range(stay.shape[1]):
            mine, other = 2 * block + ids[bit], 2 * block + 1 - ids[bit]
            go[block] = plus(keep[side, other], got[other])
            stay[side, block] = plus(keep[side, mine], got[mine])


def ffn_finish_kernel(ids, keep, got0, got1, up_grad, down_grad):
    up_grad[...] = keep[0, 0].astype(F32) + got0[0].astype(F32)
    down_grad[...] = keep[1, 0].astype(F32) + got1[0].astype(F32)


def memory_back_kernel(
    ids,
    ds_ref,
    pc_ref,
    cq_ref,
    gcm_ref,
    featp,
    ki,
    vi,
    cross_proj,
    gpos_ref,
    small_a,
    small_b,
    bup,
    held,
    gm_ref,
    keep,
    send,
    gk_ref,
    gv_ref,
    work,
    small,
    *,
    rows_used,
):
    pb, core = ids[0], ids[1]
    width = featp.shape[1]
    rows = gpos_ref.shape[0]
    block = rows // GROUPS
    padded = featp.shape[0] // GROUPS
    pairs_q = [pair(cq_ref[...], g) for g in range(GROUPS)]
    pairs_g = [pair(gcm_ref[...], g) for g in range(GROUPS)]
    for j in range(GROUPS):
        here = slice(j * padded, (j + 1) * padded)
        for g in range(GROUPS):
            lanes = slice(g * LANES, (g + 1) * LANES)
            gk_ref[here, lanes] = nn(ds_ref[g, here], pairs_q[g]).astype(BF)
            gv_ref[here, lanes] = nn(pc_ref[g, here], pairs_g[g]).astype(BF)
        gm = (nt(gk_ref[here], cross_proj[1]) + nt(gv_ref[here], cross_proj[2])).astype(BF)
        gm_ref[here] = gm
    put_halves(core, ki, gk_ref[...], 0, keep, send)
    put_halves(core, vi, gv_ref[...], 4, keep, send)
    put_halves(core, featp, gm_ref[...], 8, keep, send)

    small[...] = gpos_ref[...]
    extras = [
        row(small_b, 1),
        row(small_a, 2),
        row(small_a, 0),
        row(small_b, 2),
        row(small_a, 3),
        row(small_a, 1),
        row(small_b, 4),
        row(small_b, 5),
        row(small_b, 3),
        row(small_b, 0),
        column_sum(gv_ref[...]),
        row(small_a, 5),
        row(small_a, 4),
        column_sum(gm_ref[...]),
    ]
    for index, value in enumerate(extras):
        at = spare_row(index, block, rows_used)
        small[at : at + 1] = value
    for b in range(GROUPS):
        at = b * block + rows_used + 5
        total = bup[b ^ pb]
        small[at : at + 1] = total[:, :width]
        small[at + 1 : at + 2] = total[:, width:]
    for b in range(2):
        for side, ref in ((core, keep), (1 - core, send)):
            low = small[:, b * LANES : (b + 1) * LANES]
            high = small[:, (2 + b) * LANES : (3 + b) * LANES]
            ref[12, b * rows : (b + 1) * rows] = jnp.where(side == 0, low, high).astype(BF)


def feature_grad_kernel(ids, gm_ref, in_proj, res_ref, gx_ref, rows0, rows1, rows2, rows3, gf_ref):
    pb = ids[0]
    padded = gf_ref.shape[1]
    block = res_ref.shape[0] // GROUPS
    for j in range(GROUPS):
        gf_ref[j] = nt(gm_ref[j * padded : (j + 1) * padded], in_proj[...]).astype(BF)
    for k, ref in enumerate((rows0, rows1, rows2, rows3)):
        at = pl.multiple_of((pb ^ k) * block, block)
        ref[0:padded] = gf_ref[pb ^ k]
        ref[padded : padded + block] = gx_ref[pl.ds(at, block), :]
        ref[padded + block : padded + 2 * block] = res_ref[pl.ds(at, block), :]


def spare_row(index, block, rows_used):
    return index // 5 * block + rows_used + index % 5


def write_rows(core, refs, places, work, sems):
    half = work.shape[1]
    rows = pl.ds(pl.multiple_of(core * half, half), half)
    copies = []
    for n, (ref, first, matrix) in enumerate(places):
        for b in range(4):
            work[n, :, b * LANES : (b + 1) * LANES] = refs[ref][first + b].astype(F32)
        copies.append(pltpu.make_async_copy(work.at[n], matrix.at[rows], sems.at[n]))
        copies[-1].start()
    return copies


def chain_places(cross, self_out, cross_out, self_proj):
    return [
        (0, 0, cross.at[0]),
        (0, 4, self_out),
        (0, 8, cross_out),
        (1, 0, self_proj.at[0]),
        (1, 4, self_proj.at[1]),
        (1, 8, self_proj.at[2]),
    ]


def chain_own_kernel(ids, va, vb, cross, self_out, cross_out, self_proj, work, sems):
    places = chain_places(cross, self_out, cross_out, self_proj)
    for copy in write_rows(ids[1], (va, vb), places, work, sems):
        copy.wait()


def chain_other_kernel(
    ids, ra, rb, in0, in1, in2, in3, cross, self_out, cross_out, self_proj, work, sems
):
    places = chain_places(cross, self_out, cross_out, self_proj)
    for copy in write_rows(1 - ids[1], (ra, rb), places, work, sems):
        copy.wait()


def memory_places(cross, in_):
    return [(0, 0, cross.at[1]), (0, 4, cross.at[2]), (0, 8, in_)]


def memory_own_kernel(ids, vc, cross_in, cross, in_, work, sems):
    for copy in write_rows(ids[1], (vc,), memory_places(cross, in_), work, sems):
        copy.wait()


def memory_other_kernel(
    ids,
    rc,
    vc,
    cross_in,
    in_in,
    pos_,
    self_bias_,
    cross_bias_,
    bup_,
    bdown_,
    gain_,
    shift_,
    inb_,
    cross,
    in_,
    work,
    sems,
    small,
    tiles,
    *,
    rows_used,
    units,
):
    core = ids[1]
    copies = write_rows(1 - core, (rc,), memory_places(cross, in_), work, sems)
    rows, width = small.shape
    block = rows // GROUPS
    for b in range(2):
        here = slice(b * rows, (b + 1) * rows)
        first = vc[12, here].astype(F32)
        second = rc[12, here].astype(F32)
        small[:, b * LANES : (b + 1) * LANES] = jnp.where(core == 0, first, second)
        small[:, (2 + b) * LANES : (3 + b) * LANES] = jnp.where(core == 0, second, first)
    lane = lax.broadcasted_iota(jnp.int32, (8, LANES), 1)
    tiles[...] = jnp.zeros(tiles.shape, F32)
    for b in range(GROUPS):
        pos_[b * rows_used : (b + 1) * rows_used] = small[b * block : b * block + rows_used]
        at = b * block + rows_used + 5
        first, shift = b * units // LANES, b * units % LANES
        both = [
            small[at + n : at + n + 1, m * LANES : (m + 1) * LANES]
            for n in range(2)
            for m in range(4)
        ]
        part = jnp.concatenate(both, axis=0)
        if shift:
            part = pltpu.roll(part, shift, 1)
        tiles[first : first + 8] += jnp.where(lane >= shift, part, 0.0)
        tiles[first + 1 : first + 9] += jnp.where(lane < shift, part, 0.0)
    bup_[...] = tiles[: bup_.shape[0]]

    def spare(index):
        at = spare_row(index, block, rows_used)
        return small[at : at + 1]

    for ref, index in ((gain_, 0), (shift_, 3), (self_bias_, 6), (cross_bias_, 9)):
        for i in range(3):
            ref[i : i + 1] = spare(index + i)
    bdown_[...] = spare(12)
    inb_[...] = spare(13)
    for copy in copies:
        copy.wait()


def hold_kernel(ids, got1, got2, got3, branch, out):
    out[...] = got1[:16, :LANES] + got2[:16, :LANES] + got3[:16, :LANES] + branch[:16, :LANES]


def order_kernel(ids, own, got1, got2, got3, out, grad, feats, *, block):
    pb = ids[0]
    part, used = feats.shape[1], out.shape[1]
    padded = own.shape[0] - 2 * block
    for k, ref in enumerate((own, got1, got2, got3)):
        feats[pb ^ k] = ref[0:part]
        grad[pb ^ k] = ref[padded : padded + used]
        out[pb ^ k] = ref[padded + block : padded + block + used]


class Far:
    def __init__(self, value, parts=None, emit=False):
        self.value, self.parts, self.emit = value, parts, emit


class Raw:
    def __init__(self, value):
        self.value = value


class Late:
    def __init__(self, ref, buffers, sems, parts):
        self.shape = ref.shape
        self.parts = parts
        self.buffers = buffers
        sources = [ref] if parts is None else [ref.at[part] for part in parts]
        self.copies = [
            pltpu.make_async_copy(source, buffer, sems.at[n])
            for n, (source, buffer) in enumerate(zip(sources, buffers))
        ]
        for copy in self.copies:
            copy.start()
        self.waiting = set(range(len(sources)))

    def ready(self, n):
        if n in self.waiting:
            self.waiting.discard(n)
            self.copies[n].wait()

    def __getitem__(self, index):
        if self.parts is None:
            self.ready(0)
            return self.buffers[0][index]
        n = self.parts.index(index)
        self.ready(n)
        return self.buffers[n][...]


class Places:
    def __getitem__(self, index):
        if index == 0:
            return lax.axis_index("pb")
        axis, bit = BITS[index - 1]
        return lax.rem(lax.div(lax.axis_index(axis), bit), 2)


CORE, X_WAY, Y_WAY = ("dp", 1), ("pb", 1), ("pb", 2)
BITS = [CORE, X_WAY, Y_WAY] + [("dp", 2 << n) for n in range(16)]


def place_of(way):
    return 1 + BITS.index(way)


class Order:
    def __init__(self):
        self.token = None

    def after(self, values):
        if self.token is None:
            return list(values)
        return list(lax.optimization_barrier((*values, self.token)))[:-1]


def call(
    order, kernel, args, outs, scratch=(), limit=16, near=True, micros=0.6, through=(), raw=(), alias=()
):
    through = order.after(through)
    bare = order.after([arg.value if isinstance(arg, (Far, Raw)) else arg for arg in args])
    args = [
        Far(value, arg.parts, arg.emit)
        if isinstance(arg, Far)
        else Raw(value)
        if isinstance(arg, Raw)
        else value
        for value, arg in zip(bare, args)
    ]
    specs, values, extra, emitted, plans = [], [], [], [], []
    outs, raw = list(outs), list(raw)
    for arg in args:
        if isinstance(arg, (Far, Raw)):
            value = arg.value
            specs.append(pl.BlockSpec(memory_space=pl.ANY))
            values.append(pltpu.with_memory_space_constraint(value, pltpu.HBM))
            if isinstance(arg, Raw):
                plans.append(None)
                continue
            count = 1 if arg.parts is None else len(arg.parts)
            if arg.emit:
                plans.append((None, len(emitted), len(extra), count, arg.parts))
                emitted.append((value.shape, value.dtype))
            else:
                plans.append((len(extra), None, len(extra) + count, count, arg.parts))
                shape = value.shape if arg.parts is None else value.shape[1:]
                extra += [pltpu.VMEM(shape, value.dtype)] * count
            extra.append(pltpu.SemaphoreType.DMA((count,)))
        elif jnp.issubdtype(arg.dtype, jnp.integer):
            specs.append(pl.BlockSpec(memory_space=pltpu.SMEM))
            values.append(arg)
            plans.append(None)
        else:
            specs.append(pl.BlockSpec(memory_space=pltpu.VMEM))
            values.append(pltpu.with_memory_space_constraint(arg, pltpu.VMEM))
            plans.append(None)

    def body(*refs):
        given, rest = list(refs[: len(args)]), refs[len(args) + len(through) :]
        first, rest = rest[: len(outs) + len(raw)], rest[len(outs) + len(raw) :]
        copies, rest = rest[: len(emitted)], rest[len(emitted) + len(through) :]
        own, late = rest[: len(scratch)], rest[len(scratch) :]
        waits = []
        for index, plan in enumerate(plans):
            if plan is None:
                continue
            at, place, sem, count, parts = plan
            if place is None:
                buffers = late[at : at + count]
            elif parts is None:
                buffers = [copies[place]]
            else:
                buffers = [copies[place].at[part] for part in parts]
            given[index] = Late(given[index], buffers, late[sem], parts)
            waits.append(given[index])
        kernel(Places(), *given, *first, *own)
        for one in waits:
            for n in sorted(one.waiting):
                one.ready(n)

    whole = [(o, near) for o in outs] + [(o, False) for o in raw] + [(o, True) for o in emitted]
    spaces = [pltpu.VMEM] * len(outs) + [pl.ANY] * len(raw) + [pltpu.VMEM] * len(emitted)
    result = pl.pallas_call(
        body,
        out_shape=[pltpu.VMEM(*o) if here else jax.ShapeDtypeStruct(*o) for o, here in whole]
        + [jax.ShapeDtypeStruct(value.shape, value.dtype) for value in through],
        in_specs=specs + [pl.BlockSpec(memory_space=pl.ANY)] * len(through),
        out_specs=[pl.BlockSpec(memory_space=space) for space in spaces]
        + [pl.BlockSpec(memory_space=pl.ANY)] * len(through),
        input_output_aliases={len(args) + n: len(whole) + n for n in range(len(through))} | dict(alias),
        scratch_shapes=list(scratch) + extra,
        compiler_params=pltpu.CompilerParams(vmem_limit_bytes=limit * 1024 * 1024),
        cost_estimate=pl.CostEstimate(
            flops=int(micros * RATE) + 1, bytes_accessed=int(micros * 3.7e6) + 1, transcendentals=0
        ),
    )(*values, *through)
    order.token = result[0]
    return result


def swap(value, axis, bit):
    size = lax.axis_size(axis)
    return lax.ppermute(value, axis, [(i, i ^ bit) for i in range(size)])


def bit_of(axis, bit):
    return (lax.axis_index(axis) // bit) % 2


def plus(left, right):
    return (left.astype(F32) + right.astype(F32)).astype(BF)


def bit_of(way):
    axis, bit = way
    return (lax.axis_index(axis) // bit) % 2


def halve(keep, got, bit):
    half = keep.shape[1] // 2
    total = plus(keep, got)
    mine = lax.dynamic_slice_in_dim(total, bit * half, half, 1)
    other = lax.dynamic_slice_in_dim(total, (1 - bit) * half, half, 1)
    return mine, other


def fold(order, groups, micros=0.6):
    rows = groups[0][0][0][0].shape[1] // 2
    if rows % 16:
        result = []
        for pieces, way in groups:
            done = [
                halve(keep[a:b], got[a - m : b - m], bit_of(way)) for keep, got, a, b, m in pieces
            ]
            result += [jnp.concatenate(side) for side in zip(*done)]
        return result
    args, outs = [], []
    for pieces, way in groups:
        count = sum(b - a for _, _, a, b, _ in pieces)
        outs += [((count, rows, LANES), BF)] * 2
        for keep, got, _, _, _ in pieces:
            args += [keep, got]

    def kernel(ids, *refs):
        given, made = list(refs[: len(args)]), list(refs[len(args) :])
        for pieces, way in groups:
            stay, go = made.pop(0), made.pop(0)
            bit = ids[place_of(way)]
            mine = pl.multiple_of(bit * rows, rows)
            other = pl.multiple_of((1 - bit) * rows, rows)
            at = 0
            for _, _, a, b, m in pieces:
                keep, got = given.pop(0), given.pop(0)
                for block in range(a, b):
                    for ref, start in ((go, other), (stay, mine)):
                        here = pl.ds(start, rows)
                        ref[at] = plus(keep[block, here], got[block - m, here])
                    at += 1

    return call(order, kernel, args, outs, limit=4, micros=micros)


def add_up(order, pieces, micros=0.6):
    if pieces[0][0].shape[1] % 16:
        return jnp.concatenate([plus(keep, got) for keep, got in pieces])

    def kernel(ids, *refs):
        at = 0
        for keep, got in zip(refs[0:-1:2], refs[1:-1:2]):
            refs[-1][at : at + keep.shape[0]] = plus(keep[...], got[...])
            at += keep.shape[0]

    count = sum(keep.shape[0] for keep, _ in pieces)
    shape = (count,) + pieces[0][0].shape[1:]
    args = [ref for piece in pieces for ref in piece]
    return call(order, kernel, args, [(shape, BF)], limit=4, micros=micros)[0]


def join(order, pieces, micros=0.6, through=()):
    if pieces[0][0].shape[1] % 16:
        result = []
        for value, got, way, cuts in pieces:
            full = jnp.where(
                bit_of(way) == 0, jnp.concatenate([value, got], 1), jnp.concatenate([got, value], 1)
            )
            result += [full[a:b] for a, b in cuts]
        return result + list(through)
    outs = []
    for value, _, _, cuts in pieces:
        outs += [((b - a, 2 * value.shape[1], LANES), BF) for a, b in cuts]

    def kernel(ids, *refs):
        given, made = list(refs[: 2 * len(pieces)]), list(refs[2 * len(pieces) :])
        for _, _, way, cuts in pieces:
            value, got = given.pop(0), given.pop(0)
            rows = value.shape[1]
            bit = ids[place_of(way)]
            mine = pl.multiple_of(bit * rows, rows)
            other = pl.multiple_of((1 - bit) * rows, rows)
            for a, b in cuts:
                out = made.pop(0)
                for block in range(a, b):
                    out[block - a, pl.ds(mine, rows)] = value[block]
                    out[block - a, pl.ds(other, rows)] = got[block]

    args = [ref for value, got, _, _ in pieces for ref in (value, got)]
    return call(order, kernel, args, outs, limit=4, micros=micros, through=through)


def on_device(
    tokens,
    query_pos,
    features,
    camera_mask,
    out_grad,
    self_proj,
    self_out,
    self_bias,
    cross_proj,
    cross_out,
    cross_bias,
    w_up,
    b_up,
    w_down,
    b_down,
    norm_gain,
    norm_bias,
    in_proj,
    in_bias,
):
    order = Order()
    pb_size = lax.axis_size("pb")
    dp_size = lax.axis_size("dp")
    ways = [("dp", 1 << i) for i in range(1, dp_size.bit_length() - 1)]
    width = tokens.shape[2]
    used = tokens.shape[1]
    block = -(-used // 16) * 16
    rows = block * pb_size
    mem = features.shape[1]
    part = mem // pb_size
    padded = -(-part // 16) * 16
    slots = padded * pb_size
    units = b_up.shape[0]

    up, down = w_up.T, w_down.T
    cut = units // 2
    def pick(count):
        return call(
            order,
            pick_kernel,
            [Raw(up), Raw(down)],
            [((count, width), BF)] * 2,
            scratch=[pltpu.SemaphoreType.DMA((4,))],
            limit=4,
            micros=0.0,
        )

    up_half, down_half = pick(cut)
    fy0 = swap(up_half, *Y_WAY)
    fx1 = swap(down_half, *X_WAY)
    up_wide, down_wide = pick(cut + 16)
    misc = (
        jnp.pad(in_bias[None], ((0, 3), (0, 0)))
        + jnp.pad(b_down[None], ((1, 2), (0, 0)))
        + jnp.pad(jnp.pad(b_up, (0, 2 * width - units)).reshape(2, width), ((2, 0), (0, 0)))
    )
    turn = lambda value: value.transpose(1, 0, 2)
    send = call(
        order,
        functools.partial(start_kernel, rows_used=used),
        [turn(tokens), turn(out_grad), misc],
        [((block, 2 * width), BF)] * 4,
        scratch=[
            pltpu.VMEM((used * pb_size, 2 * width), F32),
            pltpu.VMEM((rows, 2 * width), F32),
        ],
    )
    got = [send[0]] + [swap(send[k], "pb", k) for k in range(1, pb_size)]
    column = np.arange(width)
    rate = 1.0 / 10000.0 ** ((column // 2 * 2) / width)
    angle = np.arange(padded)[:, None] * rate
    start = np.arange(pb_size)[:, None] * part * rate
    even = column % 2 == 0
    waves = np.concatenate(
        [
            np.where(even, np.sin(start), np.cos(start)),
            np.where(even, np.cos(start), -np.sin(start)),
        ]
    )
    sines, cosines, waves = [
        jnp.asarray(value.astype(np.float32)) for value in (np.sin(angle), np.cos(angle), waves)
    ]

    wide = (slots, width)
    featp, ki, vi, ck, cv, in_proj, cross_proj = call(
        order,
        memory_kernel,
        [
            Raw(features),
            Far(sines),
            Far(cosines),
            Far(waves),
            Far(in_proj, emit=True),
            misc,
            Far(cross_proj, (1, 2, 0), emit=True),
            Far(cross_bias),
        ],
        [(wide, BF)] * 5,
        micros=START_COSTS[0],
        scratch=[pltpu.VMEM((mem, width), BF), pltpu.SemaphoreType.DMA],
    )
    fx1, fy0, up_wide, down_wide = order.after((fx1, fy0, up_wide, down_wide))
    fx0 = swap(up_wide, *X_WAY)
    fy1 = swap(down_wide, *Y_WAY)
    fx1, fy0, *got = order.after((fx1, fy0, *got))
    fd0 = swap(fy0, *X_WAY)
    fd1 = swap(fx1, *Y_WAY)
    flat = (rows, width)
    scores = (GROUPS, slots, 2 * rows)
    (x, cot, ai, sq, sk, sv, ps, sm, xhat1, rstd1, ci, cq, pc, cm, h2, xhat2, rstd2, bups, h2b, self_proj, self_out, cross_out, norm_gain, norm_bias, up, down) = call(
        order,
        functools.partial(forward_kernel, rows_used=used),
        [
            camera_mask,
            *got,
            Far(query_pos),
            Far(self_proj, (0, 1, 2), emit=True),
            Far(self_out, emit=True),
            Far(self_bias),
            cross_proj,
            Far(cross_out, emit=True),
            Far(cross_bias),
            Far(norm_gain, emit=True),
            Far(norm_bias, emit=True),
            ck,
            cv,
            Far(up, emit=True),
            Far(down, emit=True),
        ],
        [
            (flat, BF),
            (flat, BF),
            (flat, BF),
            (flat, BF),
            (flat, BF),
            (flat, BF),
            ((GROUPS, rows, 2 * rows), BF),
            (flat, BF),
            (flat, F32),
            ((rows, 1), F32),
            (flat, BF),
            (flat, BF),
            (scores, BF),
            (flat, BF),
            (flat, F32),
            (flat, F32),
            ((rows, 1), F32),
            ((2 * pb_size, width), F32),
            (flat, BF),
        ],
        micros=START_COSTS[1],
        scratch=[pltpu.VMEM((slots, 2 * rows), F32), pltpu.VMEM(flat, F32)],
    )
    fx1, fy0, fd0, fd1 = order.after((fx1, fy0, fd0, fd1))
    sx1, sy0 = swap(fx1, *CORE), swap(fy0, *CORE)
    sd0, sd1 = swap(fd0, *CORE), swap(fd1, *CORE)
    down_part, pre_own, pre_far = call(
        order,
        ffn_first_kernel,
        [h2b, bups, up, down, fd0, fd1, sd0, sd1],
        [(flat, F32), ((rows, units), F32), ((2, rows, cut), F32)],
        micros=START_COSTS[2],
    )
    fx0, fy1 = order.after((fx0, fy1))
    sx0, sy1 = swap(fx0, *CORE), swap(fy1, *CORE)
    pieces = [fx0, fx1, fy0, fy1, fd0, fd1, sx0, sx1, sy0, sy1, sd0, sd1]
    dense = (-(-used * pb_size // 8) * 8, 2 * width)
    res, ops, g2, small_a, bup = call(
        order,
        functools.partial(ffn_second_kernel, rows_used=used),
        [
            h2,
            h2b,
            cot,
            xhat2,
            rstd2,
            bups,
            up,
            down,
            down_part,
            pre_own,
            pre_far,
            misc,
            norm_gain,
            norm_bias,
            *pieces,
        ],
        [
            (flat, BF),
            (dense, BF),
            (flat, F32),
            ((8, width), F32),
            ((pb_size, 1, 2 * width), F32),
        ],
        micros=START_COSTS[3],
        scratch=[pltpu.VMEM((4, rows, cut), F32), pltpu.VMEM(dense, F32)],
    )
    others = [swap(ops, "pb", k) for k in range(1, pb_size)]
    halves = ((24, width // 2, LANES), BF)
    ds, gcm, gx, gpos, small_b, keep12, *sends12 = call(
        order,
        backward_kernel,
        [
            g2,
            pc,
            ck,
            cv,
            cq,
            ci,
            cm,
            xhat1,
            rstd1,
            x,
            ai,
            sq,
            sk,
            sv,
            ps,
            sm,
            self_proj,
            self_out,
            cross_proj,
            cross_out,
            norm_gain,
        ],
        [
            (scores, BF),
            (flat, BF),
            (flat, BF),
            (flat, F32),
            ((8, width), F32),
            halves,
        ]
        + [((12, width // 2, LANES), BF)] * 2,
        micros=START_COSTS[4],
        scratch=[
            pltpu.VMEM((width, width), F32),
            pltpu.VMEM(flat, BF),
            pltpu.VMEM(flat, BF),
            pltpu.VMEM(flat, BF),
        ],
    )
    got12 = [swap(send, *CORE) for send in sends12]
    piece = width // dp_size
    (held,) = call(order, hold_kernel, [*others, gcm], [((16, LANES), BF)], limit=2, micros=START_COSTS[5])
    ka, sa, kb, sb = fold(
        order,
        [
            ([(keep12, got12[0], 0, 12, 0)], X_WAY),
            ([(keep12, got12[1], 12, 24, 12)], Y_WAY),
        ],
    )
    ra, rb = swap(sa, *X_WAY), swap(sb, *Y_WAY)

    def ffn_fold(keep, gots, micros):
        way = ways[(dp_size // 2).bit_length() - keep.shape[1].bit_length()]
        half = keep.shape[1] // 2
        keep, *sends = call(
            order,
            functools.partial(ffn_fold_kernel, bit=place_of(way)),
            [keep, *gots],
            [((2, half, piece, units), BF)] + [((half, piece, units), BF)] * 2,
            limit=4,
            micros=micros,
        )
        return keep, [swap(send, *way) for send in sends]

    halves3 = ((13, width // 2, LANES), BF)
    z_way, far_ways = ways[0], ways[1:]
    matrix = ((width, width), F32)
    three = ((3, width, width), F32)
    st = {"ra": ra, "rb": rb}

    def ffn_fold(micros):
        keep = st["fkeep"]
        way = ways[(dp_size // 2).bit_length() - keep.shape[1].bit_length()]
        half = keep.shape[1] // 2
        st["fkeep"], *sends = call(
            order,
            functools.partial(ffn_fold_kernel, bit=place_of(way)),
            [keep, *st["fgots"]],
            [((2, half, piece, units), BF)] + [((half, piece, units), BF)] * 2,
            limit=4,
            micros=micros,
        )
        st["fgots"] = [swap(send, *way) for send in sends]

    def memory(micros):
        st["gm"], st["keep3"], st["send3"] = call(
            order,
            functools.partial(memory_back_kernel, rows_used=used),
            [ds, pc, cq, gcm, featp, ki, vi, cross_proj, gpos, small_a, small_b, bup, held],
            [(wide, BF), halves3, halves3],
            micros=micros,
            scratch=[
                pltpu.VMEM(wide, BF),
                pltpu.VMEM(wide, BF),
                pltpu.VMEM((width, width), F32),
                pltpu.VMEM(flat, F32),
            ],
        )

    def ffn(micros):
        st["fkeep"], *sends = call(
            order,
            ffn_grad_kernel,
            [ops, *others, up, misc, down],
            [((2, dp_size // 2, piece, units), BF)] + [((dp_size // 2, piece, units), BF)] * 2,
            micros=micros,
            scratch=[pltpu.VMEM((width, units), F32)],
        )
        st["fgots"] = [swap(send, *CORE) for send in sends]

    def ffn_last(micros):
        st["ffn"] = call(
            order,
            ffn_finish_kernel,
            [st["fkeep"], *st["fgots"]],
            [((piece, units), F32)] * 2,
            near=False,
            micros=micros,
        )

    def features_step(micros):
        rows_out = call(
            order,
            feature_grad_kernel,
            [st["gm"], in_proj, res, gx],
            [((padded + 2 * block, width), BF)] * 4,
            micros=micros,
            scratch=[pltpu.VMEM((pb_size, padded, width), BF)],
        )
        st["arrived"] = [rows_out[0]] + [swap(rows_out[k], "pb", k) for k in range(1, pb_size)]

    def ab2(micros):
        ra, rb, send3 = order.after([st["ra"], st["rb"], st["send3"]])
        st["got3"] = swap(send3, *CORE)
        st["ka"], sa, st["kb"], sb = fold(
            order,
            [([(ka, ra, 0, 12, 0)], Y_WAY), ([(kb, rb, 0, 12, 0)], X_WAY)],
            micros,
        )
        st["ra"], st["rb"] = swap(sa, *Y_WAY), swap(sb, *X_WAY)

    def ab3(micros):
        st["kab"], send = fold(
            order, [([(st["ka"], st["ra"], 0, 12, 0), (st["kb"], st["rb"], 0, 12, 0)], z_way)], micros
        )
        st["rab"] = swap(send, *z_way)

    def exchange(name, keep, got, micros):
        total = add_up(order, [(keep, got)], micros)
        for way in far_ways[:-1]:
            total = add_up(order, [(total, swap(total, *way))], micros)
        st["v" + name] = total
        st["r" + name] = swap(total, *far_ways[-1])

    def ab4(micros):
        exchange("ab", st["kab"], st["rab"], micros)

    def ab5(micros):
        st["vab"] = add_up(order, [(st["vab"], st["rab"])], micros)
        st["rab"] = swap(st["vab"], *z_way)

    def ab6(micros):
        va, vb = join(order, [(st["vab"], st["rab"], z_way, [(0, 12), (12, 24)])], micros)
        st["va"], st["vb"] = va, vb
        st["ra"], st["rb"] = swap(va, *Y_WAY), swap(vb, *X_WAY)

    def ab7(micros):
        va, vb = join(
            order,
            [(st["va"], st["ra"], Y_WAY, [(0, 12)]), (st["vb"], st["rb"], X_WAY, [(0, 12)])],
            micros,
        )
        st["va"], st["vb"] = va, vb
        st["ra"], st["rb"] = swap(va, *X_WAY), swap(vb, *Y_WAY)

    def ab8(micros):
        va, vb, *st["exchanged"] = join(
            order,
            [(st["va"], st["ra"], X_WAY, [(0, 12)]), (st["vb"], st["rb"], Y_WAY, [(0, 12)])],
            micros,
            st["exchanged"],
        )
        st["va"], st["vb"] = va, vb
        st["ra"], st["rb"] = swap(va, *CORE), swap(vb, *CORE)

    def c_fold(way, first=False):
        def run(micros):
            keep, got = (st["keep3"], st["got3"]) if first else (st["kc"], st["rc"])
            st["kc"], send = fold(order, [([(keep, got, 0, 13, 0)], way)], micros)
            st["rc"] = swap(send, *way)

        return run

    def c4(micros):
        exchange("c", st["kc"], st["rc"], micros)

    def c5(micros):
        st["vc"] = add_up(order, [(st["vc"], st["rc"])], micros)
        st["rc"] = swap(st["vc"], *Y_WAY)

    def c_join(way, onward):
        def run(micros):
            (st["vc"],) = join(order, [(st["vc"], st["rc"], way, [(0, 13)])], micros)
            st["rc"] = swap(st["vc"], *onward)

        return run

    def order_rows(micros):
        exchanged = call(
            order,
            functools.partial(order_kernel, block=block),
            st["arrived"],
            [(tokens.shape, BF), (tokens.shape, BF), ((pb_size, part, width), BF)],
            micros=micros,
        )
        st["exchanged"] = [turn(value) for value in exchanged]

    half = width // 2
    six = [pltpu.VMEM((6, half, width), F32), pltpu.SemaphoreType.DMA((6,))]
    chain = [three, matrix, matrix, three]

    def own(micros):
        st["chain"] = call(
            order, chain_own_kernel, [st["va"], st["vb"]], [], raw=chain, scratch=six, micros=micros
        )

    def finish(micros):
        st["chain"] = call(
            order,
            chain_other_kernel,
            [st["ra"], st["rb"], *[Raw(value) for value in st["chain"]]],
            [],
            raw=chain,
            alias=[(2 + n, n) for n in range(4)],
            scratch=six,
            micros=micros,
        )

    def c_own(micros):
        cross, *rest = st["chain"]
        cross, st["in_proj"] = call(
            order,
            memory_own_kernel,
            [st["vc"], Raw(cross)],
            [],
            raw=[three, matrix],
            alias=[(1, 0)],
            scratch=[pltpu.VMEM((3, half, width), F32), pltpu.SemaphoreType.DMA((3,))],
            micros=micros,
        )
        st["chain"] = [cross, *rest]

    steps = {
        "memory": memory,
        "ffn": ffn,
        "ffn1": ffn_fold,
        "ffn2": lambda micros: [ffn_fold(micros) for _ in far_ways],
        "ffn3": ffn_last,
        "features": features_step,
        "ab2": ab2,
        "ab3": ab3,
        "ab4": ab4,
        "ab5": ab5,
        "ab6": ab6,
        "ab7": ab7,
        "ab8": ab8,
        "c1": c_fold(z_way, True),
        "c2": c_fold(X_WAY),
        "c3": c_fold(Y_WAY),
        "c4": c4,
        "c5": c5,
        "c6": c_join(Y_WAY, X_WAY),
        "c7": c_join(X_WAY, z_way),
        "c8": c_join(z_way, CORE),
        "order": order_rows,
        "finish": finish,
        "own": own,
        "c_own": c_own,
    }
    waits = {"ab5": ("rab",), "ab6": ("rab",), "ab7": ("ra",), "c5": ("rc",), "c6": ("rc",), "ab8": ("ra",)}
    for name, micros in STEPS:
        for at, rows_from in ((NEAR_AT, (1, 2)), (FAR_AT, (3,))):
            if name == at:
                key = waits[name][0]
                st[key], *rows_here = lax.optimization_barrier(
                    (st[key], *[st["arrived"][k] for k in rows_from])
                )
                for k, value in zip(rows_from, rows_here):
                    st["arrived"][k] = value
        steps[name](micros)
    ffn_up, ffn_down = st["ffn"]
    cross_grad, g_self_out, g_cross_out, g_self_proj = st["chain"]
    layer_out, grad_tokens, grad_features = [turn(value) for value in st["exchanged"]]
    bias3 = ((3, width), F32)
    bias1 = ((1, width), F32)
    (
        g_pos,
        g_self_bias,
        g_cross_bias,
        g_bup,
        g_bdown,
        g_gain,
        g_shift,
        g_inb,
        g_cross_proj,
        g_in_proj,
    ) = call(
        order,
        functools.partial(memory_other_kernel, rows_used=used, units=units),
        [st["rc"], st["vc"], Raw(cross_grad), Raw(st["in_proj"])],
        [
            (query_pos.shape, F32),
            bias3,
            bias3,
            ((-(-pb_size * units // LANES), LANES), F32),
            bias1,
            bias3,
            bias3,
            bias1,
        ],
        raw=[three, matrix],
        alias=[(2, 8), (3, 9)],
        scratch=[
            pltpu.VMEM((3, half, width), F32),
            pltpu.SemaphoreType.DMA((3,)),
            pltpu.VMEM(flat, F32),
            pltpu.VMEM((40, LANES), F32),
        ],
        near=False,
    )

    return (
        layer_out,
        grad_tokens,
        grad_features,
        g_pos,
        g_self_proj,
        g_self_out,
        g_self_bias,
        g_cross_proj,
        g_cross_out,
        g_cross_bias,
        ffn_up,
        g_bup.reshape(-1)[: pb_size * units],
        ffn_down,
        g_bdown[0],
        g_gain,
        g_shift,
        g_in_proj,
        g_inb[0],
    )


def solution(mesh):
    return jax.shard_map(
        on_device,
        mesh=mesh,
        in_specs=(
            P("dp", "pb", None),
            P(),
            P("dp", None, None),
            P("dp", None),
            P("dp", "pb", None),
            P(),
            P(),
            P(),
            P(),
            P(),
            P(),
            P(None, "pb"),
            P("pb"),
            P(None, "pb"),
            P(),
            P(),
            P(),
            P(),
            P(),
        ),
        out_specs=(
            P("dp", "pb", None),
            P("dp", "pb", None),
            P("dp", "pb", None),
            P(),
            P(),
            P(),
            P(),
            P(),
            P(),
            P(),
            P("dp", "pb"),
            P(),
            P("dp", "pb"),
            P(),
            P(),
            P(),
            P(),
            P(),
        ),
        check_vma=False,
    )
```

```python
import functools

import jax
import jax.numpy as jnp
import numpy as np
from jax import lax
from jax.experimental import pallas as pl
from jax.experimental.pallas import tpu as pltpu
from jax.sharding import PartitionSpec as P

BF = jnp.bfloat16
F32 = jnp.float32
HEADS = 8
LANES = 128
GROUPS = 4
FAR = -1e30
START_COSTS = (0.0, 8.0, 0.0, 6.0, 7.8, 6.2)
RATE = 1.15e9
STEPS = (
    ("memory", 5.0),
    ("ffn", 0.5),
    ("features", 0.3),
    ("ab2", 0.3),
    ("c1", 0.3),
    ("ab3", 2.7),
    ("ffn1", 0.0),
    ("c2", 0.3),
    ("ab4", 0.6),
    ("c3", 0.3),
    ("ffn2", 0.0),
    ("c4", 0.3),
    ("ab5", 0.3),
    ("c5", 1.2),
    ("ab6", 0.3),
    ("c6", 1.2),
    ("ab7", 0.5),
    ("c7", 2.4),
    ("order", 0.3),
    ("ffn3", 0.6),
    ("ab8", 0.6),
    ("own", 0.0),
    ("c8", 4.0),
    ("c_own", 0.0),
    ("finish", 1.5),
)
NEAR_AT, FAR_AT = "ab5", "ab6"


def dims(left, right, a, b):
    return lax.dot_general(left, right, (((a,), (b,)), ((), ())), preferred_element_type=F32)


def nn(left, right):
    return dims(left, right, 1, 0)


def nt(left, right):
    return dims(left, right, 1, 1)


def tn(left, right):
    return dims(left, right, 0, 0)


def lane_masks(dtype=BF):
    lane = lax.broadcasted_iota(jnp.int32, (1, LANES), 1)
    low = (lane < LANES // 2).astype(F32)
    return low.astype(dtype), (1.0 - low).astype(dtype)


def pair(value, group):
    part = value[:, group * LANES : (group + 1) * LANES]
    low, high = lane_masks()
    return jnp.concatenate([part * low, part * high], axis=0)


def unpair(value):
    rows = value.shape[0] // 2
    lane = lax.broadcasted_iota(jnp.int32, (rows, LANES), 1)
    return jnp.where(lane < LANES // 2, value[:rows], value[rows:])


def row_totals(mix, grad, group):
    lanes = slice(group * LANES, (group + 1) * LANES)
    product = (mix[:, lanes].astype(F32) * grad[:, lanes].astype(F32)).astype(BF)
    low, high = lane_masks()
    heads = jnp.concatenate([low, high, jnp.zeros((14, LANES), BF)], axis=0)
    sums = nt(heads, product)
    return jnp.concatenate([sums[0:1], sums[1:2]], axis=1)


def eights(value, op):
    return op(value.reshape(value.shape[0] // 8, 8, value.shape[1]), axis=0)


def norm(value):
    center = value - jnp.mean(value, -1, keepdims=True)
    rstd = lax.rsqrt(jnp.mean(center * center, -1, keepdims=True) + 1e-05)
    return center * rstd, rstd


def norm_back(xhat, rstd, gain, grad):
    scaled = grad * gain
    inner = jnp.mean(scaled, -1, keepdims=True) + xhat * jnp.mean(
        scaled * xhat, -1, keepdims=True
    )
    return (
        rstd * (scaled - inner),
        jnp.sum(grad * xhat, 0, keepdims=True),
        jnp.sum(grad, 0, keepdims=True),
    )


def column_sum(value):
    return jnp.sum(value.astype(F32), 0, keepdims=True)


def row(ref, index):
    return ref[index : index + 1, :].astype(F32)


def cdf(value):
    return 0.5 * (1.0 + lax.erf(value * np.float32(0.7071067811865476)))


def density(value):
    return jnp.exp(-0.5 * value * value) * np.float32(0.3989422804014327)


class Chain:
    def __init__(self, refs):
        self.refs = refs

    def __setitem__(self, index, value):
        size = self.refs[0].shape[0]
        self.refs[index // size][index % size] = value


def put_halves(core, left_ref, grad, index, keep_ref, send_ref):
    half = left_ref.shape[1] // 2
    for ref, place in ((send_ref, 1 - core), (keep_ref, core)):
        columns = pl.ds(pl.multiple_of(place * half, LANES), half)
        value = tn(left_ref[:, columns], grad).astype(BF)
        for block in range(value.shape[1] // LANES):
            ref[index + block] = value[:, block * LANES : (block + 1) * LANES]


def pick_kernel(ids, up, down, up_part, down_part, sems):
    core = ids[1]
    copies = []
    for ref, out in ((up, up_part), (down, down_part)):
        start = core * (ref.shape[0] - out.shape[0])
        middle = -(-out.shape[0] // 32) * 16
        for at, size in ((0, middle), (middle, out.shape[0] - middle)):
            copies.append(
                pltpu.make_async_copy(
                    ref.at[pl.ds(pl.multiple_of(start + at, 16), size)],
                    out.at[pl.ds(at, size)],
                    sems.at[len(copies)],
                )
            )
    for copy in copies:
        copy.start()
    for copy in copies:
        copy.wait()


def start_kernel(
    ids, tokens, cots, misc, send0, send1, send2, send3, flat, turned, *, rows_used
):
    pb = ids[0]
    rows, width2 = turned.shape
    width = width2 // 2
    block = rows // GROUPS
    count = rows_used * GROUPS
    for q in range(rows_used):
        flat[q * GROUPS : (q + 1) * GROUPS, :width] = tokens[q].astype(F32)
        flat[q * GROUPS : (q + 1) * GROUPS, width:] = cots[q].astype(F32)
    place = lax.broadcasted_iota(jnp.int32, (rows, count), 0)
    query = lax.broadcasted_iota(jnp.int32, (rows, count), 1)
    hit = query == lax.rem(place, block) * GROUPS + lax.div(place, block)
    used = lax.rem(place, block) < rows_used
    chosen = jnp.where(jnp.logical_and(hit, used), 1.0, 0.0).astype(BF)
    turned[...] = nn(chosen, flat[...].astype(BF))
    for b in range(GROUPS):
        at = b * block + rows_used
        turned[at : at + 2, :width] = misc[2:4, :].astype(F32)
    for k, ref in enumerate((send0, send1, send2, send3)):
        at = pl.multiple_of((pb ^ k) * block, block)
        ref[...] = turned[pl.ds(at, block), :].astype(BF)


def memory_kernel(
    ids, feats, sines, cosines, waves, in_proj, misc, cross_proj, cross_bias, featp, ki, vi, k, v, buf, sems
):
    blocks = GROUPS
    slots = buf.shape[0]
    part = slots // blocks
    padded = featp.shape[0] // blocks
    copy = pltpu.make_async_copy(feats.at[ids[0]], buf, sems)
    copy.start()
    for j in range(blocks):
        featp[(j + 1) * padded - 16 : (j + 1) * padded] = jnp.zeros((16, featp.shape[1]), BF)
    copy.wait()
    bias = row(misc, 0)
    for j in range(blocks):
        here = slice(j * padded, (j + 1) * padded)
        featp[j * padded : j * padded + part] = buf[j * part : (j + 1) * part]
        memory = nn(featp[here], in_proj[...]) + bias
        places = cosines[...] * row(waves, j) + sines[...] * row(waves, blocks + j)
        key_input = (memory + places).astype(BF)
        value_input = memory.astype(BF)
        ki[here] = key_input
        vi[here] = value_input
        k[here] = nn(key_input, cross_proj[1]).astype(BF)
        v[here] = (nn(value_input, cross_proj[2]) + row(cross_bias, 1)).astype(BF)


def forward_kernel(
    ids,
    mask,
    own,
    got1,
    got2,
    got3,
    query_pos,
    self_proj,
    self_out,
    self_bias,
    cross_proj,
    cross_out,
    cross_bias,
    gains,
    shifts,
    k_ref,
    v_ref,
    up_,
    down_,
    x_out,
    cot_out,
    ai_out,
    sq_out,
    sk_out,
    sv_out,
    ps_out,
    sm_out,
    xhat1_out,
    rstd1_out,
    ci_out,
    cq_out,
    pc_out,
    cm_out,
    h2_out,
    xhat2_out,
    rstd2_out,
    bups_out,
    h2b_out,
    scores,
    pos_ref,
    *,
    rows_used,
):
    pb = ids[0]
    width = pos_ref.shape[1]
    block = own.shape[0]
    for k, ref in enumerate((own, got1, got2, got3)):
        at = pl.multiple_of((pb ^ k) * block, block)
        x_out[pl.ds(at, block), :] = ref[:, :width]
        cot_out[pl.ds(at, block), :] = ref[:, width:]
        bups_out[2 * k : 2 * k + 2] = ref[rows_used : rows_used + 2, :width].astype(F32)
    rows = x_out.shape[0]
    pos_ref[...] = jnp.zeros(pos_ref.shape, F32)
    for b in range(GROUPS):
        pos_ref[b * block : b * block + rows_used] = query_pos[
            b * rows_used : (b + 1) * rows_used
        ].astype(F32)
    pos = pos_ref[...]
    x = x_out[...].astype(F32)
    ai = (x + pos).astype(BF)
    ai_out[...] = ai
    sq_out[...] = ((nn(ai, self_proj[0]) + row(self_bias, 0)) * 0.125).astype(BF)
    sk_out[...] = nn(ai, self_proj[1]).astype(BF)
    sv_out[...] = (nn(x_out[...], self_proj[2]) + row(self_bias, 1)).astype(BF)
    key_row = lax.broadcasted_iota(jnp.int32, (rows, 2 * rows), 0)
    spare = jnp.where(lax.rem(key_row, block) < rows_used, 0.0, FAR).astype(F32)
    for g in range(GROUPS):
        lanes = slice(g * LANES, (g + 1) * LANES)
        s = nt(sk_out[:, lanes], pair(sq_out[...], g)) + spare
        e = jnp.exp(s - jnp.max(s, 0, keepdims=True))
        p = (e * (1.0 / jnp.sum(e, 0, keepdims=True))).astype(BF)
        ps_out[g] = p
        sm_out[:, lanes] = unpair(tn(p, sv_out[:, lanes])).astype(BF)
    xhat, rstd = norm(x + nn(sm_out[...], self_out[...]) + row(self_bias, 2))
    xhat1_out[...] = xhat
    rstd1_out[...] = rstd
    h1 = xhat * row(gains, 0) + row(shifts, 0)
    ci = (h1 + pos).astype(BF)
    ci_out[...] = ci
    cq_out[...] = ((nn(ci, cross_proj[0]) + row(cross_bias, 0)) * 0.125).astype(BF)

    padded = k_ref.shape[0] // GROUPS
    used = rows_used * 12
    slot_row = lax.broadcasted_iota(jnp.int32, (padded, 2 * rows), 0)
    for g in range(GROUPS):
        lanes = slice(g * LANES, (g + 1) * LANES)
        queries = pair(cq_out[...], g)
        top = jnp.full((8, 2 * rows), FAR, F32)
        for j in range(GROUPS):
            here = slice(j * padded, (j + 1) * padded)
            live = jnp.where(mask[pb, j] > 0, 0.0, -1000000000.0).astype(F32)
            s = nt(k_ref[here, lanes], queries) + jnp.where(slot_row < used, live, FAR)
            scores[here] = s
            top = jnp.maximum(top, eights(s, jnp.max))
        top = jnp.max(top, 0, keepdims=True)
        total = jnp.zeros((8, 2 * rows), F32)
        for j in range(GROUPS):
            here = slice(j * padded, (j + 1) * padded)
            e = jnp.exp(scores[here] - top)
            scores[here] = e
            total = total + eights(e, jnp.sum)
        inverse = 1.0 / jnp.sum(total, 0, keepdims=True)
        for j in range(GROUPS):
            here = slice(j * padded, (j + 1) * padded)
            pc_out[g, here] = (scores[here] * inverse).astype(BF)
        cm_out[:, lanes] = unpair(tn(pc_out[g], v_ref[:, lanes])).astype(BF)
    xhat, rstd = norm(h1 + nn(cm_out[...], cross_out[...]) + row(cross_bias, 2))
    xhat2_out[...] = xhat
    rstd2_out[...] = rstd
    h2 = xhat * row(gains, 1) + row(shifts, 1)
    h2_out[...] = h2
    h2b_out[...] = h2.astype(BF)


def part_of(ref, cut, core):
    spare = ref.shape[0] - cut
    return ref[pl.ds(pl.multiple_of(core * spare, 16), cut), :]


def bias_of(bups, p, units):
    width = bups.shape[1]
    return jnp.concatenate(
        [bups[2 * p : 2 * p + 1], bups[2 * p + 1 : 2 * p + 2, : units - width]], axis=1
    )


def bias_halves(bups, p, units, core):
    whole = bias_of(bups, p, units)
    low, high = whole[:, : units // 2], whole[:, units // 2 :]
    return jnp.where(core == 0, low, high), jnp.where(core == 0, high, low)


def ffn_first_kernel(
    ids, h2_ref, bups, up_own, down_own, up_f, down_f, up_s, down_s, down_out, pre_own, pre_far
):
    core = ids[1]
    h2 = h2_ref[...]
    units = up_own.shape[0]
    pre = nt(h2, up_own[...]) + bias_of(bups, 0, units)
    pre_own[...] = pre
    down = nn((pre * cdf(pre)).astype(BF), down_own[...])
    biases = bias_halves(bups, 3, units, core)
    for n, (up, dn) in enumerate(((up_f, down_f), (up_s, down_s))):
        pre = nt(h2, up[...]) + biases[n]
        pre_far[n] = pre
        down = down + nn((pre * cdf(pre)).astype(BF), dn[...])
    down_out[...] = down


def ffn_second_kernel(
    ids,
    h2_ref,
    h2b_ref,
    cot_ref,
    xhat2_ref,
    rstd2_ref,
    bups,
    up_own,
    down_own,
    down_ref,
    pre_own,
    pre_far,
    misc,
    gains,
    shifts,
    xu_f,
    xd_f,
    yu_f,
    yd_f,
    du_f,
    dd_f,
    xu_s,
    xd_s,
    yu_s,
    yd_s,
    du_s,
    dd_s,
    res_out,
    ops_out,
    g2_out,
    small_out,
    bup_out,
    pre_near,
    dense,
    *,
    rows_used,
):
    core = ids[1]
    units = up_own.shape[0]
    cut = units // 2
    width = h2_ref.shape[1]
    near = (
        (xu_f, xd_f, core),
        (xu_s, xd_s, 1 - core),
        (yu_f, yd_f, core),
        (yu_s, yd_s, 1 - core),
    )
    h2b = h2b_ref[...]
    down = down_ref[...]
    for n, (up, dn, place) in enumerate(near):
        pre = nt(h2b, part_of(up, cut, place)) + bias_halves(bups, n // 2 + 1, units, core)[n % 2]
        pre_near[n] = pre
        down = down + nn((pre * cdf(pre)).astype(BF), part_of(dn, cut, place))
    xhat, rstd = norm(h2_ref[...] + down + row(misc, 1))
    res_out[...] = (xhat * row(gains, 2) + row(shifts, 2)).astype(BF)
    g3, dgain3, dshift3 = norm_back(xhat, rstd, row(gains, 2), cot_ref[...].astype(F32))
    gb = g3.astype(BF)
    block = h2b.shape[0] // GROUPS
    dense[...] = jnp.zeros(dense.shape, F32)
    for b in range(GROUPS):
        here = slice(b * block, b * block + rows_used)
        there = slice(b * rows_used, (b + 1) * rows_used)
        dense[there, :width] = h2b[here].astype(F32)
        dense[there, width:] = gb[here].astype(F32)
    ops_out[...] = dense[...].astype(BF)

    def unit_grads(pre, dn):
        ga = nt(gb, dn).astype(BF).astype(F32)
        return (ga * (cdf(pre) + pre * density(pre))).astype(BF)

    tail = jnp.zeros((1, 2 * width - units), F32)
    gp = unit_grads(pre_own[...], down_own[...])
    bup_out[0] = jnp.concatenate([column_sum(gp), tail], axis=1)
    gh = g3 + nn(gp, up_own[...])
    blocks = list(near) + [(du_f, dd_f, core), (du_s, dd_s, 1 - core)]
    for p in range(3):
        sums = []
        for n in (2 * p, 2 * p + 1):
            up, dn, place = blocks[n]
            gp = unit_grads(pre_near[n] if n < 4 else pre_far[n - 4], part_of(dn, cut, place))
            sums.append(column_sum(gp))
            gh = gh + nn(gp, part_of(up, cut, place))
        low = jnp.where(core == 0, sums[0], sums[1])
        high = jnp.where(core == 0, sums[1], sums[0])
        bup_out[p + 1] = jnp.concatenate([low, high, tail], axis=1)
    g2, dgain2, dshift2 = norm_back(xhat2_ref[...], rstd2_ref[...], row(gains, 1), gh)
    g2_out[...] = g2
    small_out[0:1] = dgain3
    small_out[1:2] = dshift3
    small_out[2:3] = dgain2
    small_out[3:4] = dshift2
    small_out[4:5] = column_sum(gb)
    small_out[5:6] = column_sum(g2.astype(BF))
    small_out[6:8] = jnp.zeros((2, width), F32)


def backward_kernel(
    ids,
    g2_ref,
    pc_ref,
    k_ref,
    v_ref,
    cq_ref,
    ci_ref,
    cm_ref,
    xhat1_ref,
    rstd1_ref,
    x_ref,
    ai_ref,
    sq_ref,
    sk_ref,
    sv_ref,
    ps_ref,
    sm_ref,
    self_proj,
    self_out,
    cross_proj,
    cross_out,
    gains,
    ds_out,
    gcm_out,
    gx_out,
    gpos_out,
    small_out,
    keep,
    send0,
    send1,
    work,
    gq_ref,
    gk_ref,
    gv_ref,
):
    core = ids[1]
    send = Chain((send0, send1))
    width = x_ref.shape[1]
    rows = x_ref.shape[0]
    g2 = g2_ref[...]
    branch = g2.astype(BF)
    gcm_out[...] = nt(branch, cross_out[...]).astype(BF)
    padded = k_ref.shape[0] // GROUPS
    gcm = gcm_out[...]
    for g in range(GROUPS):
        lanes = slice(g * LANES, (g + 1) * LANES)
        grads = pair(gcm, g)
        total = row_totals(cm_ref[...], gcm, g)
        for j in range(GROUPS):
            here = slice(j * padded, (j + 1) * padded)
            dp = nt(v_ref[here, lanes], grads)
            ds_out[g, here] = (pc_ref[g, here].astype(F32) * (dp - total)).astype(BF)
        gq_ref[:, lanes] = unpair(tn(ds_out[g], k_ref[:, lanes])).astype(BF) * 0.125
    gcq = gq_ref[...]
    gci = nt(gcq, cross_proj[0])
    small_out[0:1] = column_sum(gcq)
    put_halves(core, ci_ref, gcq, 0, keep, send)
    put_halves(core, cm_ref, branch, 8, keep, send)
    g1, dgain1, dshift1 = norm_back(xhat1_ref[...], rstd1_ref[...], row(gains, 0), g2 + gci)
    small_out[1:2] = dgain1
    small_out[2:3] = dshift1
    sbranch = g1.astype(BF)
    small_out[3:4] = column_sum(sbranch)
    put_halves(core, sm_ref, sbranch, 4, keep, send)
    gsm = nt(sbranch, self_out[...]).astype(BF)
    for g in range(GROUPS):
        lanes = slice(g * LANES, (g + 1) * LANES)
        grads = pair(gsm, g)
        p = ps_ref[g]
        dp = nt(sv_ref[:, lanes], grads)
        ds = (p.astype(F32) * (dp - row_totals(sm_ref[...], gsm, g))).astype(BF)
        gq_ref[:, lanes] = unpair(tn(ds, sk_ref[:, lanes])).astype(BF) * 0.125
        gk_ref[:, lanes] = nn(ds, pair(sq_ref[...], g)).astype(BF)
        gv_ref[:, lanes] = nn(p, grads).astype(BF)
    gq, gk, gv = gq_ref[...], gk_ref[...], gv_ref[...]
    gai = nt(gq, self_proj[0]) + nt(gk, self_proj[1])
    gx_out[...] = (g1 + gai + nt(gv, self_proj[2])).astype(BF)
    gpos_out[...] = gai + gci
    small_out[4:5] = column_sum(gq)
    small_out[5:6] = column_sum(gv)
    small_out[6:8] = jnp.zeros((2, width), F32)
    put_halves(core, ai_ref, gq, 12, keep, send)
    put_halves(core, ai_ref, gk, 16, keep, send)
    put_halves(core, x_ref, gv, 20, keep, send)


def ffn_grad_kernel(ids, *refs):
    up_own, misc, down_own, keep, send0, send1, work = refs[4:]
    core = ids[1]
    units, width = up_own.shape
    ops = jnp.concatenate([ref[...] for ref in refs[:4]], axis=0)
    inputs, branch = ops[:, :width], ops[:, width:]
    bias = jnp.concatenate([row(misc, 2), row(misc, 3)[:, : units - width]], axis=1)
    pre = nt(inputs, up_own[...]) + bias
    phi = cdf(pre)
    act = (pre * phi).astype(BF)
    gact = nt(branch, down_own[...]).astype(BF).astype(F32)
    gpre = (gact * (phi + pre * density(pre))).astype(BF)
    blocks, size = keep.shape[1], keep.shape[2]
    for side, grad in enumerate((tn(inputs, gpre), tn(branch, act))):
        work[...] = grad
        for block in range(blocks):
            mine = pl.multiple_of((2 * block + core) * size, size)
            other = pl.multiple_of((2 * block + 1 - core) * size, size)
            keep[side, block] = work[pl.ds(mine, size), :].astype(BF)
            (send0, send1)[side][block] = work[pl.ds(other, size), :].astype(BF)


def ffn_fold_kernel(ids, keep, got0, got1, stay, go0, go1, *, bit):
    for side, (got, go) in enumerate(((got0, go0), (got1, go1))):
        for block in range(stay.shape[1]):
            mine, other = 2 * block + ids[bit], 2 * block + 1 - ids[bit]
            go[block] = plus(keep[side, other], got[other])
            stay[side, block] = plus(keep[side, mine], got[mine])


def ffn_finish_kernel(ids, keep, got0, got1, up_grad, down_grad):
    up_grad[...] = keep[0, 0].astype(F32) + got0[0].astype(F32)
    down_grad[...] = keep[1, 0].astype(F32) + got1[0].astype(F32)


def memory_back_kernel(
    ids,
    ds_ref,
    pc_ref,
    cq_ref,
    gcm_ref,
    featp,
    ki,
    vi,
    cross_proj,
    gpos_ref,
    small_a,
    small_b,
    bup,
    held,
    gm_ref,
    keep,
    send,
    gk_ref,
    gv_ref,
    work,
    small,
    *,
    rows_used,
):
    pb, core = ids[0], ids[1]
    width = featp.shape[1]
    rows = gpos_ref.shape[0]
    block = rows // GROUPS
    padded = featp.shape[0] // GROUPS
    pairs_q = [pair(cq_ref[...], g) for g in range(GROUPS)]
    pairs_g = [pair(gcm_ref[...], g) for g in range(GROUPS)]
    for j in range(GROUPS):
        here = slice(j * padded, (j + 1) * padded)
        for g in range(GROUPS):
            lanes = slice(g * LANES, (g + 1) * LANES)
            gk_ref[here, lanes] = nn(ds_ref[g, here], pairs_q[g]).astype(BF)
            gv_ref[here, lanes] = nn(pc_ref[g, here], pairs_g[g]).astype(BF)
        gm = (nt(gk_ref[here], cross_proj[1]) + nt(gv_ref[here], cross_proj[2])).astype(BF)
        gm_ref[here] = gm
    put_halves(core, ki, gk_ref[...], 0, keep, send)
    put_halves(core, vi, gv_ref[...], 4, keep, send)
    put_halves(core, featp, gm_ref[...], 8, keep, send)

    small[...] = gpos_ref[...]
    extras = [
        row(small_b, 1),
        row(small_a, 2),
        row(small_a, 0),
        row(small_b, 2),
        row(small_a, 3),
        row(small_a, 1),
        row(small_b, 4),
        row(small_b, 5),
        row(small_b, 3),
        row(small_b, 0),
        column_sum(gv_ref[...]),
        row(small_a, 5),
        row(small_a, 4),
        column_sum(gm_ref[...]),
    ]
    for index, value in enumerate(extras):
        at = spare_row(index, block, rows_used)
        small[at : at + 1] = value
    for b in range(GROUPS):
        at = b * block + rows_used + 5
        total = bup[b ^ pb]
        small[at : at + 1] = total[:, :width]
        small[at + 1 : at + 2] = total[:, width:]
    for b in range(2):
        for side, ref in ((core, keep), (1 - core, send)):
            low = small[:, b * LANES : (b + 1) * LANES]
            high = small[:, (2 + b) * LANES : (3 + b) * LANES]
            ref[12, b * rows : (b + 1) * rows] = jnp.where(side == 0, low, high).astype(BF)


def feature_grad_kernel(ids, gm_ref, in_proj, res_ref, gx_ref, rows0, rows1, rows2, rows3, gf_ref):
    pb = ids[0]
    padded = gf_ref.shape[1]
    block = res_ref.shape[0] // GROUPS
    for j in range(GROUPS):
        gf_ref[j] = nt(gm_ref[j * padded : (j + 1) * padded], in_proj[...]).astype(BF)
    for k, ref in enumerate((rows0, rows1, rows2, rows3)):
        at = pl.multiple_of((pb ^ k) * block, block)
        ref[0:padded] = gf_ref[pb ^ k]
        ref[padded : padded + block] = gx_ref[pl.ds(at, block), :]
        ref[padded + block : padded + 2 * block] = res_ref[pl.ds(at, block), :]


def spare_row(index, block, rows_used):
    return index // 5 * block + rows_used + index % 5


def write_rows(core, refs, places, work, sems):
    half = work.shape[1]
    rows = pl.ds(pl.multiple_of(core * half, half), half)
    copies = []
    for n, (ref, first, matrix) in enumerate(places):
        for b in range(4):
            work[n, :, b * LANES : (b + 1) * LANES] = refs[ref][first + b].astype(F32)
        copies.append(pltpu.make_async_copy(work.at[n], matrix.at[rows], sems.at[n]))
        copies[-1].start()
    return copies


def chain_places(cross, self_out, cross_out, self_proj):
    return [
        (0, 0, cross.at[0]),
        (0, 4, self_out),
        (0, 8, cross_out),
        (1, 0, self_proj.at[0]),
        (1, 4, self_proj.at[1]),
        (1, 8, self_proj.at[2]),
    ]


def chain_own_kernel(ids, va, vb, cross, self_out, cross_out, self_proj, work, sems):
    places = chain_places(cross, self_out, cross_out, self_proj)
    for copy in write_rows(ids[1], (va, vb), places, work, sems):
        copy.wait()


def chain_other_kernel(
    ids, ra, rb, in0, in1, in2, in3, cross, self_out, cross_out, self_proj, work, sems
):
    places = chain_places(cross, self_out, cross_out, self_proj)
    for copy in write_rows(1 - ids[1], (ra, rb), places, work, sems):
        copy.wait()


def memory_places(cross, in_):
    return [(0, 0, cross.at[1]), (0, 4, cross.at[2]), (0, 8, in_)]


def memory_own_kernel(ids, vc, cross_in, cross, in_, work, sems):
    for copy in write_rows(ids[1], (vc,), memory_places(cross, in_), work, sems):
        copy.wait()


def memory_other_kernel(
    ids,
    rc,
    vc,
    cross_in,
    in_in,
    pos_,
    self_bias_,
    cross_bias_,
    bup_,
    bdown_,
    gain_,
    shift_,
    inb_,
    cross,
    in_,
    work,
    sems,
    small,
    tiles,
    *,
    rows_used,
    units,
):
    core = ids[1]
    copies = write_rows(1 - core, (rc,), memory_places(cross, in_), work, sems)
    rows, width = small.shape
    block = rows // GROUPS
    for b in range(2):
        here = slice(b * rows, (b + 1) * rows)
        first = vc[12, here].astype(F32)
        second = rc[12, here].astype(F32)
        small[:, b * LANES : (b + 1) * LANES] = jnp.where(core == 0, first, second)
        small[:, (2 + b) * LANES : (3 + b) * LANES] = jnp.where(core == 0, second, first)
    lane = lax.broadcasted_iota(jnp.int32, (8, LANES), 1)
    tiles[...] = jnp.zeros(tiles.shape, F32)
    for b in range(GROUPS):
        pos_[b * rows_used : (b + 1) * rows_used] = small[b * block : b * block + rows_used]
        at = b * block + rows_used + 5
        first, shift = b * units // LANES, b * units % LANES
        both = [
            small[at + n : at + n + 1, m * LANES : (m + 1) * LANES]
            for n in range(2)
            for m in range(4)
        ]
        part = jnp.concatenate(both, axis=0)
        if shift:
            part = pltpu.roll(part, shift, 1)
        tiles[first : first + 8] += jnp.where(lane >= shift, part, 0.0)
        tiles[first + 1 : first + 9] += jnp.where(lane < shift, part, 0.0)
    bup_[...] = tiles[: bup_.shape[0]]

    def spare(index):
        at = spare_row(index, block, rows_used)
        return small[at : at + 1]

    for ref, index in ((gain_, 0), (shift_, 3), (self_bias_, 6), (cross_bias_, 9)):
        for i in range(3):
            ref[i : i + 1] = spare(index + i)
    bdown_[...] = spare(12)
    inb_[...] = spare(13)
    for copy in copies:
        copy.wait()


def hold_kernel(ids, got1, got2, got3, branch, out):
    out[...] = got1[:16, :LANES] + got2[:16, :LANES] + got3[:16, :LANES] + branch[:16, :LANES]


def order_kernel(ids, own, got1, got2, got3, out, grad, feats, *, block):
    pb = ids[0]
    part, used = feats.shape[1], out.shape[1]
    padded = own.shape[0] - 2 * block
    for k, ref in enumerate((own, got1, got2, got3)):
        feats[pb ^ k] = ref[0:part]
        grad[pb ^ k] = ref[padded : padded + used]
        out[pb ^ k] = ref[padded + block : padded + block + used]


class Far:
    def __init__(self, value, parts=None, emit=False):
        self.value, self.parts, self.emit = value, parts, emit


class Raw:
    def __init__(self, value):
        self.value = value


class Late:
    def __init__(self, ref, buffers, sems, parts):
        self.shape = ref.shape
        self.parts = parts
        self.buffers = buffers
        sources = [ref] if parts is None else [ref.at[part] for part in parts]
        self.copies = [
            pltpu.make_async_copy(source, buffer, sems.at[n])
            for n, (source, buffer) in enumerate(zip(sources, buffers))
        ]
        for copy in self.copies:
            copy.start()
        self.waiting = set(range(len(sources)))

    def ready(self, n):
        if n in self.waiting:
            self.waiting.discard(n)
            self.copies[n].wait()

    def __getitem__(self, index):
        if self.parts is None:
            self.ready(0)
            return self.buffers[0][index]
        n = self.parts.index(index)
        self.ready(n)
        return self.buffers[n][...]


class Places:
    def __getitem__(self, index):
        if index == 0:
            return lax.axis_index("pb")
        axis, bit = BITS[index - 1]
        return lax.rem(lax.div(lax.axis_index(axis), bit), 2)


CORE, X_WAY, Y_WAY = ("dp", 1), ("pb", 1), ("pb", 2)
BITS = [CORE, X_WAY, Y_WAY] + [("dp", 2 << n) for n in range(16)]


def place_of(way):
    return 1 + BITS.index(way)


class Order:
    def __init__(self):
        self.token = None

    def after(self, values):
        if self.token is None:
            return list(values)
        return list(lax.optimization_barrier((*values, self.token)))[:-1]


def call(
    order, kernel, args, outs, scratch=(), limit=16, near=True, micros=0.6, through=(), raw=(), alias=()
):
    through = order.after(through)
    bare = order.after([arg.value if isinstance(arg, (Far, Raw)) else arg for arg in args])
    args = [
        Far(value, arg.parts, arg.emit)
        if isinstance(arg, Far)
        else Raw(value)
        if isinstance(arg, Raw)
        else value
        for value, arg in zip(bare, args)
    ]
    specs, values, extra, emitted, plans = [], [], [], [], []
    outs, raw = list(outs), list(raw)
    for arg in args:
        if isinstance(arg, (Far, Raw)):
            value = arg.value
            specs.append(pl.BlockSpec(memory_space=pl.ANY))
            values.append(pltpu.with_memory_space_constraint(value, pltpu.HBM))
            if isinstance(arg, Raw):
                plans.append(None)
                continue
            count = 1 if arg.parts is None else len(arg.parts)
            if arg.emit:
                plans.append((None, len(emitted), len(extra), count, arg.parts))
                emitted.append((value.shape, value.dtype))
            else:
                plans.append((len(extra), None, len(extra) + count, count, arg.parts))
                shape = value.shape if arg.parts is None else value.shape[1:]
                extra += [pltpu.VMEM(shape, value.dtype)] * count
            extra.append(pltpu.SemaphoreType.DMA((count,)))
        elif jnp.issubdtype(arg.dtype, jnp.integer):
            specs.append(pl.BlockSpec(memory_space=pltpu.SMEM))
            values.append(arg)
            plans.append(None)
        else:
            specs.append(pl.BlockSpec(memory_space=pltpu.VMEM))
            values.append(pltpu.with_memory_space_constraint(arg, pltpu.VMEM))
            plans.append(None)

    def body(*refs):
        given, rest = list(refs[: len(args)]), refs[len(args) + len(through) :]
        first, rest = rest[: len(outs) + len(raw)], rest[len(outs) + len(raw) :]
        copies, rest = rest[: len(emitted)], rest[len(emitted) + len(through) :]
        own, late = rest[: len(scratch)], rest[len(scratch) :]
        waits = []
        for index, plan in enumerate(plans):
            if plan is None:
                continue
            at, place, sem, count, parts = plan
            if place is None:
                buffers = late[at : at + count]
            elif parts is None:
                buffers = [copies[place]]
            else:
                buffers = [copies[place].at[part] for part in parts]
            given[index] = Late(given[index], buffers, late[sem], parts)
            waits.append(given[index])
        kernel(Places(), *given, *first, *own)
        for one in waits:
            for n in sorted(one.waiting):
                one.ready(n)

    whole = [(o, near) for o in outs] + [(o, False) for o in raw] + [(o, True) for o in emitted]
    spaces = [pltpu.VMEM] * len(outs) + [pl.ANY] * len(raw) + [pltpu.VMEM] * len(emitted)
    result = pl.pallas_call(
        body,
        out_shape=[pltpu.VMEM(*o) if here else jax.ShapeDtypeStruct(*o) for o, here in whole]
        + [jax.ShapeDtypeStruct(value.shape, value.dtype) for value in through],
        in_specs=specs + [pl.BlockSpec(memory_space=pl.ANY)] * len(through),
        out_specs=[pl.BlockSpec(memory_space=space) for space in spaces]
        + [pl.BlockSpec(memory_space=pl.ANY)] * len(through),
        input_output_aliases={len(args) + n: len(whole) + n for n in range(len(through))} | dict(alias),
        scratch_shapes=list(scratch) + extra,
        compiler_params=pltpu.CompilerParams(vmem_limit_bytes=limit * 1024 * 1024),
        cost_estimate=pl.CostEstimate(
            flops=int(micros * RATE) + 1, bytes_accessed=int(micros * 3.7e6) + 1, transcendentals=0
        ),
    )(*values, *through)
    order.token = result[0]
    return result


def swap(value, axis, bit):
    size = lax.axis_size(axis)
    return lax.ppermute(value, axis, [(i, i ^ bit) for i in range(size)])


def bit_of(axis, bit):
    return (lax.axis_index(axis) // bit) % 2


def plus(left, right):
    return (left.astype(F32) + right.astype(F32)).astype(BF)


def bit_of(way):
    axis, bit = way
    return (lax.axis_index(axis) // bit) % 2


def halve(keep, got, bit):
    half = keep.shape[1] // 2
    total = plus(keep, got)
    mine = lax.dynamic_slice_in_dim(total, bit * half, half, 1)
    other = lax.dynamic_slice_in_dim(total, (1 - bit) * half, half, 1)
    return mine, other


def fold(order, groups, micros=0.6):
    rows = groups[0][0][0][0].shape[1] // 2
    if rows % 16:
        result = []
        for pieces, way in groups:
            done = [
                halve(keep[a:b], got[a - m : b - m], bit_of(way)) for keep, got, a, b, m in pieces
            ]
            result += [jnp.concatenate(side) for side in zip(*done)]
        return result
    args, outs = [], []
    for pieces, way in groups:
        count = sum(b - a for _, _, a, b, _ in pieces)
        outs += [((count, rows, LANES), BF)] * 2
        for keep, got, _, _, _ in pieces:
            args += [keep, got]

    def kernel(ids, *refs):
        given, made = list(refs[: len(args)]), list(refs[len(args) :])
        for pieces, way in groups:
            stay, go = made.pop(0), made.pop(0)
            bit = ids[place_of(way)]
            mine = pl.multiple_of(bit * rows, rows)
            other = pl.multiple_of((1 - bit) * rows, rows)
            at = 0
            for _, _, a, b, m in pieces:
                keep, got = given.pop(0), given.pop(0)
                for block in range(a, b):
                    for ref, start in ((go, other), (stay, mine)):
                        here = pl.ds(start, rows)
                        ref[at] = plus(keep[block, here], got[block - m, here])
                    at += 1

    return call(order, kernel, args, outs, limit=4, micros=micros)


def add_up(order, pieces, micros=0.6):
    if pieces[0][0].shape[1] % 16:
        return jnp.concatenate([plus(keep, got) for keep, got in pieces])

    def kernel(ids, *refs):
        at = 0
        for keep, got in zip(refs[0:-1:2], refs[1:-1:2]):
            refs[-1][at : at + keep.shape[0]] = plus(keep[...], got[...])
            at += keep.shape[0]

    count = sum(keep.shape[0] for keep, _ in pieces)
    shape = (count,) + pieces[0][0].shape[1:]
    args = [ref for piece in pieces for ref in piece]
    return call(order, kernel, args, [(shape, BF)], limit=4, micros=micros)[0]


def join(order, pieces, micros=0.6, through=()):
    if pieces[0][0].shape[1] % 16:
        result = []
        for value, got, way, cuts in pieces:
            full = jnp.where(
                bit_of(way) == 0, jnp.concatenate([value, got], 1), jnp.concatenate([got, value], 1)
            )
            result += [full[a:b] for a, b in cuts]
        return result + list(through)
    outs = []
    for value, _, _, cuts in pieces:
        outs += [((b - a, 2 * value.shape[1], LANES), BF) for a, b in cuts]

    def kernel(ids, *refs):
        given, made = list(refs[: 2 * len(pieces)]), list(refs[2 * len(pieces) :])
        for _, _, way, cuts in pieces:
            value, got = given.pop(0), given.pop(0)
            rows = value.shape[1]
            bit = ids[place_of(way)]
            mine = pl.multiple_of(bit * rows, rows)
            other = pl.multiple_of((1 - bit) * rows, rows)
            for a, b in cuts:
                out = made.pop(0)
                for block in range(a, b):
                    out[block - a, pl.ds(mine, rows)] = value[block]
                    out[block - a, pl.ds(other, rows)] = got[block]

    args = [ref for value, got, _, _ in pieces for ref in (value, got)]
    return call(order, kernel, args, outs, limit=4, micros=micros, through=through)


def on_device(
    tokens,
    query_pos,
    features,
    camera_mask,
    out_grad,
    self_proj,
    self_out,
    self_bias,
    cross_proj,
    cross_out,
    cross_bias,
    w_up,
    b_up,
    w_down,
    b_down,
    norm_gain,
    norm_bias,
    in_proj,
    in_bias,
):
    order = Order()
    pb_size = lax.axis_size("pb")
    dp_size = lax.axis_size("dp")
    ways = [("dp", 1 << i) for i in range(1, dp_size.bit_length() - 1)]
    width = tokens.shape[2]
    used = tokens.shape[1]
    block = -(-used // 16) * 16
    rows = block * pb_size
    mem = features.shape[1]
    part = mem // pb_size
    padded = -(-part // 16) * 16
    slots = padded * pb_size
    units = b_up.shape[0]

    up, down = w_up.T, w_down.T
    cut = units // 2
    def pick(count):
        return call(
            order,
            pick_kernel,
            [Raw(up), Raw(down)],
            [((count, width), BF)] * 2,
            scratch=[pltpu.SemaphoreType.DMA((4,))],
            limit=4,
            micros=0.0,
        )

    up_half, down_half = pick(cut)
    fy0 = swap(up_half, *Y_WAY)
    fx1 = swap(down_half, *X_WAY)
    up_wide, down_wide = pick(cut + 16)
    misc = (
        jnp.pad(in_bias[None], ((0, 3), (0, 0)))
        + jnp.pad(b_down[None], ((1, 2), (0, 0)))
        + jnp.pad(jnp.pad(b_up, (0, 2 * width - units)).reshape(2, width), ((2, 0), (0, 0)))
    )
    turn = lambda value: value.transpose(1, 0, 2)
    send = call(
        order,
        functools.partial(start_kernel, rows_used=used),
        [turn(tokens), turn(out_grad), misc],
        [((block, 2 * width), BF)] * 4,
        scratch=[
            pltpu.VMEM((used * pb_size, 2 * width), F32),
            pltpu.VMEM((rows, 2 * width), F32),
        ],
    )
    got = [send[0]] + [swap(send[k], "pb", k) for k in range(1, pb_size)]
    column = np.arange(width)
    rate = 1.0 / 10000.0 ** ((column // 2 * 2) / width)
    angle = np.arange(padded)[:, None] * rate
    start = np.arange(pb_size)[:, None] * part * rate
    even = column % 2 == 0
    waves = np.concatenate(
        [
            np.where(even, np.sin(start), np.cos(start)),
            np.where(even, np.cos(start), -np.sin(start)),
        ]
    )
    sines, cosines, waves = [
        jnp.asarray(value.astype(np.float32)) for value in (np.sin(angle), np.cos(angle), waves)
    ]

    wide = (slots, width)
    featp, ki, vi, ck, cv, in_proj, cross_proj = call(
        order,
        memory_kernel,
        [
            Raw(features),
            Far(sines),
            Far(cosines),
            Far(waves),
            Far(in_proj, emit=True),
            misc,
            Far(cross_proj, (1, 2, 0), emit=True),
            Far(cross_bias),
        ],
        [(wide, BF)] * 5,
        micros=START_COSTS[0],
        scratch=[pltpu.VMEM((mem, width), BF), pltpu.SemaphoreType.DMA],
    )
    fx1, fy0, up_wide, down_wide = order.after((fx1, fy0, up_wide, down_wide))
    fx0 = swap(up_wide, *X_WAY)
    fy1 = swap(down_wide, *Y_WAY)
    fx1, fy0, *got = order.after((fx1, fy0, *got))
    fd0 = swap(fy0, *X_WAY)
    fd1 = swap(fx1, *Y_WAY)
    flat = (rows, width)
    scores = (GROUPS, slots, 2 * rows)
    (x, cot, ai, sq, sk, sv, ps, sm, xhat1, rstd1, ci, cq, pc, cm, h2, xhat2, rstd2, bups, h2b, self_proj, self_out, cross_out, norm_gain, norm_bias, up, down) = call(
        order,
        functools.partial(forward_kernel, rows_used=used),
        [
            camera_mask,
            *got,
            Far(query_pos),
            Far(self_proj, (0, 1, 2), emit=True),
            Far(self_out, emit=True),
            Far(self_bias),
            cross_proj,
            Far(cross_out, emit=True),
            Far(cross_bias),
            Far(norm_gain, emit=True),
            Far(norm_bias, emit=True),
            ck,
            cv,
            Far(up, emit=True),
            Far(down, emit=True),
        ],
        [
            (flat, BF),
            (flat, BF),
            (flat, BF),
            (flat, BF),
            (flat, BF),
            (flat, BF),
            ((GROUPS, rows, 2 * rows), BF),
            (flat, BF),
            (flat, F32),
            ((rows, 1), F32),
            (flat, BF),
            (flat, BF),
            (scores, BF),
            (flat, BF),
            (flat, F32),
            (flat, F32),
            ((rows, 1), F32),
            ((2 * pb_size, width), F32),
            (flat, BF),
        ],
        micros=START_COSTS[1],
        scratch=[pltpu.VMEM((slots, 2 * rows), F32), pltpu.VMEM(flat, F32)],
    )
    fx1, fy0, fd0, fd1 = order.after((fx1, fy0, fd0, fd1))
    sx1, sy0 = swap(fx1, *CORE), swap(fy0, *CORE)
    sd0, sd1 = swap(fd0, *CORE), swap(fd1, *CORE)
    down_part, pre_own, pre_far = call(
        order,
        ffn_first_kernel,
        [h2b, bups, up, down, fd0, fd1, sd0, sd1],
        [(flat, F32), ((rows, units), F32), ((2, rows, cut), F32)],
        micros=START_COSTS[2],
    )
    fx0, fy1 = order.after((fx0, fy1))
    sx0, sy1 = swap(fx0, *CORE), swap(fy1, *CORE)
    pieces = [fx0, fx1, fy0, fy1, fd0, fd1, sx0, sx1, sy0, sy1, sd0, sd1]
    dense = (-(-used * pb_size // 8) * 8, 2 * width)
    res, ops, g2, small_a, bup = call(
        order,
        functools.partial(ffn_second_kernel, rows_used=used),
        [
            h2,
            h2b,
            cot,
            xhat2,
            rstd2,
            bups,
            up,
            down,
            down_part,
            pre_own,
            pre_far,
            misc,
            norm_gain,
            norm_bias,
            *pieces,
        ],
        [
            (flat, BF),
            (dense, BF),
            (flat, F32),
            ((8, width), F32),
            ((pb_size, 1, 2 * width), F32),
        ],
        micros=START_COSTS[3],
        scratch=[pltpu.VMEM((4, rows, cut), F32), pltpu.VMEM(dense, F32)],
    )
    others = [swap(ops, "pb", k) for k in range(1, pb_size)]
    halves = ((24, width // 2, LANES), BF)
    ds, gcm, gx, gpos, small_b, keep12, *sends12 = call(
        order,
        backward_kernel,
        [
            g2,
            pc,
            ck,
            cv,
            cq,
            ci,
            cm,
            xhat1,
            rstd1,
            x,
            ai,
            sq,
            sk,
            sv,
            ps,
            sm,
            self_proj,
            self_out,
            cross_proj,
            cross_out,
            norm_gain,
        ],
        [
            (scores, BF),
            (flat, BF),
            (flat, BF),
            (flat, F32),
            ((8, width), F32),
            halves,
        ]
        + [((12, width // 2, LANES), BF)] * 2,
        micros=START_COSTS[4],
        scratch=[
            pltpu.VMEM((width, width), F32),
            pltpu.VMEM(flat, BF),
            pltpu.VMEM(flat, BF),
            pltpu.VMEM(flat, BF),
        ],
    )
    got12 = [swap(send, *CORE) for send in sends12]
    piece = width // dp_size
    (held,) = call(order, hold_kernel, [*others, gcm], [((16, LANES), BF)], limit=2, micros=START_COSTS[5])
    ka, sa, kb, sb = fold(
        order,
        [
            ([(keep12, got12[0], 0, 12, 0)], X_WAY),
            ([(keep12, got12[1], 12, 24, 12)], Y_WAY),
        ],
    )
    ra, rb = swap(sa, *X_WAY), swap(sb, *Y_WAY)

    def ffn_fold(keep, gots, micros):
        way = ways[(dp_size // 2).bit_length() - keep.shape[1].bit_length()]
        half = keep.shape[1] // 2
        keep, *sends = call(
            order,
            functools.partial(ffn_fold_kernel, bit=place_of(way)),
            [keep, *gots],
            [((2, half, piece, units), BF)] + [((half, piece, units), BF)] * 2,
            limit=4,
            micros=micros,
        )
        return keep, [swap(send, *way) for send in sends]

    halves3 = ((13, width // 2, LANES), BF)
    z_way, far_ways = ways[0], ways[1:]
    matrix = ((width, width), F32)
    three = ((3, width, width), F32)
    st = {"ra": ra, "rb": rb}

    def ffn_fold(micros):
        keep = st["fkeep"]
        way = ways[(dp_size // 2).bit_length() - keep.shape[1].bit_length()]
        half = keep.shape[1] // 2
        st["fkeep"], *sends = call(
            order,
            functools.partial(ffn_fold_kernel, bit=place_of(way)),
            [keep, *st["fgots"]],
            [((2, half, piece, units), BF)] + [((half, piece, units), BF)] * 2,
            limit=4,
            micros=micros,
        )
        st["fgots"] = [swap(send, *way) for send in sends]

    def memory(micros):
        st["gm"], st["keep3"], st["send3"] = call(
            order,
            functools.partial(memory_back_kernel, rows_used=used),
            [ds, pc, cq, gcm, featp, ki, vi, cross_proj, gpos, small_a, small_b, bup, held],
            [(wide, BF), halves3, halves3],
            micros=micros,
            scratch=[
                pltpu.VMEM(wide, BF),
                pltpu.VMEM(wide, BF),
                pltpu.VMEM((width, width), F32),
                pltpu.VMEM(flat, F32),
            ],
        )

    def ffn(micros):
        st["fkeep"], *sends = call(
            order,
            ffn_grad_kernel,
            [ops, *others, up, misc, down],
            [((2, dp_size // 2, piece, units), BF)] + [((dp_size // 2, piece, units), BF)] * 2,
            micros=micros,
            scratch=[pltpu.VMEM((width, units), F32)],
        )
        st["fgots"] = [swap(send, *CORE) for send in sends]

    def ffn_last(micros):
        st["ffn"] = call(
            order,
            ffn_finish_kernel,
            [st["fkeep"], *st["fgots"]],
            [((piece, units), F32)] * 2,
            near=False,
            micros=micros,
        )

    def features_step(micros):
        rows_out = call(
            order,
            feature_grad_kernel,
            [st["gm"], in_proj, res, gx],
            [((padded + 2 * block, width), BF)] * 4,
            micros=micros,
            scratch=[pltpu.VMEM((pb_size, padded, width), BF)],
        )
        st["arrived"] = [rows_out[0]] + [swap(rows_out[k], "pb", k) for k in range(1, pb_size)]

    def ab2(micros):
        ra, rb, send3 = order.after([st["ra"], st["rb"], st["send3"]])
        st["got3"] = swap(send3, *CORE)
        st["ka"], sa, st["kb"], sb = fold(
            order,
            [([(ka, ra, 0, 12, 0)], Y_WAY), ([(kb, rb, 0, 12, 0)], X_WAY)],
            micros,
        )
        st["ra"], st["rb"] = swap(sa, *Y_WAY), swap(sb, *X_WAY)

    def ab3(micros):
        st["kab"], send = fold(
            order, [([(st["ka"], st["ra"], 0, 12, 0), (st["kb"], st["rb"], 0, 12, 0)], z_way)], micros
        )
        st["rab"] = swap(send, *z_way)

    def exchange(name, keep, got, micros):
        total = add_up(order, [(keep, got)], micros)
        for way in far_ways[:-1]:
            total = add_up(order, [(total, swap(total, *way))], micros)
        st["v" + name] = total
        st["r" + name] = swap(total, *far_ways[-1])

    def ab4(micros):
        exchange("ab", st["kab"], st["rab"], micros)

    def ab5(micros):
        st["vab"] = add_up(order, [(st["vab"], st["rab"])], micros)
        st["rab"] = swap(st["vab"], *z_way)

    def ab6(micros):
        va, vb = join(order, [(st["vab"], st["rab"], z_way, [(0, 12), (12, 24)])], micros)
        st["va"], st["vb"] = va, vb
        st["ra"], st["rb"] = swap(va, *Y_WAY), swap(vb, *X_WAY)

    def ab7(micros):
        va, vb = join(
            order,
            [(st["va"], st["ra"], Y_WAY, [(0, 12)]), (st["vb"], st["rb"], X_WAY, [(0, 12)])],
            micros,
        )
        st["va"], st["vb"] = va, vb
        st["ra"], st["rb"] = swap(va, *X_WAY), swap(vb, *Y_WAY)

    def ab8(micros):
        va, vb, *st["exchanged"] = join(
            order,
            [(st["va"], st["ra"], X_WAY, [(0, 12)]), (st["vb"], st["rb"], Y_WAY, [(0, 12)])],
            micros,
            st["exchanged"],
        )
        st["va"], st["vb"] = va, vb
        st["ra"], st["rb"] = swap(va, *CORE), swap(vb, *CORE)

    def c_fold(way, first=False):
        def run(micros):
            keep, got = (st["keep3"], st["got3"]) if first else (st["kc"], st["rc"])
            st["kc"], send = fold(order, [([(keep, got, 0, 13, 0)], way)], micros)
            st["rc"] = swap(send, *way)

        return run

    def c4(micros):
        exchange("c", st["kc"], st["rc"], micros)

    def c5(micros):
        st["vc"] = add_up(order, [(st["vc"], st["rc"])], micros)
        st["rc"] = swap(st["vc"], *Y_WAY)

    def c_join(way, onward):
        def run(micros):
            (st["vc"],) = join(order, [(st["vc"], st["rc"], way, [(0, 13)])], micros)
            st["rc"] = swap(st["vc"], *onward)

        return run

    def order_rows(micros):
        exchanged = call(
            order,
            functools.partial(order_kernel, block=block),
            st["arrived"],
            [(tokens.shape, BF), (tokens.shape, BF), ((pb_size, part, width), BF)],
            micros=micros,
        )
        st["exchanged"] = [turn(value) for value in exchanged]

    half = width // 2
    six = [pltpu.VMEM((6, half, width), F32), pltpu.SemaphoreType.DMA((6,))]
    chain = [three, matrix, matrix, three]

    def own(micros):
        st["chain"] = call(
            order, chain_own_kernel, [st["va"], st["vb"]], [], raw=chain, scratch=six, micros=micros
        )

    def finish(micros):
        st["chain"] = call(
            order,
            chain_other_kernel,
            [st["ra"], st["rb"], *[Raw(value) for value in st["chain"]]],
            [],
            raw=chain,
            alias=[(2 + n, n) for n in range(4)],
            scratch=six,
            micros=micros,
        )

    def c_own(micros):
        cross, *rest = st["chain"]
        cross, st["in_proj"] = call(
            order,
            memory_own_kernel,
            [st["vc"], Raw(cross)],
            [],
            raw=[three, matrix],
            alias=[(1, 0)],
            scratch=[pltpu.VMEM((3, half, width), F32), pltpu.SemaphoreType.DMA((3,))],
            micros=micros,
        )
        st["chain"] = [cross, *rest]

    steps = {
        "memory": memory,
        "ffn": ffn,
        "ffn1": ffn_fold,
        "ffn2": lambda micros: [ffn_fold(micros) for _ in far_ways],
        "ffn3": ffn_last,
        "features": features_step,
        "ab2": ab2,
        "ab3": ab3,
        "ab4": ab4,
        "ab5": ab5,
        "ab6": ab6,
        "ab7": ab7,
        "ab8": ab8,
        "c1": c_fold(z_way, True),
        "c2": c_fold(X_WAY),
        "c3": c_fold(Y_WAY),
        "c4": c4,
        "c5": c5,
        "c6": c_join(Y_WAY, X_WAY),
        "c7": c_join(X_WAY, z_way),
        "c8": c_join(z_way, CORE),
        "order": order_rows,
        "finish": finish,
        "own": own,
        "c_own": c_own,
    }
    waits = {"ab5": ("rab",), "ab6": ("rab",), "ab7": ("ra",), "c5": ("rc",), "c6": ("rc",), "ab8": ("ra",)}
    for name, micros in STEPS:
        for at, rows_from in ((NEAR_AT, (1, 2)), (FAR_AT, (3,))):
            if name == at:
                key = waits[name][0]
                st[key], *rows_here = lax.optimization_barrier(
                    (st[key], *[st["arrived"][k] for k in rows_from])
                )
                for k, value in zip(rows_from, rows_here):
                    st["arrived"][k] = value
        steps[name](micros)
    ffn_up, ffn_down = st["ffn"]
    cross_grad, g_self_out, g_cross_out, g_self_proj = st["chain"]
    layer_out, grad_tokens, grad_features = [turn(value) for value in st["exchanged"]]
    bias3 = ((3, width), F32)
    bias1 = ((1, width), F32)
    (
        g_pos,
        g_self_bias,
        g_cross_bias,
        g_bup,
        g_bdown,
        g_gain,
        g_shift,
        g_inb,
        g_cross_proj,
        g_in_proj,
    ) = call(
        order,
        functools.partial(memory_other_kernel, rows_used=used, units=units),
        [st["rc"], st["vc"], Raw(cross_grad), Raw(st["in_proj"])],
        [
            (query_pos.shape, F32),
            bias3,
            bias3,
            ((-(-pb_size * units // LANES), LANES), F32),
            bias1,
            bias3,
            bias3,
            bias1,
        ],
        raw=[three, matrix],
        alias=[(2, 8), (3, 9)],
        scratch=[
            pltpu.VMEM((3, half, width), F32),
            pltpu.SemaphoreType.DMA((3,)),
            pltpu.VMEM(flat, F32),
            pltpu.VMEM((40, LANES), F32),
        ],
        near=False,
    )

    return (
        layer_out,
        grad_tokens,
        grad_features,
        g_pos,
        g_self_proj,
        g_self_out,
        g_self_bias,
        g_cross_proj,
        g_cross_out,
        g_cross_bias,
        ffn_up,
        g_bup.reshape(-1)[: pb_size * units],
        ffn_down,
        g_bdown[0],
        g_gain,
        g_shift,
        g_in_proj,
        g_inb[0],
    )


def solution(mesh):
    return jax.shard_map(
        on_device,
        mesh=mesh,
        in_specs=(
            P("dp", "pb", None),
            P(),
            P("dp", None, None),
            P("dp", None),
            P("dp", "pb", None),
            P(),
            P(),
            P(),
            P(),
            P(),
            P(),
            P(None, "pb"),
            P("pb"),
            P(None, "pb"),
            P(),
            P(),
            P(),
            P(),
            P(),
        ),
        out_specs=(
            P("dp", "pb", None),
            P("dp", "pb", None),
            P("dp", "pb", None),
            P(),
            P(),
            P(),
            P(),
            P(),
            P(),
            P(),
            P("dp", "pb"),
            P(),
            P("dp", "pb"),
            P(),
            P(),
            P(),
            P(),
            P(),
        ),
        check_vma=False,
    )
```
